128 devices in a mesh: shard: 8 (over z, y_lo), ctx: 16 (over y_hi, x, core).
Axes of the slice: x: 4, y: 4 (y_hi: 2, y_lo: 2; y = y_hi * 2 + y_lo), z: 4, core: 2. Of those that a mesh axis runs over, the one named last changes fastest.
Arguments:
- states: bfloat16 [8, 2048, 768], P('shard', 'ctx'), may hold values from -6 to 6
- cotangent: bfloat16 [8, 2048, 768], P('shard', 'ctx'), may hold values from -6 to 6
- pair_order: int32 [16], replicated, may hold values from 0 to 15, each once
- norm1_gain: bfloat16 [2, 768], P(None, 'shard'), may hold values from 0.5 to 1.5
- norm1_bias: bfloat16 [2, 768], P(None, 'shard'), may hold values from -2 to 2
- qkv_weight: bfloat16 [2, 768, 2304], P(None, 'shard'), may hold values from -0.21875 to 0.21875
- query_bias: bfloat16 [2, 768], P(None, 'shard'), may hold values from -2 to 2
- value_bias: bfloat16 [2, 768], P(None, 'shard'), may hold values from -0.29882812 to 0.29882812
- out_weight: bfloat16 [2, 768, 768], P(None, 'shard'), may hold values from -1.75 to 1.75
- out_bias: bfloat16 [2, 768], P(None, 'shard'), may hold values from -2 to 2
- norm2_gain: bfloat16 [2, 768], P(None, 'shard'), may hold values from 0.5 to 1.5
- norm2_bias: bfloat16 [2, 768], P(None, 'shard'), may hold values from -2 to 2
- up_weight: bfloat16 [2, 768, 3072], P(None, 'shard'), may hold values from -0.21875 to 0.21875
- up_bias: bfloat16 [2, 3072], P(None, 'shard'), may hold values from -2 to 2
- down_weight: bfloat16 [2, 3072, 768], P(None, 'shard'), may hold values from -0.109375 to 0.109375
- down_bias: bfloat16 [2, 768], P(None, 'shard'), may hold values from -2 to 2
Outputs:
- states_out: bfloat16 [8, 2048, 768], P('shard', 'ctx')
- states_grad: bfloat16 [8, 2048, 768], P('shard', 'ctx')
- norm1_gain_grad: float32 [2, 768], P(None, 'shard')
- norm1_bias_grad: float32 [2, 768], P(None, 'shard')
- qkv_weight_grad: float32 [2, 768, 2304], P(None, 'shard')
- query_bias_grad: float32 [2, 768], P(None, 'shard')
- value_bias_grad: float32 [2, 768], P(None, 'shard')
- out_weight_grad: float32 [2, 768, 768], P(None, 'shard')
- out_bias_grad: float32 [2, 768], P(None, 'shard')
- norm2_gain_grad: float32 [2, 768], P(None, 'shard')
- norm2_bias_grad: float32 [2, 768], P(None, 'shard')
- up_weight_grad: float32 [2, 768, 3072], P(None, 'shard')
- up_bias_grad: float32 [2, 3072], P(None, 'shard')
- down_weight_grad: float32 [2, 3072, 768], P(None, 'shard')
- down_bias_grad: float32 [2, 768], P(None, 'shard')
The draws below stay inside these ranges and needn't reach their ends.
Inputs may be any that keep to these rules, and one draw needn't show every extreme that they name: `pair_order`: each number appears once.
All inputs are finite; a program needn't handle non-finite values.
Results may differ from the reference program's by a relative error of at most 0.02.
Values may be sent and summed in bfloat16 or wider, within the bound.
No kernel may reach another device: no remote copies, remote signals or barrier semaphores. Data moves between devices by JAX's collectives and lax.ppermute only.
A program may use at most 192 MiB of HBM per device.

```python
import math
import jax
import jax.numpy as jnp
from jax import lax

D = 768
H = 12
HD = 64
FF = 3072
LAYERS = 2
BLK = 64
SEQS = 8
LEN = 2048
N_CTX = 16


def level_of(key, extent, pieces, least, high):
    level = 1.0
    for position, shards_of in pieces:
        steps = jax.random.uniform(jax.random.fold_in(jax.random.fold_in(key, 6), position), (shards_of,), jnp.float32, least / len(pieces), high / len(pieces))
        level = level * jnp.repeat(jnp.exp(steps), extent[position] // shards_of).reshape((-1,) + (1,) * (len(extent) - 1 - position))
    return level


def noise(key, extent, deviation, limit, shards=(), kind=jnp.bfloat16):
    entries = deviation * jax.random.normal(key, extent, jnp.float32)
    if shards:
        entries = entries * level_of(key, extent, shards, -0.22, 0.18)
    return jnp.clip(entries, -limit, limit).astype(kind)


def setup_inputs(seed: int = 0) -> dict:
    key_list = jax.random.split(jax.random.key(seed), 17)
    states = noise(key_list[0], (SEQS, LEN, D), 1.0, 6.0, ((0, 8), (1, 16)))
    cotangent = noise(key_list[1], (SEQS, LEN, D), 1.0, 6.0, ((0, 8), (1, 16)))
    pair_order = jax.random.permutation(key_list[2], N_CTX).astype(jnp.int32)
    norm1_gain = jnp.clip(1.0 + 0.1 * jax.random.normal(key_list[3], (LAYERS, D), jnp.float32), 0.5, 1.5).astype(jnp.bfloat16)
    norm1_bias = noise(key_list[4], (LAYERS, D), 0.3, 2.0, ((1, 8),))
    qkv_weight = noise(key_list[5], (LAYERS, D, 3 * D), D ** -0.5, 0.21875, ((1, 8),))
    query_bias = noise(key_list[6], (LAYERS, D), 0.3, 2.0, ((1, 8),))
    value_bias = noise(key_list[7], (LAYERS, D), 0.05, 0.29882812, ((1, 8),))
    out_weight = noise(key_list[8], (LAYERS, D, D), (D // 64) ** -0.5, 1.75, ((1, 8),))
    out_bias = noise(key_list[9], (LAYERS, D), 0.3, 2.0, ((1, 8),))
    norm2_gain = jnp.clip(1.0 + 0.1 * jax.random.normal(key_list[10], (LAYERS, D), jnp.float32), 0.5, 1.5).astype(jnp.bfloat16)
    norm2_bias = noise(key_list[11], (LAYERS, D), 0.3, 2.0, ((1, 8),))
    up_weight = noise(key_list[12], (LAYERS, D, FF), D ** -0.5, 0.21875, ((1, 8),))
    up_bias = noise(key_list[13], (LAYERS, FF), 0.3, 2.0, ((1, 8),))
    down_weight = noise(key_list[14], (LAYERS, FF, D), FF ** -0.5, 0.109375, ((1, 8),))
    down_bias = noise(key_list[15], (LAYERS, D), 0.3, 2.0, ((1, 8),))
    return dict(states=states, cotangent=cotangent, pair_order=pair_order, norm1_gain=norm1_gain, norm1_bias=norm1_bias, qkv_weight=qkv_weight, query_bias=query_bias, value_bias=value_bias, out_weight=out_weight, out_bias=out_bias, norm2_gain=norm2_gain, norm2_bias=norm2_bias, up_weight=up_weight, up_bias=up_bias, down_weight=down_weight, down_bias=down_bias)


HIGH = lax.Precision.HIGHEST
EPSILON = 1e-05
NEGATIVE = -1e+30

@jax.custom_vjp
def low(v):
    return lax.optimization_barrier(v.astype(jnp.bfloat16)).astype(jnp.float32)

@jax.custom_vjp
def low_back(v):
    return v

def low_keep(v):
    return (low(v), None)

def low_pass(kept, grad):
    return (grad,)

def back_keep(v):
    return (v, None)

def back_low(kept, grad):
    return (low(grad),)
low.defvjp(low_keep, low_pass)
low_back.defvjp(back_keep, back_low)

def layer_norm(states, gain, shift):
    average = lax.optimization_barrier(jnp.mean(states, axis=-1, keepdims=True))
    centered = states - average
    spread = lax.optimization_barrier(jnp.mean(centered * centered, axis=-1, keepdims=True))
    return centered * lax.rsqrt(spread + EPSILON) * gain + shift

def matmul(left, right):
    return jnp.dot(left, right, precision=HIGH, preferred_element_type=jnp.float32)

def block_positions(pair_order):
    within = jnp.arange(2 * BLK, dtype=jnp.int32)
    blocks = jnp.where(within[None, :] < BLK, pair_order[:, None], 2 * N_CTX - 1 - pair_order[:, None])
    return (blocks * BLK + within[None, :] % BLK).reshape(-1).astype(jnp.int32)

def attend_block(queries, keys, values, query_pos, key_pos):
    scale = 1.0 / math.sqrt(HD)
    scores = low_back(jnp.einsum('qhd,khd->hqk', queries, keys, precision=HIGH) * scale)
    scores = jnp.where(query_pos[None, :, None] >= key_pos[None, None, :], scores, NEGATIVE)
    probs = jax.nn.softmax(scores, axis=-1)
    return jnp.einsum('hqk,khd->qhd', low(probs), values, precision=HIGH)

def attend_sequence(packed, positions):
    queries, keys, values = packed
    rows = math.gcd(LEN, 512)
    count = LEN // rows
    query_blocks = queries.reshape(count, rows, H, HD)
    pos_blocks = positions.reshape(count, rows)
    checked = jax.checkpoint(attend_block)
    result = lax.map(lambda item: checked(item[0], keys, values, item[1], positions), (query_blocks, pos_blocks))
    return result.reshape(LEN, D)

def layer_forward(states, weights, positions):
    norm1_gain, norm1_bias, qkv_weight, query_bias, value_bias, out_weight, out_bias, norm2_gain, norm2_bias, up_weight, up_bias, down_weight, down_bias = weights
    normed = low(layer_norm(states, norm1_gain, norm1_bias))
    projected = matmul(normed, qkv_weight)
    queries = low(low_back(projected[:, :D] + query_bias))
    keys = low(low_back(projected[:, D:2 * D]))
    values = low(low_back(projected[:, 2 * D:] + value_bias))
    shaped = lambda part: part.reshape(SEQS, LEN, H, HD)
    checked = jax.checkpoint(attend_sequence)
    mixed = lax.map(lambda item: checked(item, positions), (shaped(queries), shaped(keys), shaped(values)))
    mixed = low(low_back(mixed.reshape(SEQS * LEN, D)))
    attended = low_back(matmul(mixed, out_weight) + out_bias)
    middle = states + attended
    second = low(layer_norm(middle, norm2_gain, norm2_bias))
    hidden = low_back(matmul(second, up_weight) + up_bias)
    activated = low(jax.nn.gelu(hidden, approximate=True))
    return middle + low_back(matmul(activated, down_weight) + down_bias)

def reference(states, cotangent, pair_order, norm1_gain, norm1_bias, qkv_weight, query_bias, value_bias, out_weight, out_bias, norm2_gain, norm2_bias, up_weight, up_bias, down_weight, down_bias):
    positions = block_positions(pair_order)
    weights = (norm1_gain.astype(jnp.float32), norm1_bias.astype(jnp.float32), qkv_weight.astype(jnp.float32), query_bias.astype(jnp.float32), value_bias.astype(jnp.float32), out_weight.astype(jnp.float32), out_bias.astype(jnp.float32), norm2_gain.astype(jnp.float32), norm2_bias.astype(jnp.float32), up_weight.astype(jnp.float32), up_bias.astype(jnp.float32), down_weight.astype(jnp.float32), down_bias.astype(jnp.float32))

    def forward(inputs, params):
        flowing = inputs.reshape(SEQS * LEN, D)
        for layer_index in range(LAYERS):
            flowing = layer_forward(flowing, tuple((member[layer_index] for member in params)), positions)
        return flowing.reshape(SEQS, LEN, D)
    result, pullback = jax.vjp(forward, states.astype(jnp.float32), weights)
    input_grad, grads = pullback(cotangent.astype(jnp.float32))
    return (result.astype(jnp.bfloat16), input_grad.astype(jnp.bfloat16), grads[0], grads[1], grads[2], grads[3], grads[4], grads[5], grads[6], grads[7], grads[8], grads[9], grads[10], grads[11], grads[12])
```

```python
import math

import jax
import jax.numpy as jnp
from jax import lax
from jax.experimental import pallas as pl
from jax.experimental.pallas import tpu as pltpu
from jax.sharding import PartitionSpec as P

H = 12
HD = 64
D = 768
FF = 3072
LAYERS = 2
S = 8
C = 16
TOK = 128
LEN = TOK * C
BLK = TOK // 2
ROWS = 256
EPSILON = 1e-05
NEGATIVE = -1e30
F32 = jnp.float32
BF16 = jnp.bfloat16

CHIP_GROUPS = [[2 * q + core for q in range(8)] for core in range(2)]
X_GROUPS = [[8 * y + 2 * x + core for x in range(4)] for y in range(2) for core in range(2)]
SWAP = [(i, i ^ 1) for i in range(C)]


def layer_norm(states, gain, shift):
    average = jnp.mean(states, axis=-1, keepdims=True)
    centered = states - average
    spread = jnp.mean(centered * centered, axis=-1, keepdims=True)
    return centered * lax.rsqrt(spread + EPSILON) * gain + shift


def exchange(parts, axis, groups=None):
    return lax.all_to_all(parts, axis, 0, 0, tiled=True, axis_index_groups=groups)


def spread_to(part, count, axis, groups=None):
    return exchange(jnp.broadcast_to(part[None], (count,) + part.shape), axis, groups)


def swap_core(part):
    return lax.ppermute(part, "ctx", SWAP)


def gather_ctx(part):
    own = spread_to(part, 8, "ctx", CHIP_GROUPS)
    return own, swap_core(own)


def gather_x(part):
    own = spread_to(part, 4, "ctx", X_GROUPS)
    return jnp.concatenate([own, swap_core(own)], axis=0)


def scatter_x(partial):
    theirs = swap_core(partial[4:].astype(BF16))
    mine = partial[:4] + theirs.astype(F32)
    parts = exchange(mine.astype(BF16), "ctx", X_GROUPS)
    return jnp.sum(parts.astype(F32), axis=0)


def dot(left, right, dims=((1,), (0,))):
    return lax.dot_general(left, right, (dims, ((), ())), preferred_element_type=F32)


def rows_of(block):
    return pl.ds(pl.multiple_of(block * BLK, BLK), BLK)


def attend_kernel(arrive_pos, ctx_pos, normed_ref, weight_ref, shift_ref, mixed_ref, q_ref, k_ref, v_ref, out_ref):
    for step in range(LEN // ROWS):
        piece = dot(normed_ref[step * ROWS : (step + 1) * ROWS, :], weight_ref[...]) + shift_ref[...]
        for part in range(ROWS // BLK):
            rows = rows_of(arrive_pos[step * (ROWS // BLK) + part])
            block = piece[part * BLK : (part + 1) * BLK, :]
            q_ref[rows, :] = (block[:, :HD].astype(BF16).astype(F32) * 0.125).astype(BF16)
            k_ref[rows, :] = block[:, HD : 2 * HD].astype(BF16)
            v_ref[rows, :] = block[:, 2 * HD :].astype(BF16)
    keep = lax.broadcasted_iota(jnp.int32, (ROWS, ROWS), 0) >= lax.broadcasted_iota(
        jnp.int32, (ROWS, ROWS), 1
    )
    for step in range(LEN // ROWS):
        start = step * ROWS
        queries = q_ref[start : start + ROWS, :]
        near = dot(queries, k_ref[start : start + ROWS, :], ((1,), (1,)))
        near = jnp.where(keep, near, NEGATIVE)
        highest = jnp.max(near, axis=1, keepdims=True)
        if step:
            far = dot(queries, k_ref[:start, :], ((1,), (1,)))
            highest = jnp.maximum(highest, jnp.max(far, axis=1, keepdims=True))
        weights = jnp.exp(near - highest)
        total = jnp.sum(weights, axis=1, keepdims=True)
        mixed = dot(weights.astype(BF16), v_ref[start : start + ROWS, :])
        if step:
            weights = jnp.exp(far - highest)
            total = total + jnp.sum(weights, axis=1, keepdims=True)
            mixed = mixed + dot(weights.astype(BF16), v_ref[:start, :])
        out_ref[start : start + ROWS, :] = (mixed / total).astype(BF16)
    for block in range(LEN // BLK):
        mixed_ref[block * BLK : (block + 1) * BLK, :] = out_ref[rows_of(ctx_pos[block]), :]


def attend_back_kernel(
    arrive_pos, ctx_pos, q_ref, k_ref, v_ref, grad_ref, to_ctx_ref, to_arrive_ref, do_ref, dk_ref, dv_ref, all_ref
):
    for block in range(LEN // BLK):
        do_ref[rows_of(ctx_pos[block]), :] = grad_ref[block * BLK : (block + 1) * BLK, :]
    keep = lax.broadcasted_iota(jnp.int32, (ROWS, ROWS), 0) <= lax.broadcasted_iota(
        jnp.int32, (ROWS, ROWS), 1
    )
    for step in range(LEN // ROWS - 1, -1, -1):
        start = step * ROWS
        end = start + ROWS
        queries = q_ref[start:end, :]
        grads = do_ref[start:end, :]
        near_keys, near_values = k_ref[start:end, :], v_ref[start:end, :]
        near = jnp.where(keep, dot(near_keys, queries, ((1,), (1,))), NEGATIVE)
        highest = jnp.max(near, axis=0, keepdims=True)
        if step:
            far_keys, far_values = k_ref[:start, :], v_ref[:start, :]
            far = dot(far_keys, queries, ((1,), (1,)))
            highest = jnp.maximum(highest, jnp.max(far, axis=0, keepdims=True))
        near = jnp.exp(near - highest)
        total = jnp.sum(near, axis=0, keepdims=True)
        if step:
            far = jnp.exp(far - highest)
            total = total + jnp.sum(far, axis=0, keepdims=True)
        inverse = 1.0 / total
        near = near * inverse
        near_grad = dot(near_values, grads, ((1,), (1,)))
        inner = jnp.sum(near * near_grad, axis=0, keepdims=True)
        if step:
            far = far * inverse
            far_grad = dot(far_values, grads, ((1,), (1,)))
            inner = inner + jnp.sum(far * far_grad, axis=0, keepdims=True)
        near_scores = (near * (near_grad - inner)).astype(BF16)
        near_dk = dot(near_scores, queries)
        near_dv = dot(near.astype(BF16), grads)
        query_grad = dot(near_scores, near_keys, ((0,), (0,)))
        if step == LEN // ROWS - 1:
            dk_ref[start:end, :] = near_dk
            dv_ref[start:end, :] = near_dv
        else:
            dk_ref[start:end, :] += near_dk
            dv_ref[start:end, :] += near_dv
        if step:
            far_scores = (far * (far_grad - inner)).astype(BF16)
            far_dk = dot(far_scores, queries)
            far_dv = dot(far.astype(BF16), grads)
            query_grad = query_grad + dot(far_scores, far_keys, ((0,), (0,)))
            if step == LEN // ROWS - 1:
                dk_ref[:start, :] = far_dk
                dv_ref[:start, :] = far_dv
            else:
                dk_ref[:start, :] += far_dk
                dv_ref[:start, :] += far_dv
        all_ref[start:end, :] = jnp.concatenate(
            [query_grad * 0.125, dk_ref[start:end, :], dv_ref[start:end, :]], axis=1
        ).astype(BF16)
    for block in range(LEN // BLK):
        to_ctx_ref[block * BLK : (block + 1) * BLK, :] = all_ref[rows_of(ctx_pos[block]), :]
        to_arrive_ref[block * BLK : (block + 1) * BLK, :] = all_ref[rows_of(arrive_pos[block]), :]


SMEM = pl.BlockSpec(memory_space=pltpu.SMEM)
VMEM = pl.BlockSpec(memory_space=pltpu.VMEM)
VMEM_BYTES = 48 * 2**20


def attend(arrive_pos, ctx_pos, normed, weight, shift):
    head = jax.ShapeDtypeStruct((LEN, HD), BF16)
    return pl.pallas_call(
        attend_kernel,
        out_shape=(head, head, head, head),
        in_specs=[SMEM, SMEM, VMEM, VMEM, VMEM],
        out_specs=(VMEM, VMEM, VMEM, VMEM),
        scratch_shapes=[pltpu.VMEM((LEN, HD), BF16)],
        compiler_params=pltpu.CompilerParams(vmem_limit_bytes=VMEM_BYTES),
        cost_estimate=pl.CostEstimate(flops=2 * 10**9, bytes_accessed=5 * 10**6, transcendentals=2 * 10**6),
    )(arrive_pos, ctx_pos, normed, weight, shift)


def attend_back(arrive_pos, ctx_pos, queries, keys, values, grads):
    wide = jax.ShapeDtypeStruct((LEN, 3 * HD), BF16)
    return pl.pallas_call(
        attend_back_kernel,
        out_shape=(wide, wide),
        in_specs=[SMEM, SMEM, VMEM, VMEM, VMEM, VMEM],
        out_specs=(VMEM, VMEM),
        scratch_shapes=[
            pltpu.VMEM((LEN, HD), BF16),
            pltpu.VMEM((LEN, HD), F32),
            pltpu.VMEM((LEN, HD), F32),
            pltpu.VMEM((LEN, 3 * HD), BF16),
        ],
        compiler_params=pltpu.CompilerParams(vmem_limit_bytes=VMEM_BYTES),
        cost_estimate=pl.CostEstimate(flops=4 * 10**9, bytes_accessed=5 * 10**6, transcendentals=2 * 10**6),
    )(arrive_pos, ctx_pos, queries, keys, values, grads)


def join_cores(core, own, other, axis):
    return jnp.where(
        core == 0, jnp.concatenate([own, other], axis=axis), jnp.concatenate([other, own], axis=axis)
    )


def gather_halves(core, weight):
    layers, rows, columns = weight.shape
    half = columns // 2
    piece = lax.dynamic_slice_in_dim(weight, core * half, half, axis=2)
    own = lax.all_gather(piece, "shard", axis=0)
    other = swap_core(own)
    return [
        join_cores(core, own[:, layer], other[:, layer], 2).reshape(S * rows, columns) for layer in range(layers)
    ]


def forward_layer(flowing, params, small, places):
    arrive_pos, ctx_pos = places
    head_weight, out_full, up_part, down_part = params
    head_shift, vectors, up_shift = small
    gain_one, bias_one, unused, unused, out_shift, gain_two, bias_two, down_shift = vectors
    normed = layer_norm(flowing, gain_one, bias_one).astype(BF16)
    own, other = gather_ctx(normed)
    normed_all = jnp.concatenate([own, other], axis=0).reshape(LEN, D)
    mixed_head, queries, keys, values = attend(arrive_pos, ctx_pos, normed_all, head_weight, head_shift)
    mixed = exchange(mixed_head.reshape(C, TOK, HD), "ctx")[:H]
    mixed = mixed.transpose(1, 0, 2).reshape(TOK, D)
    middle = flowing + dot(mixed, out_full) + out_shift
    second = layer_norm(middle, gain_two, bias_two).astype(BF16)
    second_all = gather_x(second).reshape(8 * TOK, D)
    hidden = dot(second_all, up_part) + up_shift
    activated = jax.nn.gelu(hidden, approximate=True).astype(BF16)
    partial = dot(activated, down_part).reshape(8, TOK, D)
    output = middle + scatter_x(partial) + down_shift
    saved = (flowing, normed_all, queries, keys, values, mixed, middle, second_all, hidden, activated)
    return output, saved


def backward_layer(grad_out, saved, params, small, places):
    arrive_pos, ctx_pos = places
    qkv_full, out_full, up_part, down_part = params
    unused, vectors, unused = small
    gain_one, bias_one, unused, unused, unused, gain_two, bias_two, unused = vectors
    flowing, normed_all, queries, keys, values, mixed, middle, second_all, hidden, activated = saved
    down_in = grad_out.astype(BF16)
    down_shift_grad = jnp.sum(down_in.astype(F32), axis=0)
    down_all = gather_x(down_in).reshape(8 * TOK, D)
    activated_grad = dot(down_all, down_part, ((1,), (1,)))
    unused, gelu_back = jax.vjp(lambda inner: jax.nn.gelu(inner, approximate=True), hidden)
    hidden_grad = gelu_back(activated_grad)[0].astype(BF16)
    second_grad = scatter_x(dot(hidden_grad, up_part, ((1,), (1,))).reshape(8, TOK, D))
    down_grad = dot(activated, down_all, ((0,), (0,)))
    up_grad = dot(second_all, hidden_grad, ((0,), (0,)))
    up_shift_grad = jnp.sum(hidden_grad.astype(F32), axis=0)
    unused, norm_back = jax.vjp(layer_norm, middle, gain_two, bias_two)
    middle_part, gain_two_grad, bias_two_grad = norm_back(second_grad)
    middle_grad = grad_out + middle_part
    attended_in = middle_grad.astype(BF16)
    out_shift_grad = jnp.sum(attended_in.astype(F32), axis=0)
    mixed_grad = dot(attended_in, out_full, ((1,), (1,))).astype(BF16)
    mixed_grad = mixed_grad.reshape(TOK, H, HD).transpose(1, 0, 2)
    mixed_grad = jnp.concatenate([mixed_grad, jnp.zeros((C - H, TOK, HD), BF16)], axis=0)
    mixed_grad = exchange(mixed_grad, "ctx").reshape(LEN, HD)
    out_grad = dot(mixed, attended_in, ((0,), (0,))).astype(BF16)
    out_grad = lax.psum_scatter(out_grad, "shard", scatter_dimension=0, tiled=True)
    to_ctx, to_arrive = attend_back(arrive_pos, ctx_pos, queries, keys, values, mixed_grad)
    project_grad = exchange(to_ctx.reshape(C, TOK, 3 * HD), "ctx")[:H]
    project_grad = project_grad.reshape(H, TOK, 3, HD).transpose(1, 2, 0, 3).reshape(TOK, 3 * D)
    query_shift_grad = jnp.sum(project_grad[:, :D].astype(F32), axis=0)
    value_shift_grad = jnp.sum(project_grad[:, 2 * D :].astype(F32), axis=0)
    normed_grad = dot(project_grad, qkv_full, ((1,), (1,)))
    unused, first_back = jax.vjp(layer_norm, flowing, gain_one, bias_one)
    flowing_part, gain_one_grad, bias_one_grad = first_back(normed_grad)
    head_grad = dot(normed_all, to_arrive, ((0,), (0,)))
    shifts = (
        gain_one_grad,
        bias_one_grad,
        query_shift_grad,
        value_shift_grad,
        out_shift_grad,
        gain_two_grad,
        bias_two_grad,
        down_shift_grad,
    )
    return middle_grad + flowing_part, (head_grad, up_grad, down_grad, up_shift_grad, shifts, out_grad)


def reduce_grads(core, grads):
    head_grad, up_grad, down_grad, up_shift_grad, shifts, out_grad = grads
    heads = head_grad.astype(BF16).reshape(S, 4, 24, 3 * HD).transpose(0, 2, 1, 3).reshape(S, 24, D)
    ups = up_grad.astype(BF16).reshape(S, 2, 48, 384)
    ups = jnp.concatenate([ups[:, 0], ups[:, 1]], axis=2)
    downs = down_grad.astype(BF16).reshape(S, 48, D)
    vectors = jnp.stack(shifts).reshape(8, S, 96).transpose(1, 0, 2).reshape(S, 1, D)
    hiddens = jnp.pad(up_shift_grad.reshape(S, 1, 48), ((0, 0), (0, 0), (0, D - 48)))
    rest = jnp.concatenate([vectors, hiddens, jnp.zeros((S, 6, D), F32)], axis=1).astype(BF16)
    packed = jnp.concatenate([heads, ups, downs, rest], axis=1)
    owned = jnp.sum(exchange(packed, "shard").astype(F32), axis=0)
    outs = jnp.sum(exchange(out_grad.reshape(C, 6, D), "ctx").astype(F32), axis=0)
    owned = jnp.concatenate([owned[:122], outs], axis=0).astype(BF16)
    own, other = gather_ctx(owned)
    every = jnp.where(core == 0, jnp.stack([own, other], 1), jnp.stack([other, own], 1))
    every = every.reshape(C, 128, D)
    qkv = every[:H, :24].reshape(H, 24, 4, 3, HD).transpose(2, 1, 3, 0, 4).reshape(96, 3 * D).astype(F32)
    halves = every.reshape(2, 8, 128, D)
    ups = halves[0, :, 24:72].astype(F32) + halves[1, :, 24:72].astype(F32)
    ups = ups.reshape(8, 48, 2, S, 48).transpose(2, 1, 3, 0, 4).reshape(96, FF)
    downs = (halves[0, :, 72:120].astype(F32) + halves[1, :, 72:120].astype(F32)).reshape(384, D)
    vectors = jnp.sum(every[:, 120].astype(F32), axis=0).reshape(8, 96)
    hiddens = (halves[0, :, 121, :48].astype(F32) + halves[1, :, 121, :48].astype(F32)).reshape(384)
    outs = every[:, 122:].reshape(96, D).astype(F32)
    return (
        vectors[0],
        vectors[1],
        qkv,
        vectors[2],
        vectors[3],
        outs,
        vectors[4],
        vectors[5],
        vectors[6],
        ups,
        hiddens,
        downs,
        vectors[7],
    )


def shards(
    states,
    cotangent,
    pair_order,
    norm1_gain,
    norm1_bias,
    qkv_weight,
    query_bias,
    value_bias,
    out_weight,
    out_bias,
    norm2_gain,
    norm2_bias,
    up_weight,
    up_bias,
    down_weight,
    down_bias,
):
    place = lax.axis_index("ctx")
    core = place % 2
    rank = place % 8
    head = jnp.minimum(place, H - 1)
    pairs = jnp.stack([pair_order, 2 * C - 1 - pair_order], axis=1)
    ctx_pos = pairs.reshape(-1)
    by_core = pairs.reshape(8, 2, 2).transpose(1, 0, 2)
    arrive_pos = jnp.where(core == 0, by_core, by_core[::-1]).reshape(-1)
    places = (arrive_pos, ctx_pos)

    vectors = jnp.stack(
        [norm1_gain, norm1_bias, query_bias, value_bias, out_bias, norm2_gain, norm2_bias, down_bias]
    )
    head_piece = lax.dynamic_slice_in_dim(qkv_weight.reshape(LAYERS, 96, 3, D), head * HD, HD, axis=3)
    packed = jnp.concatenate(
        [head_piece.reshape(LAYERS * 96 * 3 * HD // D, D), vectors.reshape(2, D), up_bias.reshape(1, D)], axis=0
    )
    packed = jnp.pad(packed, ((0, 13), (0, 0)))
    gathered = spread_to(packed, S, "shard")
    head_weights = gathered[:, :48].reshape(S, LAYERS, 96, 3 * HD)
    vectors = gathered[:, 48:50].reshape(S, 8, LAYERS, 96).transpose(2, 1, 0, 3).reshape(LAYERS, 8, D)
    vectors = vectors.astype(F32)
    up_shifts = gathered[:, 50].reshape(S, LAYERS, 8, 48)
    up_shifts = lax.dynamic_index_in_dim(up_shifts, rank, 2, False).transpose(1, 0, 2).reshape(LAYERS, 1, 384)
    up_shifts = up_shifts.astype(F32)
    head_shifts = jnp.concatenate(
        [
            lax.dynamic_slice_in_dim(vectors[:, 2], head * HD, HD, axis=1),
            jnp.zeros((LAYERS, HD), F32),
            lax.dynamic_slice_in_dim(vectors[:, 3], head * HD, HD, axis=1),
        ],
        axis=1,
    ).reshape(LAYERS, 1, 3 * HD)

    out_full = gather_halves(core, out_weight)
    unit = lax.broadcasted_iota(jnp.int32, (FF, 384), 0)
    column = lax.broadcasted_iota(jnp.int32, (FF, 384), 1)
    pick = (unit == (column // 48) * 384 + rank * 48 + column % 48).astype(BF16)
    up_piece = dot(up_weight.reshape(LAYERS * 96, FF), pick).astype(BF16).reshape(LAYERS, 96, 384)
    down_piece = lax.dynamic_slice_in_dim(down_weight, rank * 48, 48, axis=1)
    up_parts, down_parts = [], []
    for layer in range(LAYERS):
        up_parts.append(lax.all_gather(up_piece[layer], "shard", axis=0, tiled=True))
        down_parts.append(lax.all_gather(down_piece[layer], "shard", axis=0, tiled=True))
    qkv_full = gather_halves(core, qkv_weight)

    flowing = states.reshape(TOK, D).astype(F32)
    saved_all = []
    smalls = []
    for layer in range(LAYERS):
        small = (
            head_shifts[layer],
            [vectors[layer, member : member + 1] for member in range(8)],
            up_shifts[layer],
        )
        small = (small[0], [member.reshape(D) for member in small[1]], small[2])
        smalls.append(small)
        head_weight = head_weights[:, layer].reshape(D, 3 * HD)
        params = (head_weight, out_full[layer], up_parts[layer], down_parts[layer])
        flowing, saved = forward_layer(flowing, params, small, places)
        saved_all.append(saved)
    result = flowing.astype(BF16).reshape(states.shape)
    grad_flow = cotangent.reshape(TOK, D).astype(F32)
    collected = [None] * LAYERS
    for layer in range(LAYERS - 1, -1, -1):
        params = (qkv_full[layer], out_full[layer], up_parts[layer], down_parts[layer])
        grad_flow, grads = backward_layer(grad_flow, saved_all[layer], params, smalls[layer], places)
        collected[layer] = reduce_grads(core, grads)
    stacked = tuple(
        jnp.stack([collected[layer][member] for layer in range(LAYERS)]) for member in range(13)
    )
    return (result, grad_flow.astype(BF16).reshape(states.shape)) + stacked


def solution(mesh):
    matrix = P(None, "shard", None)
    vector = P(None, "shard")
    rows = P("shard", "ctx", None)
    params = (
        vector,
        vector,
        matrix,
        vector,
        vector,
        matrix,
        vector,
        vector,
        vector,
        matrix,
        vector,
        matrix,
        vector,
    )
    return jax.shard_map(
        shards,
        mesh=mesh,
        in_specs=(rows, rows, P()) + params,
        out_specs=(rows, rows) + params,
        check_vma=False,
    )
```

```python
import functools

import jax
import jax.numpy as jnp
from jax import lax
from jax.experimental import pallas as pl
from jax.experimental.pallas import tpu as pltpu
from jax.sharding import PartitionSpec as P

H = 12
HD = 64
D = 768
FF = 3072
LAYERS = 2
S = 8
C = 16
TOK = 128
LEN = TOK * C
BLK = TOK // 2
ROWS = 256
EPSILON = 1e-05
NEGATIVE = -1e30
F32 = jnp.float32
BF16 = jnp.bfloat16

CHIP_GROUPS = [[2 * q + core for q in range(8)] for core in range(2)]
X_GROUPS = [[8 * y + 2 * x + core for x in range(4)] for y in range(2) for core in range(2)]
SWAP = [(i, i ^ 1) for i in range(C)]


def layer_norm(states, gain, shift):
    average = jnp.mean(states, axis=-1, keepdims=True)
    centered = states - average
    spread = jnp.mean(centered * centered, axis=-1, keepdims=True)
    return centered * lax.rsqrt(spread + EPSILON) * gain + shift


def exchange(parts, axis, groups=None):
    return lax.all_to_all(parts, axis, 0, 0, tiled=True, axis_index_groups=groups)


def spread_to(part, count, axis, groups=None):
    return exchange(jnp.broadcast_to(part[None], (count,) + part.shape), axis, groups)


def swap_core(part):
    return lax.ppermute(part, "ctx", SWAP)


def gather_ctx(part):
    own = spread_to(part, 8, "ctx", CHIP_GROUPS)
    return own, swap_core(own)


def gather_x(part):
    own = spread_to(part, 4, "ctx", X_GROUPS)
    return jnp.concatenate([own, swap_core(own)], axis=0)


def scatter(near, far, groups):
    mine = near.astype(F32) + swap_core(far.astype(BF16)).astype(F32)
    parts = exchange(mine.astype(BF16), "ctx", groups)
    return jnp.sum(parts.astype(F32), axis=0)


def scatter_x(partial):
    return scatter(partial[:4], partial[4:], X_GROUPS)


def dot(left, right, dims=((1,), (0,))):
    return lax.dot_general(left, right, (dims, ((), ())), preferred_element_type=F32)


def rows_of(block):
    return pl.ds(pl.multiple_of(block * BLK, BLK), BLK)


def attend_kernel(fresh, arrive_pos, ctx_pos, own_ref, other_ref, weight_ref, shift_ref, *rest):
    if fresh:
        gain_ref, bias_ref, mixed_ref, q_ref, k_ref, v_ref, own_normed, other_normed, out_ref = rest
    else:
        mixed_ref, q_ref, k_ref, v_ref, out_ref = rest
    for step in range(LEN // ROWS):
        half = LEN // ROWS // 2
        source = own_ref if step < half else other_ref
        rows = slice(step % half * ROWS, (step % half + 1) * ROWS)
        normed = source[rows, :]
        if fresh:
            normed = layer_norm(normed.astype(F32), gain_ref[...], bias_ref[...]).astype(BF16)
            (own_normed if step < half else other_normed)[rows, :] = normed
        piece = dot(normed, weight_ref[...]) + shift_ref[...]
        for part in range(ROWS // BLK):
            rows = rows_of(arrive_pos[step * (ROWS // BLK) + part])
            block = piece[part * BLK : (part + 1) * BLK, :]
            q_ref[rows, :] = (block[:, :HD].astype(BF16).astype(F32) * 0.125).astype(BF16)
            k_ref[rows, :] = block[:, HD : 2 * HD].astype(BF16)
            v_ref[rows, :] = block[:, 2 * HD :].astype(BF16)
    keep = lax.broadcasted_iota(jnp.int32, (ROWS, ROWS), 0) >= lax.broadcasted_iota(
        jnp.int32, (ROWS, ROWS), 1
    )
    for step in range(LEN // ROWS):
        start = step * ROWS
        queries = q_ref[start : start + ROWS, :]
        near = dot(queries, k_ref[start : start + ROWS, :], ((1,), (1,)))
        near = jnp.where(keep, near, NEGATIVE)
        highest = jnp.max(near, axis=1, keepdims=True)
        if step:
            far = dot(queries, k_ref[:start, :], ((1,), (1,)))
            highest = jnp.maximum(highest, jnp.max(far, axis=1, keepdims=True))
        weights = jnp.exp(near - highest)
        total = jnp.sum(weights, axis=1, keepdims=True)
        mixed = dot(weights.astype(BF16), v_ref[start : start + ROWS, :])
        if step:
            weights = jnp.exp(far - highest)
            total = total + jnp.sum(weights, axis=1, keepdims=True)
            mixed = mixed + dot(weights.astype(BF16), v_ref[:start, :])
        out_ref[start : start + ROWS, :] = (mixed / total).astype(BF16)
    for block in range(LEN // BLK):
        mixed_ref[block * BLK : (block + 1) * BLK, :] = out_ref[rows_of(ctx_pos[block]), :]


def attend_back_kernel(
    arrive_pos, ctx_pos, q_ref, k_ref, v_ref, grad_ref, weight_ref,
    to_arrive_ref, near_ref, far_ref, sums_ref, do_ref, dk_ref, dv_ref, all_ref
):
    for block in range(LEN // BLK):
        do_ref[rows_of(ctx_pos[block]), :] = grad_ref[block * BLK : (block + 1) * BLK, :]
    keep = lax.broadcasted_iota(jnp.int32, (ROWS, ROWS), 0) <= lax.broadcasted_iota(
        jnp.int32, (ROWS, ROWS), 1
    )
    for step in range(LEN // ROWS - 1, -1, -1):
        start = step * ROWS
        end = start + ROWS
        queries = q_ref[start:end, :]
        grads = do_ref[start:end, :]
        near_keys, near_values = k_ref[start:end, :], v_ref[start:end, :]
        near = jnp.where(keep, dot(near_keys, queries, ((1,), (1,))), NEGATIVE)
        highest = jnp.max(near, axis=0, keepdims=True)
        if step:
            far_keys, far_values = k_ref[:start, :], v_ref[:start, :]
            far = dot(far_keys, queries, ((1,), (1,)))
            highest = jnp.maximum(highest, jnp.max(far, axis=0, keepdims=True))
        near = jnp.exp(near - highest)
        total = jnp.sum(near, axis=0, keepdims=True)
        if step:
            far = jnp.exp(far - highest)
            total = total + jnp.sum(far, axis=0, keepdims=True)
        inverse = 1.0 / total
        near = near * inverse
        near_grad = dot(near_values, grads, ((1,), (1,)))
        inner = jnp.sum(near * near_grad, axis=0, keepdims=True)
        if step:
            far = far * inverse
            far_grad = dot(far_values, grads, ((1,), (1,)))
            inner = inner + jnp.sum(far * far_grad, axis=0, keepdims=True)
        near_scores = (near * (near_grad - inner)).astype(BF16)
        near_dk = dot(near_scores, queries)
        near_dv = dot(near.astype(BF16), grads)
        query_grad = dot(near_scores, near_keys, ((0,), (0,)))
        if step == LEN // ROWS - 1:
            dk_ref[start:end, :] = near_dk
            dv_ref[start:end, :] = near_dv
        else:
            dk_ref[start:end, :] += near_dk
            dv_ref[start:end, :] += near_dv
        if step:
            far_scores = (far * (far_grad - inner)).astype(BF16)
            far_dk = dot(far_scores, queries)
            far_dv = dot(far.astype(BF16), grads)
            query_grad = query_grad + dot(far_scores, far_keys, ((0,), (0,)))
            if step == LEN // ROWS - 1:
                dk_ref[:start, :] = far_dk
                dv_ref[:start, :] = far_dv
            else:
                dk_ref[:start, :] += far_dk
                dv_ref[:start, :] += far_dv
        all_ref[start:end, :] = jnp.concatenate(
            [query_grad * 0.125, dk_ref[start:end, :], dv_ref[start:end, :]], axis=1
        ).astype(BF16)
    for block in range(LEN // BLK):
        to_arrive_ref[block * BLK : (block + 1) * BLK, : 3 * HD] = all_ref[rows_of(arrive_pos[block]), :]
    to_arrive_ref[:, 3 * HD :] = jnp.zeros((LEN, HD), BF16)
    sums_ref[...] = jnp.sum(all_ref[...].astype(F32), axis=0, keepdims=True)
    for step in range(LEN // ROWS):
        rows = slice(step * ROWS, (step + 1) * ROWS)
        part = dot(to_arrive_ref[rows, : 3 * HD], weight_ref[...], ((1,), (1,))).astype(BF16)
        if step * ROWS < LEN // 2:
            near_ref[rows, :] = part
        else:
            far_ref[step * ROWS - LEN // 2 : (step + 1) * ROWS - LEN // 2, :] = part


SMEM = pl.BlockSpec(memory_space=pltpu.SMEM)
VMEM = pl.BlockSpec(memory_space=pltpu.VMEM)
VMEM_BYTES = 48 * 2**20


def attend(arrive_pos, ctx_pos, own, other, weight, shift, norm=None):
    head = jax.ShapeDtypeStruct((LEN, HD), BF16)
    fresh = norm is not None
    outs = (head,) * 4
    extra = ()
    if fresh:
        outs = outs + (jax.ShapeDtypeStruct((LEN // 2, D), BF16),) * 2
        extra = tuple(member.reshape(1, D) for member in norm)
    return pl.pallas_call(
        functools.partial(attend_kernel, fresh),
        out_shape=outs,
        in_specs=[SMEM, SMEM] + [VMEM] * (4 + len(extra)),
        out_specs=(VMEM,) * len(outs),
        scratch_shapes=[pltpu.VMEM((LEN, HD), BF16)],
        compiler_params=pltpu.CompilerParams(vmem_limit_bytes=VMEM_BYTES),
        cost_estimate=pl.CostEstimate(flops=2 * 10**9, bytes_accessed=5 * 10**6, transcendentals=2 * 10**6),
    )(arrive_pos, ctx_pos, own, other, weight, shift, *extra)


def attend_back(arrive_pos, ctx_pos, queries, keys, values, grads, weight):
    return pl.pallas_call(
        attend_back_kernel,
        out_shape=(
            jax.ShapeDtypeStruct((LEN, 4 * HD), BF16),
            jax.ShapeDtypeStruct((LEN // 2, D), BF16),
            jax.ShapeDtypeStruct((LEN // 2, D), BF16),
            jax.ShapeDtypeStruct((1, 3 * HD), F32),
        ),
        in_specs=[SMEM, SMEM] + [VMEM] * 5,
        out_specs=(VMEM,) * 4,
        scratch_shapes=[
            pltpu.VMEM((LEN, HD), BF16),
            pltpu.VMEM((LEN, HD), F32),
            pltpu.VMEM((LEN, HD), F32),
            pltpu.VMEM((LEN, 3 * HD), BF16),
        ],
        compiler_params=pltpu.CompilerParams(vmem_limit_bytes=VMEM_BYTES),
        cost_estimate=pl.CostEstimate(flops=4 * 10**9, bytes_accessed=5 * 10**6, transcendentals=2 * 10**6),
    )(arrive_pos, ctx_pos, queries, keys, values, grads, weight)


HEADS, UPS, DOWNS, SMALL, OUTS, PACKED = 0, 32, 80, 128, 144, 240


def weight_grads_kernel(
    own_ref, other_ref, arrive_ref, second_ref, hidden_ref, active_ref, down_ref, mixed_ref, attended_ref, small_ref, out_ref
):
    both = ((0,), (0,))
    half = LEN // 2
    heads = dot(own_ref[...], arrive_ref[:half, :], both) + dot(other_ref[...], arrive_ref[half:, :], both)
    heads = heads.astype(BF16)
    for owner in range(S):
        for part in range(3):
            first = owner * 96 + part * 32
            out_ref[owner, HEADS:UPS, part * 256 : (part + 1) * 256] = heads[first : first + 32, :]
    ups = dot(second_ref[...], hidden_ref[...], both).astype(BF16)
    for owner in range(S):
        for part in range(2):
            first = owner * 96 + part * 48
            out_ref[owner, UPS:DOWNS, part * 384 : (part + 1) * 384] = ups[first : first + 48, :]
    downs = dot(active_ref[...], down_ref[...], both).astype(BF16)
    for owner in range(S):
        out_ref[owner, DOWNS:SMALL, :] = downs[owner * 48 : (owner + 1) * 48, :]
        out_ref[owner, SMALL:OUTS, :] = small_ref[owner]
    outs = dot(mixed_ref[...], attended_ref[...], both).astype(BF16)
    for owner in range(S):
        out_ref[owner, OUTS:PACKED, :] = outs[owner * 96 : (owner + 1) * 96, :]


def weight_grads(*parts):
    return pl.pallas_call(
        weight_grads_kernel,
        out_shape=jax.ShapeDtypeStruct((S, PACKED, D), BF16),
        in_specs=[VMEM] * len(parts),
        out_specs=VMEM,
        compiler_params=pltpu.CompilerParams(vmem_limit_bytes=VMEM_BYTES),
        cost_estimate=pl.CostEstimate(flops=2 * 10**9, bytes_accessed=12 * 10**6, transcendentals=0),
    )(*parts)


def unpack_kernel(slots, first_ref, second_ref, qkv_ref, out_ref, up_ref, down_ref, up_shift_ref, *vector_refs):
    for layer, source in enumerate((first_ref, second_ref)):
        def slot(place, layer=layer):
            return slots[layer * C + place]

        for head in range(H):
            block = source[slot(head), HEADS:UPS, :].astype(F32)
            for part in range(3):
                for kind in range(3):
                    lane = part * 256 + kind * HD
                    column = kind * D + head * HD
                    qkv_ref[layer, part * 32 : (part + 1) * 32, column : column + HD] = block[:, lane : lane + HD]
        for rank in range(8):
            low, high = slot(rank), slot(rank + 8)
            block = source[low, UPS:DOWNS, :].astype(F32) + source[high, UPS:DOWNS, :].astype(F32)
            for part in range(2):
                for owner in range(S):
                    lane = part * 384 + owner * 48
                    column = owner * 384 + rank * 48
                    up_ref[layer, part * 48 : (part + 1) * 48, column : column + 48] = block[:, lane : lane + 48]
            block = source[low, DOWNS:SMALL, :].astype(F32) + source[high, DOWNS:SMALL, :].astype(F32)
            down_ref[layer, rank * 48 : (rank + 1) * 48, :] = block
            small = source[low, SMALL:OUTS, :].astype(F32) + source[high, SMALL:OUTS, :].astype(F32)
            up_shift_ref[layer : layer + 1, rank * 48 : (rank + 1) * 48] = small[1:2, :48]
            vectors = small[0:1, :] if rank == 0 else vectors + small[0:1, :]
        for member, ref in enumerate(vector_refs):
            ref[layer : layer + 1, :] = vectors[:, member * 96 : (member + 1) * 96]
    for place in range(C):
        small = first_ref[slots[place], SMALL:OUTS, :].astype(F32)
        for layer in range(LAYERS):
            out_ref[layer, place * 6 : (place + 1) * 6, :] = small[2 + 6 * layer : 8 + 6 * layer, :]


def unpack(slots, first, second):
    shapes = [(96, 3 * D), (96, D), (96, FF), (384, D), (384,)] + [(96,)] * 8
    return pl.pallas_call(
        unpack_kernel,
        out_shape=tuple(jax.ShapeDtypeStruct((LAYERS,) + shape, F32) for shape in shapes),
        in_specs=[SMEM, VMEM, VMEM],
        out_specs=(VMEM,) * len(shapes),
        compiler_params=pltpu.CompilerParams(vmem_limit_bytes=VMEM_BYTES),
        cost_estimate=pl.CostEstimate(flops=10**6, bytes_accessed=14 * 10**6, transcendentals=0),
    )(slots, first, second)


def join_cores(core, own, other, axis):
    return jnp.where(
        core == 0, jnp.concatenate([own, other], axis=axis), jnp.concatenate([other, own], axis=axis)
    )


def forward_layer(flowing, params, small, places, gathered=None, carried=None):
    arrive_pos, ctx_pos = places
    head_weight, out_full, up_part, down_part = params
    head_shift, vectors, up_shift = small
    gain_one, bias_one, unused, unused, out_shift, gain_two, bias_two, down_shift = vectors
    if gathered is not None:
        mixed_head, queries, keys, values, own, other = attend(
            arrive_pos, ctx_pos, *gathered, head_weight, head_shift, (gain_one, bias_one)
        )
    else:
        normed = layer_norm(flowing, gain_one, bias_one).astype(BF16)
        own, other = (part.reshape(LEN // 2, D) for part in gather_ctx(normed))
        mixed_head, queries, keys, values = attend(arrive_pos, ctx_pos, own, other, head_weight, head_shift)
    mixed = exchange(mixed_head.reshape(C, TOK, HD), "ctx")[:H]
    mixed = mixed.transpose(1, 0, 2).reshape(TOK, D)
    middle = flowing + dot(mixed, out_full) + out_shift
    second = layer_norm(middle, gain_two, bias_two).astype(BF16)
    if carried is not None:
        both = gather_x(jnp.concatenate([second, carried], axis=0))
        second_all = both[:, :TOK].reshape(8 * TOK, D)
        carried = both[:, TOK:].reshape(8 * TOK, D)
    else:
        second_all = gather_x(second).reshape(8 * TOK, D)
    hidden = dot(second_all, up_part) + up_shift
    activated = jax.nn.gelu(hidden, approximate=True).astype(BF16)
    partial = dot(activated, down_part).reshape(8, TOK, D)
    output = middle + scatter_x(partial) + down_shift
    saved = (flowing, own, other, queries, keys, values, mixed, middle, second_all, hidden, activated)
    return output, saved, carried


def backward_layer(grad_out, down_all, saved, params, small, places, head, running=None):
    arrive_pos, ctx_pos = places
    head_weight, out_full, up_part, down_part = params
    unused, vectors, unused = small
    gain_one, bias_one, unused, unused, unused, gain_two, bias_two, unused = vectors
    flowing, own, other, queries, keys, values, mixed, middle, second_all, hidden, activated = saved
    down_in = grad_out.astype(BF16)
    down_shift_grad = jnp.sum(down_in.astype(F32), axis=0)
    if down_all is None:
        down_all = gather_x(down_in).reshape(8 * TOK, D)
    activated_grad = dot(down_all, down_part, ((1,), (1,)))
    unused, gelu_back = jax.vjp(lambda inner: jax.nn.gelu(inner, approximate=True), hidden)
    hidden_grad = gelu_back(activated_grad)[0].astype(BF16)
    second_grad = scatter_x(dot(hidden_grad, up_part, ((1,), (1,))).reshape(8, TOK, D))
    up_shift_grad = jnp.sum(hidden_grad.astype(F32), axis=0)
    unused, norm_back = jax.vjp(layer_norm, middle, gain_two, bias_two)
    middle_part, gain_two_grad, bias_two_grad = norm_back(second_grad)
    middle_grad = grad_out + middle_part
    attended_in = middle_grad.astype(BF16)
    out_shift_grad = jnp.sum(attended_in.astype(F32), axis=0)
    mixed_grad = dot(attended_in, out_full, ((1,), (1,))).astype(BF16)
    mixed_grad = mixed_grad.reshape(TOK, H, HD).transpose(1, 0, 2)
    mixed_grad = jnp.concatenate([mixed_grad, jnp.zeros((C - H, TOK, HD), BF16)], axis=0)
    mixed_grad = exchange(mixed_grad, "ctx").reshape(LEN, HD)
    if running is not None:
        mixed_grad, running = lax.optimization_barrier((mixed_grad, running))
    to_arrive, near, far, sums = attend_back(
        arrive_pos, ctx_pos, queries, keys, values, mixed_grad, head_weight
    )
    normed_grad = scatter(near.reshape(8, TOK, D), far.reshape(8, TOK, D), CHIP_GROUPS)
    sums = jnp.where(lax.axis_index("ctx") < H, sums[0], 0.0)
    query_shift_grad = lax.dynamic_update_slice_in_dim(jnp.zeros((D,), F32), sums[:HD], head * HD, 0)
    value_shift_grad = lax.dynamic_update_slice_in_dim(jnp.zeros((D,), F32), sums[2 * HD :], head * HD, 0)
    unused, first_back = jax.vjp(layer_norm, flowing, gain_one, bias_one)
    flowing_part, gain_one_grad, bias_one_grad = first_back(normed_grad)
    shifts = (
        gain_one_grad,
        bias_one_grad,
        query_shift_grad,
        value_shift_grad,
        out_shift_grad,
        gain_two_grad,
        bias_two_grad,
        down_shift_grad,
    )
    vectors = jnp.stack(shifts).reshape(8, S, 96).transpose(1, 0, 2).reshape(S, 1, D)
    hiddens = jnp.pad(up_shift_grad.reshape(S, 1, 48), ((0, 0), (0, 0), (0, D - 48)))
    rest = jnp.concatenate([vectors, hiddens, jnp.zeros((S, 14, D), F32)], axis=1).astype(BF16)
    packed = weight_grads(
        own, other, to_arrive, second_all, hidden_grad, activated, down_all, mixed, attended_in, rest
    )
    return middle_grad + flowing_part, packed, running


def shards(
    states,
    cotangent,
    pair_order,
    norm1_gain,
    norm1_bias,
    qkv_weight,
    query_bias,
    value_bias,
    out_weight,
    out_bias,
    norm2_gain,
    norm2_bias,
    up_weight,
    up_bias,
    down_weight,
    down_bias,
):
    place = lax.axis_index("ctx")
    core = place % 2
    rank = place % 8
    head = jnp.minimum(place, H - 1)
    pairs = jnp.stack([pair_order, 2 * C - 1 - pair_order], axis=1)
    ctx_pos = pairs.reshape(-1)
    by_core = pairs.reshape(8, 2, 2).transpose(1, 0, 2)
    arrive_pos = jnp.where(core == 0, by_core, by_core[::-1]).reshape(-1)
    places = (arrive_pos, ctx_pos)

    states_all = tuple(part.reshape(LEN // 2, D) for part in gather_ctx(states.reshape(TOK, D)))

    unit = lax.broadcasted_iota(jnp.int32, (FF, 384), 0)
    column = lax.broadcasted_iota(jnp.int32, (FF, 384), 1)
    pick = (unit == (column // 48) * 384 + rank * 48 + column % 48).astype(BF16)
    up_piece = dot(up_weight.reshape(LAYERS * 96, FF), pick).astype(BF16).reshape(LAYERS, 96, 384)
    down_piece = lax.dynamic_slice_in_dim(down_weight, rank * 48, 48, axis=1)
    out_piece = lax.dynamic_slice_in_dim(out_weight, core * 384, 384, axis=2)

    def beside(piece):
        return jnp.concatenate([piece[:48], piece[48:]], axis=1)

    def apart(piece):
        return jnp.concatenate([piece[..., :384], piece[..., 384:]], axis=1).reshape(D, 384)

    def split(rows):
        own = apart(rows[:, :48])
        out_full = join_cores(core, own, swap_core(own), 1)
        return out_full, apart(rows[:, 48:96]), rows[:, 96:].reshape(384, D)

    layer_pieces = [
        jnp.concatenate([beside(out_piece[layer]), beside(up_piece[layer]), down_piece[layer]], axis=0)
        for layer in range(LAYERS)
    ]

    vectors = jnp.stack(
        [norm1_gain, norm1_bias, query_bias, value_bias, out_bias, norm2_gain, norm2_bias, down_bias]
    )
    head_piece = lax.dynamic_slice_in_dim(qkv_weight.reshape(LAYERS, 96, 3, D), head * HD, HD, axis=3)
    head_piece = jnp.where(place < H, head_piece, jnp.zeros_like(head_piece))
    packed = jnp.concatenate(
        [
            head_piece.reshape(LAYERS * 96 * 3 * HD // D, D),
            vectors.reshape(2, D),
            up_bias.reshape(1, D),
            jnp.zeros((13, D), BF16),
            layer_pieces[0],
            layer_pieces[1],
        ],
        axis=0,
    )
    gathered = spread_to(packed, S, "shard")
    layer_weights = [split(gathered[:, 64:208]), split(gathered[:, 208:])]
    head_weights = gathered[:, :48].reshape(S, LAYERS, 96, 3 * HD)
    vectors = gathered[:, 48:50].reshape(S, 8, LAYERS, 96).transpose(2, 1, 0, 3).reshape(LAYERS, 8, D)
    vectors = vectors.astype(F32)
    up_shifts = gathered[:, 50].reshape(S, LAYERS, 8, 48)
    up_shifts = lax.dynamic_index_in_dim(up_shifts, rank, 2, False).transpose(1, 0, 2).reshape(LAYERS, 1, 384)
    up_shifts = up_shifts.astype(F32)
    head_shifts = jnp.concatenate(
        [
            lax.dynamic_slice_in_dim(vectors[:, 2], head * HD, HD, axis=1),
            jnp.zeros((LAYERS, HD), F32),
            lax.dynamic_slice_in_dim(vectors[:, 3], head * HD, HD, axis=1),
        ],
        axis=1,
    ).reshape(LAYERS, 1, 3 * HD)

    flowing = states.reshape(TOK, D).astype(F32)
    saved_all = []
    smalls = []
    all_params = []
    for layer in range(LAYERS):
        small = (
            head_shifts[layer],
            [vectors[layer, member : member + 1] for member in range(8)],
            up_shifts[layer],
        )
        small = (small[0], [member.reshape(D) for member in small[1]], small[2])
        smalls.append(small)
        params = (head_weights[:, layer].reshape(D, 3 * HD),) + layer_weights[layer]
        all_params.append(params)
        flowing, saved, carried = forward_layer(
            flowing,
            params,
            small,
            places,
            gathered=states_all if layer == 0 else None,
            carried=cotangent.reshape(TOK, D) if layer == LAYERS - 1 else None,
        )
        saved_all.append(saved)
    result = flowing.astype(BF16).reshape(states.shape)
    grad_flow = cotangent.reshape(TOK, D).astype(F32)
    grad_flow, packed, unused = backward_layer(
        grad_flow, carried, saved_all[1], all_params[1], smalls[1], places, head
    )
    grad_flow, packed = lax.optimization_barrier((grad_flow, packed))
    owned_last = lax.psum_scatter(packed.reshape(S * PACKED, D), "shard", scatter_dimension=0, tiled=True)
    grad_flow, packed, owned_last = backward_layer(
        grad_flow, None, saved_all[0], all_params[0], smalls[0], places, head, owned_last
    )
    every_last = lax.all_gather(owned_last[:OUTS], "ctx", axis=0)
    owned = jnp.sum(exchange(packed, "shard").astype(F32), axis=0).astype(BF16)
    outs = jnp.stack([owned[OUTS:], owned_last[OUTS:]]).reshape(LAYERS, C, 6, D)
    outs = outs.transpose(1, 0, 2, 3).reshape(C, 12, D)
    outs = exchange(jnp.pad(outs, ((0, 0), (0, 4), (0, 0))), "ctx").astype(F32)
    outs = jnp.sum(outs, axis=0)[:12].astype(BF16)
    owned = jnp.concatenate([owned[: SMALL + 2], outs, jnp.zeros((2, D), BF16)], axis=0)
    every = jnp.concatenate(gather_ctx(owned), axis=0)
    places_of = jnp.arange(C, dtype=jnp.int32)
    slots = jnp.concatenate([places_of // 2 + 8 * (places_of % 2 != core).astype(jnp.int32), places_of])
    qkv, outs, ups, downs, hiddens, *vectors = unpack(slots, every, every_last)
    return (
        result,
        grad_flow.astype(BF16).reshape(states.shape),
        vectors[0],
        vectors[1],
        qkv,
        vectors[2],
        vectors[3],
        outs,
        vectors[4],
        vectors[5],
        vectors[6],
        ups,
        hiddens,
        downs,
        vectors[7],
    )


def solution(mesh):
    matrix = P(None, "shard", None)
    vector = P(None, "shard")
    rows = P("shard", "ctx", None)
    params = (
        vector,
        vector,
        matrix,
        vector,
        vector,
        matrix,
        vector,
        vector,
        vector,
        matrix,
        vector,
        matrix,
        vector,
    )
    return jax.shard_map(
        shards,
        mesh=mesh,
        in_specs=(rows, rows, P()) + params,
        out_specs=(rows, rows) + params,
        check_vma=False,
    )
```

```python
import functools

import jax
import jax.numpy as jnp
from jax import lax
from jax.experimental import pallas as pl
from jax.experimental.pallas import tpu as pltpu
from jax.sharding import PartitionSpec as P

H = 12
HD = 64
D = 768
FF = 3072
LAYERS = 2
S = 8
C = 16
TOK = 128
LEN = TOK * C
BLK = TOK // 2
ROWS = 256
EPSILON = 1e-05
NEGATIVE = -1e30
F32 = jnp.float32
BF16 = jnp.bfloat16

CHIP_GROUPS = [[2 * q + core for q in range(8)] for core in range(2)]
X_GROUPS = [[8 * y + 2 * x + core for x in range(4)] for y in range(2) for core in range(2)]
SWAP = [(i, i ^ 1) for i in range(C)]


def layer_norm(states, gain, shift):
    average = jnp.mean(states, axis=-1, keepdims=True)
    centered = states - average
    spread = jnp.mean(centered * centered, axis=-1, keepdims=True)
    return centered * lax.rsqrt(spread + EPSILON) * gain + shift


def exchange(parts, axis, groups=None):
    return lax.all_to_all(parts, axis, 0, 0, tiled=True, axis_index_groups=groups)


def spread_to(part, count, axis, groups=None):
    return exchange(jnp.broadcast_to(part[None], (count,) + part.shape), axis, groups)


def swap_core(part):
    return lax.ppermute(part, "ctx", SWAP)


def gather_ctx(part):
    own = spread_to(part, 8, "ctx", CHIP_GROUPS)
    return own, swap_core(own)


def gather_x(part):
    own = spread_to(part, 4, "ctx", X_GROUPS)
    return jnp.concatenate([own, swap_core(own)], axis=0)


def scatter(near, far, groups):
    mine = near.astype(F32) + swap_core(far.astype(BF16)).astype(F32)
    parts = exchange(mine.astype(BF16), "ctx", groups)
    return jnp.sum(parts.astype(F32), axis=0)


def scatter_x(partial):
    return scatter(partial[:4], partial[4:], X_GROUPS)


def dot(left, right, dims=((1,), (0,))):
    return lax.dot_general(left, right, (dims, ((), ())), preferred_element_type=F32)


def rows_of(block):
    return pl.ds(pl.multiple_of(block * BLK, BLK), BLK)


def attend_kernel(fresh, arrive_pos, ctx_pos, own_ref, other_ref, weight_ref, shift_ref, *rest):
    if fresh:
        gain_ref, bias_ref, mixed_ref, q_ref, k_ref, v_ref, own_normed, other_normed, out_ref = rest
    else:
        mixed_ref, q_ref, k_ref, v_ref, out_ref = rest
    for step in range(LEN // ROWS):
        half = LEN // ROWS // 2
        source = own_ref if step < half else other_ref
        rows = slice(step % half * ROWS, (step % half + 1) * ROWS)
        normed = source[rows, :]
        if fresh:
            normed = layer_norm(normed.astype(F32), gain_ref[...], bias_ref[...]).astype(BF16)
            (own_normed if step < half else other_normed)[rows, :] = normed
        piece = dot(normed, weight_ref[...]) + shift_ref[...]
        for part in range(ROWS // BLK):
            rows = rows_of(arrive_pos[step * (ROWS // BLK) + part])
            block = piece[part * BLK : (part + 1) * BLK, :]
            q_ref[rows, :] = (block[:, :HD].astype(BF16).astype(F32) * 0.125).astype(BF16)
            k_ref[rows, :] = block[:, HD : 2 * HD].astype(BF16)
            v_ref[rows, :] = block[:, 2 * HD :].astype(BF16)
    keep = lax.broadcasted_iota(jnp.int32, (ROWS, ROWS), 0) >= lax.broadcasted_iota(
        jnp.int32, (ROWS, ROWS), 1
    )
    for step in range(LEN // ROWS):
        start = step * ROWS
        queries = q_ref[start : start + ROWS, :]
        near = dot(queries, k_ref[start : start + ROWS, :], ((1,), (1,)))
        near = jnp.where(keep, near, NEGATIVE)
        highest = jnp.max(near, axis=1, keepdims=True)
        if step:
            far = dot(queries, k_ref[:start, :], ((1,), (1,)))
            highest = jnp.maximum(highest, jnp.max(far, axis=1, keepdims=True))
        weights = jnp.exp(near - highest)
        total = jnp.sum(weights, axis=1, keepdims=True)
        mixed = dot(weights.astype(BF16), v_ref[start : start + ROWS, :])
        if step:
            weights = jnp.exp(far - highest)
            total = total + jnp.sum(weights, axis=1, keepdims=True)
            mixed = mixed + dot(weights.astype(BF16), v_ref[:start, :])
        out_ref[start : start + ROWS, :] = (mixed / total).astype(BF16)
    for block in range(LEN // BLK):
        mixed_ref[block * BLK : (block + 1) * BLK, :] = out_ref[rows_of(ctx_pos[block]), :]


def attend_back_kernel(
    arrive_pos, ctx_pos, q_ref, k_ref, v_ref, grad_ref, weight_ref,
    to_arrive_ref, near_ref, far_ref, sums_ref, do_ref, dk_ref, dv_ref, all_ref
):
    for block in range(LEN // BLK):
        do_ref[rows_of(ctx_pos[block]), :] = grad_ref[block * BLK : (block + 1) * BLK, :]
    keep = lax.broadcasted_iota(jnp.int32, (ROWS, ROWS), 0) <= lax.broadcasted_iota(
        jnp.int32, (ROWS, ROWS), 1
    )
    for step in range(LEN // ROWS - 1, -1, -1):
        start = step * ROWS
        end = start + ROWS
        queries = q_ref[start:end, :]
        grads = do_ref[start:end, :]
        near_keys, near_values = k_ref[start:end, :], v_ref[start:end, :]
        near = jnp.where(keep, dot(near_keys, queries, ((1,), (1,))), NEGATIVE)
        highest = jnp.max(near, axis=0, keepdims=True)
        if step:
            far_keys, far_values = k_ref[:start, :], v_ref[:start, :]
            far = dot(far_keys, queries, ((1,), (1,)))
            highest = jnp.maximum(highest, jnp.max(far, axis=0, keepdims=True))
        near = jnp.exp(near - highest)
        total = jnp.sum(near, axis=0, keepdims=True)
        if step:
            far = jnp.exp(far - highest)
            total = total + jnp.sum(far, axis=0, keepdims=True)
        inverse = 1.0 / total
        near = near * inverse
        near_grad = dot(near_values, grads, ((1,), (1,)))
        inner = jnp.sum(near * near_grad, axis=0, keepdims=True)
        if step:
            far = far * inverse
            far_grad = dot(far_values, grads, ((1,), (1,)))
            inner = inner + jnp.sum(far * far_grad, axis=0, keepdims=True)
        near_scores = (near * (near_grad - inner)).astype(BF16)
        near_dk = dot(near_scores, queries)
        near_dv = dot(near.astype(BF16), grads)
        query_grad = dot(near_scores, near_keys, ((0,), (0,)))
        if step == LEN // ROWS - 1:
            dk_ref[start:end, :] = near_dk
            dv_ref[start:end, :] = near_dv
        else:
            dk_ref[start:end, :] += near_dk
            dv_ref[start:end, :] += near_dv
        if step:
            far_scores = (far * (far_grad - inner)).astype(BF16)
            far_dk = dot(far_scores, queries)
            far_dv = dot(far.astype(BF16), grads)
            query_grad = query_grad + dot(far_scores, far_keys, ((0,), (0,)))
            if step == LEN // ROWS - 1:
                dk_ref[:start, :] = far_dk
                dv_ref[:start, :] = far_dv
            else:
                dk_ref[:start, :] += far_dk
                dv_ref[:start, :] += far_dv
        all_ref[start:end, :] = jnp.concatenate(
            [query_grad * 0.125, dk_ref[start:end, :], dv_ref[start:end, :]], axis=1
        ).astype(BF16)
    for block in range(LEN // BLK):
        to_arrive_ref[block * BLK : (block + 1) * BLK, : 3 * HD] = all_ref[rows_of(arrive_pos[block]), :]
    to_arrive_ref[:, 3 * HD :] = jnp.zeros((LEN, HD), BF16)
    sums_ref[...] = jnp.sum(all_ref[...].astype(F32), axis=0, keepdims=True)
    for step in range(LEN // ROWS):
        rows = slice(step * ROWS, (step + 1) * ROWS)
        part = dot(to_arrive_ref[rows, : 3 * HD], weight_ref[...], ((1,), (1,))).astype(BF16)
        if step * ROWS < LEN // 2:
            near_ref[rows, :] = part
        else:
            far_ref[step * ROWS - LEN // 2 : (step + 1) * ROWS - LEN // 2, :] = part


SMEM = pl.BlockSpec(memory_space=pltpu.SMEM)
WHOLE = pl.BlockSpec()
VMEM_BYTES = 48 * 2**20


def attend(arrive_pos, ctx_pos, own, other, weight, shift, norm=None):
    head = jax.ShapeDtypeStruct((LEN, HD), BF16)
    fresh = norm is not None
    outs = (head,) * 4
    extra = ()
    if fresh:
        outs = outs + (jax.ShapeDtypeStruct((LEN // 2, D), BF16),) * 2
        extra = tuple(norm)
    return pl.pallas_call(
        functools.partial(attend_kernel, fresh),
        out_shape=outs,
        in_specs=[SMEM, SMEM] + [WHOLE] * (4 + len(extra)),
        out_specs=(WHOLE,) * len(outs),
        scratch_shapes=[pltpu.VMEM((LEN, HD), BF16)],
        compiler_params=pltpu.CompilerParams(vmem_limit_bytes=VMEM_BYTES),
        cost_estimate=pl.CostEstimate(flops=2 * 10**9, bytes_accessed=5 * 10**6, transcendentals=2 * 10**6),
    )(arrive_pos, ctx_pos, own, other, weight, shift, *extra)


def attend_back(arrive_pos, ctx_pos, queries, keys, values, grads, weight):
    return pl.pallas_call(
        attend_back_kernel,
        out_shape=(
            jax.ShapeDtypeStruct((LEN, 4 * HD), BF16),
            jax.ShapeDtypeStruct((LEN // 2, D), BF16),
            jax.ShapeDtypeStruct((LEN // 2, D), BF16),
            jax.ShapeDtypeStruct((1, 3 * HD), F32),
        ),
        in_specs=[SMEM, SMEM] + [WHOLE] * 5,
        out_specs=(WHOLE,) * 4,
        scratch_shapes=[
            pltpu.VMEM((LEN, HD), BF16),
            pltpu.VMEM((LEN, HD), F32),
            pltpu.VMEM((LEN, HD), F32),
            pltpu.VMEM((LEN, 3 * HD), BF16),
        ],
        compiler_params=pltpu.CompilerParams(vmem_limit_bytes=VMEM_BYTES),
        cost_estimate=pl.CostEstimate(flops=4 * 10**9, bytes_accessed=5 * 10**6, transcendentals=2 * 10**6),
    )(arrive_pos, ctx_pos, queries, keys, values, grads, weight)


UPS, DOWNS, OUTS, FIRST = 0, 48, 96, 192
HEADS, SMALL, SECOND = 0, 32, 48
BOTH_ROWS = ((0,), (0,))


def first_grads_kernel(second_ref, hidden_ref, active_ref, down_ref, mixed_ref, attended_ref, out_ref):
    ups = dot(second_ref[...], hidden_ref[...], BOTH_ROWS).astype(BF16)
    for owner in range(S):
        for part in range(2):
            first = owner * 96 + part * 48
            out_ref[owner, UPS:DOWNS, part * 384 : (part + 1) * 384] = ups[first : first + 48, :]
    downs = dot(active_ref[...], down_ref[...], BOTH_ROWS).astype(BF16)
    for owner in range(S):
        out_ref[owner, DOWNS:OUTS, :] = downs[owner * 48 : (owner + 1) * 48, :]
    outs = dot(mixed_ref[...], attended_ref[...], BOTH_ROWS).astype(BF16)
    for owner in range(S):
        out_ref[owner, OUTS:FIRST, :] = outs[owner * 96 : (owner + 1) * 96, :]


def first_grads(*parts):
    return pl.pallas_call(
        first_grads_kernel,
        out_shape=jax.ShapeDtypeStruct((S, FIRST, D), BF16),
        in_specs=[WHOLE] * len(parts),
        out_specs=WHOLE,
        compiler_params=pltpu.CompilerParams(vmem_limit_bytes=VMEM_BYTES),
        cost_estimate=pl.CostEstimate(flops=2 * 10**9, bytes_accessed=9 * 10**6, transcendentals=0),
    )(*parts)


def second_grads_kernel(head, own_ref, other_ref, arrive_ref, sums_ref, hidden_sum_ref, *rest):
    vector_refs, out_ref = rest[:-1], rest[-1]
    half = LEN // 2
    heads = dot(own_ref[...], arrive_ref[:half, :], BOTH_ROWS) + dot(other_ref[...], arrive_ref[half:, :], BOTH_ROWS)
    heads = heads.astype(BF16)
    here = lax.broadcasted_iota(jnp.int32, (1, D), 1) // HD == head[0]
    queries = jnp.where(here, jnp.concatenate([sums_ref[:, :HD]] * H, axis=1), 0.0)
    values = jnp.where(here, jnp.concatenate([sums_ref[:, 2 * HD : 3 * HD]] * H, axis=1), 0.0)
    vectors = [ref[...] for ref in vector_refs]
    vectors = vectors[:2] + [queries, values] + vectors[2:]
    row = lax.broadcasted_iota(jnp.int32, (SECOND - SMALL, D), 0)
    for owner in range(S):
        for part in range(3):
            first = owner * 96 + part * 32
            out_ref[owner, HEADS:SMALL, part * 256 : (part + 1) * 256] = heads[first : first + 32, :]
        mine = jnp.concatenate([member[:, owner * 96 : (owner + 1) * 96] for member in vectors], axis=1)
        hidden = jnp.concatenate(
            [hidden_sum_ref[:, owner * 48 : (owner + 1) * 48], jnp.zeros((1, D - 48), F32)], axis=1
        )
        block = jnp.where(row == 0, mine, jnp.where(row == 1, hidden, 0.0))
        out_ref[owner, SMALL:SECOND, :] = block.astype(BF16)


def second_grads(head, *parts):
    return pl.pallas_call(
        second_grads_kernel,
        out_shape=jax.ShapeDtypeStruct((S, SECOND, D), BF16),
        in_specs=[SMEM] + [WHOLE] * len(parts),
        out_specs=WHOLE,
        compiler_params=pltpu.CompilerParams(vmem_limit_bytes=VMEM_BYTES),
        cost_estimate=pl.CostEstimate(flops=10**9, bytes_accessed=5 * 10**6, transcendentals=0),
    )(head, *parts)


def unpack_kernel(slots, first_ref, second_ref, last_ref, qkv_ref, out_ref, up_ref, down_ref, up_shift_ref, *vector_refs):
    layers = (
        ((first_ref, 0, lambda place: place), (second_ref, 0, lambda place: slots[place])),
        ((last_ref, 0, lambda place: place), (last_ref, OUTS, lambda place: place)),
    )
    for layer, (wide, late) in enumerate(layers):
        def rows(source, place, start, end):
            ref, base, slot = source
            return ref[slot(place), base + start : base + end, :].astype(F32)

        for head in range(H):
            block = rows(late, head, HEADS, SMALL)
            for part in range(3):
                for kind in range(3):
                    lane = part * 256 + kind * HD
                    column = kind * D + head * HD
                    qkv_ref[layer, part * 32 : (part + 1) * 32, column : column + HD] = block[:, lane : lane + HD]
        for rank in range(8):
            block = rows(wide, rank, UPS, DOWNS) + rows(wide, rank + 8, UPS, DOWNS)
            for part in range(2):
                for owner in range(S):
                    lane = part * 384 + owner * 48
                    column = owner * 384 + rank * 48
                    up_ref[layer, part * 48 : (part + 1) * 48, column : column + 48] = block[:, lane : lane + 48]
            block = rows(wide, rank, DOWNS, OUTS) + rows(wide, rank + 8, DOWNS, OUTS)
            down_ref[layer, rank * 48 : (rank + 1) * 48, :] = block
            small = rows(late, rank, SMALL, SECOND) + rows(late, rank + 8, SMALL, SECOND)
            up_shift_ref[layer : layer + 1, rank * 48 : (rank + 1) * 48] = small[1:2, :48]
            vectors = small[0:1, :] if rank == 0 else vectors + small[0:1, :]
        for member, ref in enumerate(vector_refs):
            ref[layer : layer + 1, :] = vectors[:, member * 96 : (member + 1) * 96]
    for place in range(C):
        small = second_ref[slots[place], SMALL:SECOND, :].astype(F32)
        for layer in range(LAYERS):
            out_ref[layer, place * 6 : (place + 1) * 6, :] = small[2 + 6 * layer : 8 + 6 * layer, :]


def unpack(slots, first, second, last):
    shapes = [(96, 3 * D), (96, D), (96, FF), (384, D), (384,)] + [(96,)] * 8
    return pl.pallas_call(
        unpack_kernel,
        out_shape=tuple(jax.ShapeDtypeStruct((LAYERS,) + shape, F32) for shape in shapes),
        in_specs=[SMEM] + [WHOLE] * 3,
        out_specs=(WHOLE,) * len(shapes),
        compiler_params=pltpu.CompilerParams(vmem_limit_bytes=VMEM_BYTES),
        cost_estimate=pl.CostEstimate(flops=10**6, bytes_accessed=14 * 10**6, transcendentals=0),
    )(slots, first, second, last)


def join_cores(core, own, other, axis):
    return jnp.where(
        core == 0, jnp.concatenate([own, other], axis=axis), jnp.concatenate([other, own], axis=axis)
    )


def forward_layer(flowing, head_weight, layer_rows, split, small, places, gathered=None, carried=None):
    arrive_pos, ctx_pos = places
    head_shift, vectors, up_shift = small
    gain_one, bias_one, unused, unused, out_shift, gain_two, bias_two, down_shift = vectors
    if gathered is not None:
        mixed_head, queries, keys, values, own, other = attend(
            arrive_pos, ctx_pos, *gathered, head_weight, head_shift, (gain_one, bias_one)
        )
    else:
        normed = layer_norm(flowing, gain_one, bias_one).astype(BF16)
        normed, layer_rows = lax.optimization_barrier((normed, layer_rows))
        own, other = (part.reshape(LEN // 2, D) for part in gather_ctx(normed))
        mixed_head, queries, keys, values = attend(arrive_pos, ctx_pos, own, other, head_weight, head_shift)
    out_full, up_part, down_part = split(layer_rows)
    mixed = exchange(mixed_head.reshape(C, TOK, HD), "ctx")[:H]
    mixed = mixed.transpose(1, 0, 2).reshape(TOK, D)
    middle = flowing + dot(mixed, out_full) + out_shift
    second = layer_norm(middle, gain_two, bias_two).astype(BF16)
    if carried is not None:
        both = gather_x(jnp.concatenate([second, carried], axis=0))
        second_all = both[:, :TOK].reshape(8 * TOK, D)
        carried = both[:, TOK:].reshape(8 * TOK, D)
    else:
        second_all = gather_x(second).reshape(8 * TOK, D)
    hidden = dot(second_all, up_part) + up_shift
    activated = jax.nn.gelu(hidden, approximate=True).astype(BF16)
    partial = dot(activated, down_part).reshape(8, TOK, D)
    output = middle + scatter_x(partial) + down_shift
    saved = (flowing, own, other, queries, keys, values, mixed, middle, second_all, hidden, activated)
    return output, saved, carried, (head_weight, out_full, up_part, down_part)


def backward_layer(grad_out, down_all, saved, params, small, places, head, last):
    arrive_pos, ctx_pos = places
    head_weight, out_full, up_part, down_part = params
    unused, vectors, unused = small
    gain_one, bias_one, unused, unused, unused, gain_two, bias_two, unused = vectors
    flowing, own, other, queries, keys, values, mixed, middle, second_all, hidden, activated = saved
    down_in = grad_out.astype(BF16)
    down_shift_grad = jnp.sum(down_in.astype(F32), axis=0, keepdims=True)
    if down_all is None:
        down_all = gather_x(down_in).reshape(8 * TOK, D)
    activated_grad = dot(down_all, down_part, ((1,), (1,)))
    unused, gelu_back = jax.vjp(lambda inner: jax.nn.gelu(inner, approximate=True), hidden)
    hidden_grad = gelu_back(activated_grad)[0].astype(BF16)
    second_grad = scatter_x(dot(hidden_grad, up_part, ((1,), (1,))).reshape(8, TOK, D))
    up_shift_grad = jnp.sum(hidden_grad.astype(F32), axis=0, keepdims=True)
    unused, norm_back = jax.vjp(layer_norm, middle, gain_two, bias_two)
    middle_part, gain_two_grad, bias_two_grad = norm_back(second_grad)
    middle_grad = grad_out + middle_part
    attended_in = middle_grad.astype(BF16)
    out_shift_grad = jnp.sum(attended_in.astype(F32), axis=0, keepdims=True)
    mixed_grad = dot(attended_in, out_full, ((1,), (1,))).astype(BF16)
    mixed_grad = mixed_grad.reshape(TOK, H, HD).transpose(1, 0, 2)
    mixed_grad = jnp.concatenate([mixed_grad, jnp.zeros((C - H, TOK, HD), BF16)], axis=0)
    mixed_grad = exchange(mixed_grad, "ctx").reshape(LEN, HD)
    packed = first_grads(second_all, hidden_grad, activated, down_all, mixed, attended_in)
    if last is not None:
        mixed_grad, last, packed = lax.optimization_barrier((mixed_grad, last, packed))
        owned = jnp.sum(exchange(packed, "shard").astype(F32), axis=0).astype(BF16)
    else:
        owned = lax.psum_scatter(packed.reshape(S * FIRST, D), "shard", scatter_dimension=0, tiled=True)
    to_arrive, near, far, sums = attend_back(
        arrive_pos, ctx_pos, queries, keys, values, mixed_grad, head_weight
    )
    if last is not None:
        near, far, owned = lax.optimization_barrier((near, far, owned))
    normed_grad = scatter(near.reshape(8, TOK, D), far.reshape(8, TOK, D), CHIP_GROUPS)
    unused, first_back = jax.vjp(layer_norm, flowing, gain_one, bias_one)
    flowing_part, gain_one_grad, bias_one_grad = first_back(normed_grad)
    late = second_grads(
        head,
        own,
        other,
        to_arrive,
        sums,
        up_shift_grad,
        gain_one_grad,
        bias_one_grad,
        out_shift_grad,
        gain_two_grad,
        bias_two_grad,
        down_shift_grad,
    )
    return middle_grad + flowing_part, owned, late, last


def shards(
    states,
    cotangent,
    pair_order,
    norm1_gain,
    norm1_bias,
    qkv_weight,
    query_bias,
    value_bias,
    out_weight,
    out_bias,
    norm2_gain,
    norm2_bias,
    up_weight,
    up_bias,
    down_weight,
    down_bias,
):
    place = lax.axis_index("ctx")
    core = place % 2
    rank = place % 8
    head = jnp.minimum(place, H - 1)
    pairs = jnp.stack([pair_order, 2 * C - 1 - pair_order], axis=1)
    ctx_pos = pairs.reshape(-1)
    by_core = pairs.reshape(8, 2, 2).transpose(1, 0, 2)
    arrive_pos = jnp.where(core == 0, by_core, by_core[::-1]).reshape(-1)
    places = (arrive_pos, ctx_pos)

    states_all = tuple(part.reshape(LEN // 2, D) for part in gather_ctx(states.reshape(TOK, D)))

    unit = lax.broadcasted_iota(jnp.int32, (FF, 384), 0)
    column = lax.broadcasted_iota(jnp.int32, (FF, 384), 1)
    pick = (unit == (column // 48) * 384 + rank * 48 + column % 48).astype(BF16)
    up_piece = dot(up_weight.reshape(LAYERS * 96, FF), pick).astype(BF16).reshape(LAYERS, 96, 384)
    down_piece = lax.dynamic_slice_in_dim(down_weight, rank * 48, 48, axis=1)
    out_piece = lax.dynamic_slice_in_dim(out_weight, core * 384, 384, axis=2)

    def beside(piece):
        return jnp.concatenate([piece[:48], piece[48:]], axis=1)

    def apart(piece):
        return jnp.concatenate([piece[..., :384], piece[..., 384:]], axis=1).reshape(D, 384)

    def split(rows):
        own = apart(rows[:, :48])
        out_full = join_cores(core, own, swap_core(own), 1)
        return out_full, apart(rows[:, 48:96]), rows[:, 96:].reshape(384, D)

    layer_pieces = [
        jnp.concatenate([beside(out_piece[layer]), beside(up_piece[layer]), down_piece[layer]], axis=0)
        for layer in range(LAYERS)
    ]

    vectors = jnp.stack(
        [norm1_gain, norm1_bias, query_bias, value_bias, out_bias, norm2_gain, norm2_bias, down_bias]
    )
    head_piece = lax.dynamic_slice_in_dim(qkv_weight.reshape(LAYERS, 96, 3, D), head * HD, HD, axis=3)
    head_piece = jnp.where(place < H, head_piece, jnp.zeros_like(head_piece))
    packed = jnp.concatenate(
        [
            head_piece.reshape(LAYERS * 96 * 3 * HD // D, D),
            vectors.reshape(2, D),
            up_bias.reshape(1, D),
            jnp.zeros((13, D), BF16),
            layer_pieces[0],
        ],
        axis=0,
    )
    gathered = spread_to(packed, S, "shard")
    layer_rows = [gathered[:, 64:], lax.all_gather(layer_pieces[1], "shard", axis=0)]
    head_weights = gathered[:, :48].reshape(S, LAYERS, 96, 3 * HD)
    vectors = gathered[:, 48:50].reshape(S, 8, LAYERS, 96).transpose(2, 1, 0, 3).reshape(LAYERS, 8, D)
    vectors = vectors.astype(F32)
    up_shifts = gathered[:, 50].reshape(S, LAYERS, 8, 48)
    up_shifts = lax.dynamic_index_in_dim(up_shifts, rank, 2, False).transpose(1, 0, 2).reshape(LAYERS, 1, 384)
    up_shifts = up_shifts.astype(F32)
    head_shifts = jnp.concatenate(
        [
            lax.dynamic_slice_in_dim(vectors[:, 2], head * HD, HD, axis=1),
            jnp.zeros((LAYERS, HD), F32),
            lax.dynamic_slice_in_dim(vectors[:, 3], head * HD, HD, axis=1),
        ],
        axis=1,
    ).reshape(LAYERS, 1, 3 * HD)

    flowing = states.reshape(TOK, D).astype(F32)
    saved_all = []
    smalls = []
    all_params = []
    for layer in range(LAYERS):
        small = (
            head_shifts[layer],
            [vectors[layer, member : member + 1] for member in range(8)],
            up_shifts[layer],
        )
        smalls.append(small)
        flowing, saved, carried, params = forward_layer(
            flowing,
            head_weights[:, layer].reshape(D, 3 * HD),
            layer_rows[layer],
            split,
            small,
            places,
            gathered=states_all if layer == 0 else None,
            carried=cotangent.reshape(TOK, D) if layer == LAYERS - 1 else None,
        )
        saved_all.append(saved)
        all_params.append(params)
    result = flowing.astype(BF16).reshape(states.shape)
    grad_flow = cotangent.reshape(TOK, D).astype(F32)
    held = jnp.where(place < H, place, -1).reshape(1)
    grad_flow, first_last, late, unused = backward_layer(
        grad_flow, carried, saved_all[1], all_params[1], smalls[1], places, held, None
    )
    grad_flow, late = lax.optimization_barrier((grad_flow, late))
    late_last = lax.psum_scatter(late.reshape(S * SECOND, D), "shard", scatter_dimension=0, tiled=True)
    grad_flow, first, late, last = backward_layer(
        grad_flow, None, saved_all[0], all_params[0], smalls[0], places, held, (first_last, late_last)
    )
    first_last, late_last = last
    every_last = lax.all_gather(jnp.concatenate([first_last[:OUTS], late_last], axis=0), "ctx", axis=0)
    every_first = lax.all_gather(first[:OUTS], "ctx", axis=0)
    outs = jnp.stack([first[OUTS:], first_last[OUTS:]]).reshape(LAYERS, C, 6, D)
    outs = outs.transpose(1, 0, 2, 3).reshape(C, 12, D)
    outs = exchange(jnp.pad(outs, ((0, 0), (0, 4), (0, 0))), "ctx").astype(F32)
    outs = jnp.sum(outs, axis=0)[:12].astype(BF16)
    late = jnp.sum(exchange(late, "shard").astype(F32), axis=0).astype(BF16)
    late = jnp.concatenate([late[: SMALL + 2], outs, jnp.zeros((2, D), BF16)], axis=0)
    every_late = jnp.concatenate(gather_ctx(late), axis=0)
    places_of = jnp.arange(C, dtype=jnp.int32)
    slots = places_of // 2 + 8 * (places_of % 2 != core).astype(jnp.int32)
    qkv, outs, ups, downs, hiddens, *vectors = unpack(slots, every_first, every_late, every_last)
    return (
        result,
        grad_flow.astype(BF16).reshape(states.shape),
        vectors[0],
        vectors[1],
        qkv,
        vectors[2],
        vectors[3],
        outs,
        vectors[4],
        vectors[5],
        vectors[6],
        ups,
        hiddens,
        downs,
        vectors[7],
    )


def solution(mesh):
    matrix = P(None, "shard", None)
    vector = P(None, "shard")
    rows = P("shard", "ctx", None)
    params = (
        vector,
        vector,
        matrix,
        vector,
        vector,
        matrix,
        vector,
        vector,
        vector,
        matrix,
        vector,
        matrix,
        vector,
    )
    return jax.shard_map(
        shards,
        mesh=mesh,
        in_specs=(rows, rows, P()) + params,
        out_specs=(rows, rows) + params,
        check_vma=False,
    )
```

```python
import functools

import jax
import jax.numpy as jnp
from jax import lax
from jax.experimental import pallas as pl
from jax.experimental.pallas import tpu as pltpu
from jax.sharding import PartitionSpec as P

H = 12
HD = 64
D = 768
FF = 3072
LAYERS = 2
S = 8
C = 16
TOK = 128
LEN = TOK * C
BLK = TOK // 2
ROWS = 256
EPSILON = 1e-05
NEGATIVE = -1e30
F32 = jnp.float32
BF16 = jnp.bfloat16

CHIP_GROUPS = [[2 * q + core for q in range(8)] for core in range(2)]
X_GROUPS = [[8 * y + 2 * x + core for x in range(4)] for y in range(2) for core in range(2)]
SWAP = [(i, i ^ 1) for i in range(C)]


def layer_norm(states, gain, shift):
    average = jnp.mean(states, axis=-1, keepdims=True)
    centered = states - average
    spread = jnp.mean(centered * centered, axis=-1, keepdims=True)
    return centered * lax.rsqrt(spread + EPSILON) * gain + shift


def exchange(parts, axis, groups=None):
    return lax.all_to_all(parts, axis, 0, 0, tiled=True, axis_index_groups=groups)


def spread_to(part, count, axis, groups=None):
    return exchange(jnp.broadcast_to(part[None], (count,) + part.shape), axis, groups)


def swap_core(part):
    return lax.ppermute(part, "ctx", SWAP)


def gather_ctx(part):
    own = spread_to(part, 8, "ctx", CHIP_GROUPS)
    return own, swap_core(own)


def gather_x(part):
    own = spread_to(part, 4, "ctx", X_GROUPS)
    return jnp.concatenate([own, swap_core(own)], axis=0)


def scatter(near, far, groups):
    mine = near.astype(F32) + swap_core(far.astype(BF16)).astype(F32)
    parts = exchange(mine.astype(BF16), "ctx", groups)
    return jnp.sum(parts.astype(F32), axis=0)


def scatter_x(partial):
    return scatter(partial[:4], partial[4:], X_GROUPS)


def dot(left, right, dims=((1,), (0,))):
    return lax.dot_general(left, right, (dims, ((), ())), preferred_element_type=F32)


def rows_of(block):
    return pl.ds(pl.multiple_of(block * BLK, BLK), BLK)


def attend_kernel(fresh, arrive_pos, ctx_pos, own_ref, other_ref, weight_ref, shift_ref, *rest):
    if fresh:
        gain_ref, bias_ref, mixed_ref, q_ref, k_ref, v_ref, own_normed, other_normed, out_ref = rest
    else:
        mixed_ref, q_ref, k_ref, v_ref, out_ref = rest
    for step in range(LEN // ROWS):
        half = LEN // ROWS // 2
        source = own_ref if step < half else other_ref
        rows = slice(step % half * ROWS, (step % half + 1) * ROWS)
        normed = source[rows, :]
        if fresh:
            normed = layer_norm(normed.astype(F32), gain_ref[...], bias_ref[...]).astype(BF16)
            (own_normed if step < half else other_normed)[rows, :] = normed
        piece = dot(normed, weight_ref[...]) + shift_ref[...]
        for part in range(ROWS // BLK):
            rows = rows_of(arrive_pos[step * (ROWS // BLK) + part])
            block = piece[part * BLK : (part + 1) * BLK, :]
            q_ref[rows, :] = (block[:, :HD].astype(BF16).astype(F32) * 0.125).astype(BF16)
            k_ref[rows, :] = block[:, HD : 2 * HD].astype(BF16)
            v_ref[rows, :] = block[:, 2 * HD :].astype(BF16)
    keep = lax.broadcasted_iota(jnp.int32, (ROWS, ROWS), 0) >= lax.broadcasted_iota(
        jnp.int32, (ROWS, ROWS), 1
    )
    for step in range(LEN // ROWS):
        start = step * ROWS
        queries = q_ref[start : start + ROWS, :]
        near = dot(queries, k_ref[start : start + ROWS, :], ((1,), (1,)))
        near = jnp.where(keep, near, NEGATIVE)
        highest = jnp.max(near, axis=1, keepdims=True)
        if step:
            far = dot(queries, k_ref[:start, :], ((1,), (1,)))
            highest = jnp.maximum(highest, jnp.max(far, axis=1, keepdims=True))
        weights = jnp.exp(near - highest)
        total = jnp.sum(weights, axis=1, keepdims=True)
        mixed = dot(weights.astype(BF16), v_ref[start : start + ROWS, :])
        if step:
            weights = jnp.exp(far - highest)
            total = total + jnp.sum(weights, axis=1, keepdims=True)
            mixed = mixed + dot(weights.astype(BF16), v_ref[:start, :])
        out_ref[start : start + ROWS, :] = (mixed / total).astype(BF16)
    for block in range(LEN // BLK):
        mixed_ref[block * BLK : (block + 1) * BLK, :] = out_ref[rows_of(ctx_pos[block]), :]


def attend_back_kernel(
    arrive_pos, ctx_pos, q_ref, k_ref, v_ref, grad_ref, weight_ref,
    to_arrive_ref, near_ref, far_ref, sums_ref, do_ref, dk_ref, dv_ref, all_ref
):
    for block in range(LEN // BLK):
        do_ref[rows_of(ctx_pos[block]), :] = grad_ref[block * BLK : (block + 1) * BLK, :]
    keep = lax.broadcasted_iota(jnp.int32, (ROWS, ROWS), 0) <= lax.broadcasted_iota(
        jnp.int32, (ROWS, ROWS), 1
    )
    for step in range(LEN // ROWS - 1, -1, -1):
        start = step * ROWS
        end = start + ROWS
        queries = q_ref[start:end, :]
        grads = do_ref[start:end, :]
        near_keys, near_values = k_ref[start:end, :], v_ref[start:end, :]
        near = jnp.where(keep, dot(near_keys, queries, ((1,), (1,))), NEGATIVE)
        highest = jnp.max(near, axis=0, keepdims=True)
        if step:
            far_keys, far_values = k_ref[:start, :], v_ref[:start, :]
            far = dot(far_keys, queries, ((1,), (1,)))
            highest = jnp.maximum(highest, jnp.max(far, axis=0, keepdims=True))
        near = jnp.exp(near - highest)
        total = jnp.sum(near, axis=0, keepdims=True)
        if step:
            far = jnp.exp(far - highest)
            total = total + jnp.sum(far, axis=0, keepdims=True)
        inverse = 1.0 / total
        near = near * inverse
        near_grad = dot(near_values, grads, ((1,), (1,)))
        inner = jnp.sum(near * near_grad, axis=0, keepdims=True)
        if step:
            far = far * inverse
            far_grad = dot(far_values, grads, ((1,), (1,)))
            inner = inner + jnp.sum(far * far_grad, axis=0, keepdims=True)
        near_scores = (near * (near_grad - inner)).astype(BF16)
        near_dk = dot(near_scores, queries)
        near_dv = dot(near.astype(BF16), grads)
        query_grad = dot(near_scores, near_keys, ((0,), (0,)))
        if step == LEN // ROWS - 1:
            dk_ref[start:end, :] = near_dk
            dv_ref[start:end, :] = near_dv
        else:
            dk_ref[start:end, :] += near_dk
            dv_ref[start:end, :] += near_dv
        if step:
            far_scores = (far * (far_grad - inner)).astype(BF16)
            far_dk = dot(far_scores, queries)
            far_dv = dot(far.astype(BF16), grads)
            query_grad = query_grad + dot(far_scores, far_keys, ((0,), (0,)))
            if step == LEN // ROWS - 1:
                dk_ref[:start, :] = far_dk
                dv_ref[:start, :] = far_dv
            else:
                dk_ref[:start, :] += far_dk
                dv_ref[:start, :] += far_dv
        all_ref[start:end, :] = jnp.concatenate(
            [query_grad * 0.125, dk_ref[start:end, :], dv_ref[start:end, :]], axis=1
        ).astype(BF16)
    for block in range(LEN // BLK):
        to_arrive_ref[block * BLK : (block + 1) * BLK, : 3 * HD] = all_ref[rows_of(arrive_pos[block]), :]
    to_arrive_ref[:, 3 * HD :] = jnp.zeros((LEN, HD), BF16)
    sums_ref[...] = jnp.sum(all_ref[...].astype(F32), axis=0, keepdims=True)
    for step in range(LEN // ROWS):
        rows = slice(step * ROWS, (step + 1) * ROWS)
        part = dot(to_arrive_ref[rows, : 3 * HD], weight_ref[...], ((1,), (1,))).astype(BF16)
        if step * ROWS < LEN // 2:
            near_ref[rows, :] = part
        else:
            far_ref[step * ROWS - LEN // 2 : (step + 1) * ROWS - LEN // 2, :] = part


SMEM = pl.BlockSpec(memory_space=pltpu.SMEM)
WHOLE = pl.BlockSpec()
VMEM_BYTES = 60 * 2**20


def attend(arrive_pos, ctx_pos, own, other, weight, shift, norm=None):
    head = jax.ShapeDtypeStruct((LEN, HD), BF16)
    fresh = norm is not None
    outs = (head,) * 4
    extra = ()
    if fresh:
        outs = outs + (jax.ShapeDtypeStruct((LEN // 2, D), BF16),) * 2
        extra = tuple(norm)
    return pl.pallas_call(
        functools.partial(attend_kernel, fresh),
        out_shape=outs,
        in_specs=[SMEM, SMEM] + [WHOLE] * (4 + len(extra)),
        out_specs=(WHOLE,) * len(outs),
        scratch_shapes=[pltpu.VMEM((LEN, HD), BF16)],
        compiler_params=pltpu.CompilerParams(vmem_limit_bytes=VMEM_BYTES),
        cost_estimate=pl.CostEstimate(flops=2 * 10**9, bytes_accessed=5 * 10**6, transcendentals=2 * 10**6),
    )(arrive_pos, ctx_pos, own, other, weight, shift, *extra)


def attend_back(arrive_pos, ctx_pos, queries, keys, values, grads, weight):
    return pl.pallas_call(
        attend_back_kernel,
        out_shape=(
            jax.ShapeDtypeStruct((LEN, 4 * HD), BF16),
            jax.ShapeDtypeStruct((LEN // 2, D), BF16),
            jax.ShapeDtypeStruct((LEN // 2, D), BF16),
            jax.ShapeDtypeStruct((1, 3 * HD), F32),
        ),
        in_specs=[SMEM, SMEM] + [WHOLE] * 5,
        out_specs=(WHOLE,) * 4,
        scratch_shapes=[
            pltpu.VMEM((LEN, HD), BF16),
            pltpu.VMEM((LEN, HD), F32),
            pltpu.VMEM((LEN, HD), F32),
            pltpu.VMEM((LEN, 3 * HD), BF16),
        ],
        compiler_params=pltpu.CompilerParams(vmem_limit_bytes=VMEM_BYTES),
        cost_estimate=pl.CostEstimate(flops=4 * 10**9, bytes_accessed=5 * 10**6, transcendentals=2 * 10**6),
    )(arrive_pos, ctx_pos, queries, keys, values, grads, weight)


UPS, DOWNS, OUTS, FIRST = 0, 48, 96, 192
HEADS, SMALL, SECOND = 0, 64, 80
BOTH_ROWS = ((0,), (0,))


def first_grads_kernel(second_ref, hidden_ref, active_ref, down_ref, mixed_ref, attended_ref, out_ref):
    ups = dot(second_ref[...], hidden_ref[...], BOTH_ROWS).astype(BF16)
    for owner in range(S):
        for part in range(2):
            first = owner * 96 + part * 48
            out_ref[owner, UPS:DOWNS, part * 384 : (part + 1) * 384] = ups[first : first + 48, :]
    downs = dot(active_ref[...], down_ref[...], BOTH_ROWS).astype(BF16)
    for owner in range(S):
        out_ref[owner, DOWNS:OUTS, :] = downs[owner * 48 : (owner + 1) * 48, :]
    outs = dot(mixed_ref[...], attended_ref[...], BOTH_ROWS).astype(BF16)
    for owner in range(S):
        out_ref[owner, OUTS:FIRST, :] = outs[owner * 96 : (owner + 1) * 96, :]


def first_grads(*parts):
    return pl.pallas_call(
        first_grads_kernel,
        out_shape=jax.ShapeDtypeStruct((S, FIRST, D), BF16),
        in_specs=[WHOLE] * len(parts),
        out_specs=WHOLE,
        compiler_params=pltpu.CompilerParams(vmem_limit_bytes=VMEM_BYTES),
        cost_estimate=pl.CostEstimate(flops=2 * 10**9, bytes_accessed=9 * 10**6, transcendentals=0),
    )(*parts)


def second_grads_kernel(layer, head, own_ref, other_ref, arrive_ref, sums_ref, hidden_sum_ref, *rest):
    vector_refs, prior_refs, out_ref = rest[:6], rest[6:-1], rest[-1]
    half = LEN // 2
    heads = dot(own_ref[...], arrive_ref[:half, :], BOTH_ROWS) + dot(other_ref[...], arrive_ref[half:, :], BOTH_ROWS)
    heads = heads.astype(BF16)
    here = lax.broadcasted_iota(jnp.int32, (1, D), 1) // HD == head[0]
    queries = jnp.where(here, jnp.concatenate([sums_ref[:, :HD]] * H, axis=1), 0.0)
    values = jnp.where(here, jnp.concatenate([sums_ref[:, 2 * HD : 3 * HD]] * H, axis=1), 0.0)
    vectors = [ref[...] for ref in vector_refs]
    vectors = vectors[:2] + [queries, values] + vectors[2:]
    row = lax.broadcasted_iota(jnp.int32, (SECOND - SMALL, D), 0)
    for owner in range(S):
        for part in range(3):
            first = owner * 96 + part * 32
            out_ref[owner, layer * 32 : (layer + 1) * 32, part * 256 : (part + 1) * 256] = heads[first : first + 32, :]
        mine = jnp.concatenate([member[:, owner * 96 : (owner + 1) * 96] for member in vectors], axis=1)
        hidden = jnp.concatenate(
            [hidden_sum_ref[:, owner * 48 : (owner + 1) * 48], jnp.zeros((1, D - 48), F32)], axis=1
        )
        block = jnp.where(row == 2 * layer, mine, jnp.where(row == 2 * layer + 1, hidden, 0.0))
        for prior_ref in prior_refs:
            block = block + prior_ref[owner, SMALL:SECOND, :].astype(F32)
            out_ref[owner, 32:SMALL, :] = prior_ref[owner, 32:SMALL, :]
        if not prior_refs:
            out_ref[owner, :32, :] = jnp.zeros((32, D), BF16)
        out_ref[owner, SMALL:SECOND, :] = block.astype(BF16)


def second_grads(layer, head, *parts):
    return pl.pallas_call(
        functools.partial(second_grads_kernel, layer),
        out_shape=jax.ShapeDtypeStruct((S, SECOND, D), BF16),
        in_specs=[SMEM] + [WHOLE] * len(parts),
        out_specs=WHOLE,
        compiler_params=pltpu.CompilerParams(vmem_limit_bytes=VMEM_BYTES),
        cost_estimate=pl.CostEstimate(flops=10**9, bytes_accessed=5 * 10**6, transcendentals=0),
    )(head, *parts)


def unpack_kernel(slots, late_ref, first_ref, last_ref, qkv_ref, out_ref, up_ref, down_ref, up_shift_ref, *vector_refs):
    for layer, wide_ref in enumerate((first_ref, last_ref)):
        def late(place, start, end):
            return late_ref[slots[place], start:end, :].astype(F32)

        def wide(place, start, end, wide_ref=wide_ref):
            return wide_ref[place, start:end, :].astype(F32)

        for head in range(H):
            block = late(head, layer * 32, (layer + 1) * 32)
            for part in range(3):
                for kind in range(3):
                    lane = part * 256 + kind * HD
                    column = kind * D + head * HD
                    qkv_ref[layer, part * 32 : (part + 1) * 32, column : column + HD] = block[:, lane : lane + HD]
        for rank in range(8):
            block = wide(rank, UPS, DOWNS) + wide(rank + 8, UPS, DOWNS)
            for part in range(2):
                for owner in range(S):
                    lane = part * 384 + owner * 48
                    column = owner * 384 + rank * 48
                    up_ref[layer, part * 48 : (part + 1) * 48, column : column + 48] = block[:, lane : lane + 48]
            block = wide(rank, DOWNS, OUTS) + wide(rank + 8, DOWNS, OUTS)
            down_ref[layer, rank * 48 : (rank + 1) * 48, :] = block
            small = late(rank, SMALL, SECOND) + late(rank + 8, SMALL, SECOND)
            up_shift_ref[layer : layer + 1, rank * 48 : (rank + 1) * 48] = small[2 * layer + 1 : 2 * layer + 2, :48]
            mine = small[2 * layer : 2 * layer + 1, :]
            vectors = mine if rank == 0 else vectors + mine
        for member, ref in enumerate(vector_refs):
            ref[layer : layer + 1, :] = vectors[:, member * 96 : (member + 1) * 96]
    for place in range(C):
        small = late_ref[slots[place], SMALL:SECOND, :].astype(F32)
        for layer in range(LAYERS):
            out_ref[layer, place * 6 : (place + 1) * 6, :] = small[4 + 6 * layer : 10 + 6 * layer, :]


def unpack(slots, late, first, last):
    shapes = [(96, 3 * D), (96, D), (96, FF), (384, D), (384,)] + [(96,)] * 8
    return pl.pallas_call(
        unpack_kernel,
        out_shape=tuple(jax.ShapeDtypeStruct((LAYERS,) + shape, F32) for shape in shapes),
        in_specs=[SMEM] + [WHOLE] * 3,
        out_specs=(WHOLE,) * len(shapes),
        compiler_params=pltpu.CompilerParams(vmem_limit_bytes=VMEM_BYTES),
        cost_estimate=pl.CostEstimate(flops=10**6, bytes_accessed=14 * 10**6, transcendentals=0),
    )(slots, late, first, last)


def join_cores(core, own, other, axis):
    return jnp.where(
        core == 0, jnp.concatenate([own, other], axis=axis), jnp.concatenate([other, own], axis=axis)
    )


def forward_layer(flowing, head_weight, layer_rows, split, small, places, gathered=None, carried=None):
    arrive_pos, ctx_pos = places
    head_shift, vectors, up_shift = small
    gain_one, bias_one, unused, unused, out_shift, gain_two, bias_two, down_shift = vectors
    if gathered is not None:
        mixed_head, queries, keys, values, own, other = attend(
            arrive_pos, ctx_pos, *gathered, head_weight, head_shift, (gain_one, bias_one)
        )
        mixed_head, layer_rows = lax.optimization_barrier((mixed_head, layer_rows))
    else:
        normed = layer_norm(flowing, gain_one, bias_one).astype(BF16)
        normed, layer_rows = lax.optimization_barrier((normed, layer_rows))
        own, other = (part.reshape(LEN // 2, D) for part in gather_ctx(normed))
        mixed_head, queries, keys, values = attend(arrive_pos, ctx_pos, own, other, head_weight, head_shift)
    out_full, up_part, down_part = split(layer_rows)
    mixed = exchange(mixed_head.reshape(C, TOK, HD), "ctx")[:H]
    mixed = mixed.transpose(1, 0, 2).reshape(TOK, D)
    middle = flowing + dot(mixed, out_full) + out_shift
    second = layer_norm(middle, gain_two, bias_two).astype(BF16)
    if carried is not None:
        both = gather_x(jnp.concatenate([second, carried], axis=0))
        second_all = both[:, :TOK].reshape(8 * TOK, D)
        carried = both[:, TOK:].reshape(8 * TOK, D)
    else:
        second_all = gather_x(second).reshape(8 * TOK, D)
    hidden = dot(second_all, up_part) + up_shift
    activated = jax.nn.gelu(hidden, approximate=True).astype(BF16)
    partial = dot(activated, down_part).reshape(8, TOK, D)
    output = middle + scatter_x(partial) + down_shift
    saved = (flowing, own, other, queries, keys, values, mixed, middle, second_all, hidden, activated)
    return output, saved, carried, (head_weight, out_full, up_part, down_part)


def backward_layer(grad_out, down_all, saved, params, small, places, head, layer, prior, spread):
    arrive_pos, ctx_pos = places
    head_weight, out_full, up_part, down_part = params
    unused, vectors, unused = small
    gain_one, bias_one, unused, unused, unused, gain_two, bias_two, unused = vectors
    flowing, own, other, queries, keys, values, mixed, middle, second_all, hidden, activated = saved
    down_in = grad_out.astype(BF16)
    down_shift_grad = jnp.sum(down_in.astype(F32), axis=0, keepdims=True)
    if down_all is None:
        down_all = gather_x(down_in).reshape(8 * TOK, D)
    activated_grad = dot(down_all, down_part, ((1,), (1,)))
    unused, gelu_back = jax.vjp(lambda inner: jax.nn.gelu(inner, approximate=True), hidden)
    hidden_grad = gelu_back(activated_grad)[0].astype(BF16)
    second_part = dot(hidden_grad, up_part, ((1,), (1,))).reshape(8, TOK, D)
    second_grad = scatter_x(second_part)
    up_shift_grad = jnp.sum(hidden_grad.astype(F32), axis=0, keepdims=True)
    unused, norm_back = jax.vjp(layer_norm, middle, gain_two, bias_two)
    middle_part, gain_two_grad, bias_two_grad = norm_back(second_grad)
    middle_grad = grad_out + middle_part
    attended_in = middle_grad.astype(BF16)
    out_shift_grad = jnp.sum(attended_in.astype(F32), axis=0, keepdims=True)
    mixed_grad = dot(attended_in, out_full, ((1,), (1,))).astype(BF16)
    mixed_grad = mixed_grad.reshape(TOK, H, HD).transpose(1, 0, 2)
    mixed_grad = jnp.concatenate([mixed_grad, jnp.zeros((C - H, TOK, HD), BF16)], axis=0)
    mixed_grad = exchange(mixed_grad, "ctx").reshape(LEN, HD)
    packed = first_grads(second_all, hidden_grad, activated, down_all, mixed, attended_in)
    mixed_grad, packed = lax.optimization_barrier((mixed_grad, packed))
    owned = jnp.sum(exchange(packed, "shard").astype(F32), axis=0).astype(BF16)
    to_arrive, near, far, sums = attend_back(
        arrive_pos, ctx_pos, queries, keys, values, mixed_grad, head_weight
    )
    near, far, owned, spread = lax.optimization_barrier((near, far, owned, spread))
    normed_grad = scatter(near.reshape(8, TOK, D), far.reshape(8, TOK, D), CHIP_GROUPS)
    unused, first_back = jax.vjp(layer_norm, flowing, gain_one, bias_one)
    flowing_part, gain_one_grad, bias_one_grad = first_back(normed_grad)
    late = second_grads(
        layer,
        head,
        own,
        other,
        to_arrive,
        sums,
        up_shift_grad,
        gain_one_grad,
        bias_one_grad,
        out_shift_grad,
        gain_two_grad,
        bias_two_grad,
        down_shift_grad,
        *prior,
    )
    return middle_grad + flowing_part, owned, late, spread


def shards(
    states,
    cotangent,
    pair_order,
    norm1_gain,
    norm1_bias,
    qkv_weight,
    query_bias,
    value_bias,
    out_weight,
    out_bias,
    norm2_gain,
    norm2_bias,
    up_weight,
    up_bias,
    down_weight,
    down_bias,
):
    place = lax.axis_index("ctx")
    core = place % 2
    rank = place % 8
    head = jnp.minimum(place, H - 1)
    pairs = jnp.stack([pair_order, 2 * C - 1 - pair_order], axis=1)
    ctx_pos = pairs.reshape(-1)
    by_core = pairs.reshape(8, 2, 2).transpose(1, 0, 2)
    arrive_pos = jnp.where(core == 0, by_core, by_core[::-1]).reshape(-1)
    places = (arrive_pos, ctx_pos)

    states_all = tuple(part.reshape(LEN // 2, D) for part in gather_ctx(states.reshape(TOK, D)))

    unit = lax.broadcasted_iota(jnp.int32, (FF, 384), 0)
    column = lax.broadcasted_iota(jnp.int32, (FF, 384), 1)
    pick = (unit == (column // 48) * 384 + rank * 48 + column % 48).astype(BF16)
    up_piece = dot(up_weight.reshape(LAYERS * 96, FF), pick).astype(BF16).reshape(LAYERS, 96, 384)
    down_piece = lax.dynamic_slice_in_dim(down_weight, rank * 48, 48, axis=1)
    out_piece = lax.dynamic_slice_in_dim(out_weight, core * 384, 384, axis=2)

    def beside(piece):
        return jnp.concatenate([piece[:48], piece[48:]], axis=1)

    def apart(piece):
        return jnp.concatenate([piece[..., :384], piece[..., 384:]], axis=1).reshape(D, 384)

    def split(rows):
        own = apart(rows[:, :48])
        out_full = join_cores(core, own, swap_core(own), 1)
        return out_full, apart(rows[:, 48:96]), rows[:, 96:].reshape(384, D)

    layer_pieces = [
        jnp.concatenate([beside(out_piece[layer]), beside(up_piece[layer]), down_piece[layer]], axis=0)
        for layer in range(LAYERS)
    ]

    vectors = jnp.stack(
        [norm1_gain, norm1_bias, query_bias, value_bias, out_bias, norm2_gain, norm2_bias, down_bias]
    )
    head_piece = lax.dynamic_slice_in_dim(qkv_weight.reshape(LAYERS, 96, 3, D), head * HD, HD, axis=3)
    head_piece = jnp.where(place < H, head_piece, jnp.zeros_like(head_piece))
    packed = jnp.concatenate(
        [
            head_piece.reshape(LAYERS * 96 * 3 * HD // D, D),
            vectors.reshape(2, D),
            up_bias.reshape(1, D),
            jnp.zeros((13, D), BF16),
        ],
        axis=0,
    )
    gathered = spread_to(packed, S, "shard")
    gathered, first_piece = lax.optimization_barrier((gathered, layer_pieces[0]))
    layer_rows = [spread_to(first_piece, S, "shard"), lax.all_gather(layer_pieces[1], "shard", axis=0)]
    head_weights = gathered[:, :48].reshape(S, LAYERS, 96, 3 * HD)
    vectors = gathered[:, 48:50].reshape(S, 8, LAYERS, 96).transpose(2, 1, 0, 3).reshape(LAYERS, 8, D)
    vectors = vectors.astype(F32)
    up_shifts = gathered[:, 50].reshape(S, LAYERS, 8, 48)
    up_shifts = lax.dynamic_index_in_dim(up_shifts, rank, 2, False).transpose(1, 0, 2).reshape(LAYERS, 1, 384)
    up_shifts = up_shifts.astype(F32)
    head_shifts = jnp.concatenate(
        [
            lax.dynamic_slice_in_dim(vectors[:, 2], head * HD, HD, axis=1),
            jnp.zeros((LAYERS, HD), F32),
            lax.dynamic_slice_in_dim(vectors[:, 3], head * HD, HD, axis=1),
        ],
        axis=1,
    ).reshape(LAYERS, 1, 3 * HD)

    flowing = states.reshape(TOK, D).astype(F32)
    saved_all = []
    smalls = []
    all_params = []
    for layer in range(LAYERS):
        small = (
            head_shifts[layer],
            [vectors[layer, member : member + 1] for member in range(8)],
            up_shifts[layer],
        )
        smalls.append(small)
        flowing, saved, carried, params = forward_layer(
            flowing,
            head_weights[:, layer].reshape(D, 3 * HD),
            layer_rows[layer],
            split,
            small,
            places,
            gathered=states_all if layer == 0 else None,
            carried=cotangent.reshape(TOK, D) if layer == LAYERS - 1 else None,
        )
        saved_all.append(saved)
        all_params.append(params)
    result = flowing.astype(BF16).reshape(states.shape)
    grad_flow = cotangent.reshape(TOK, D).astype(F32)
    held = jnp.where(place < H, place, -1).reshape(1)
    grad_flow, owned_last, late, unused = backward_layer(
        grad_flow, carried, saved_all[1], all_params[1], smalls[1], places, held, 1, (), ()
    )
    grad_flow, late = lax.optimization_barrier((grad_flow, late))
    every_last = lax.all_gather(owned_last[:OUTS], "ctx", axis=0)
    grad_flow, owned, late, every_last = backward_layer(
        grad_flow, None, saved_all[0], all_params[0], smalls[0], places, held, 0, (late,), every_last
    )
    every_first = lax.all_gather(owned[:OUTS], "ctx", axis=0)
    outs = jnp.stack([owned[OUTS:], owned_last[OUTS:]]).reshape(LAYERS, C, 6, D)
    outs = outs.transpose(1, 0, 2, 3).reshape(C, 12, D)
    outs = exchange(jnp.pad(outs, ((0, 0), (0, 4), (0, 0))), "ctx").astype(F32)
    outs = jnp.sum(outs, axis=0)[:12].astype(BF16)
    late = jnp.sum(exchange(late, "shard").astype(F32), axis=0).astype(BF16)
    late = jnp.concatenate([late[: SMALL + 4], outs], axis=0)
    every_late = jnp.concatenate(gather_ctx(late), axis=0)
    places_of = jnp.arange(C, dtype=jnp.int32)
    slots = places_of // 2 + 8 * (places_of % 2 != core).astype(jnp.int32)
    qkv, outs, ups, downs, hiddens, *vectors = unpack(slots, every_late, every_first, every_last)
    return (
        result,
        grad_flow.astype(BF16).reshape(states.shape),
        vectors[0],
        vectors[1],
        qkv,
        vectors[2],
        vectors[3],
        outs,
        vectors[4],
        vectors[5],
        vectors[6],
        ups,
        hiddens,
        downs,
        vectors[7],
    )


def solution(mesh):
    matrix = P(None, "shard", None)
    vector = P(None, "shard")
    rows = P("shard", "ctx", None)
    params = (
        vector,
        vector,
        matrix,
        vector,
        vector,
        matrix,
        vector,
        vector,
        vector,
        matrix,
        vector,
        matrix,
        vector,
    )
    return jax.shard_map(
        shards,
        mesh=mesh,
        in_specs=(rows, rows, P()) + params,
        out_specs=(rows, rows) + params,
        check_vma=False,
    )
```

```python
import functools
import math

import jax
import jax.numpy as jnp
from jax import lax
from jax.experimental import pallas as pl
from jax.experimental.pallas import tpu as pltpu
from jax.sharding import PartitionSpec as P

H = 12
HD = 64
D = 768
FF = 3072
LAYERS = 2
S = 8
C = 16
TOK = 128
LEN = TOK * C
BLK = TOK // 2
ROWS = 256
EPSILON = 1e-05
NEGATIVE = -1e30
F32 = jnp.float32
BF16 = jnp.bfloat16

CHIP_GROUPS = [[2 * q + core for q in range(8)] for core in range(2)]
X_GROUPS = [[8 * y + 2 * x + core for x in range(4)] for y in range(2) for core in range(2)]
SWAP = [(i, i ^ 1) for i in range(C)]


def layer_norm(states, gain, shift):
    average = jnp.mean(states, axis=-1, keepdims=True)
    centered = states - average
    spread = jnp.mean(centered * centered, axis=-1, keepdims=True)
    return centered * lax.rsqrt(spread + EPSILON) * gain + shift


def exchange(parts, axis, groups=None):
    return lax.all_to_all(parts, axis, 0, 0, tiled=True, axis_index_groups=groups)


def spread_to(part, count, axis, groups=None):
    return exchange(jnp.broadcast_to(part[None], (count,) + part.shape), axis, groups)


def swap_core(part):
    return lax.ppermute(part, "ctx", SWAP)


def gather_ctx(part):
    own = spread_to(part, 8, "ctx", CHIP_GROUPS)
    return own, swap_core(own)


def gather_x(part):
    own = spread_to(part, 4, "ctx", X_GROUPS)
    return own.reshape(4 * TOK, D), swap_core(own).reshape(4 * TOK, D)


def scatter(near, far, groups):
    mine = near.astype(F32) + swap_core(far.astype(BF16)).astype(F32)
    parts = exchange(mine.astype(BF16), "ctx", groups)
    return jnp.sum(parts.astype(F32), axis=0)


def scatter_x(near, far):
    return scatter(near.reshape(4, TOK, D), far.reshape(4, TOK, D), X_GROUPS)


def dot(left, right, dims=((1,), (0,))):
    return lax.dot_general(left, right, (dims, ((), ())), preferred_element_type=F32)


def rows_of(block):
    return pl.ds(pl.multiple_of(block * BLK, BLK), BLK)


def attend_kernel(fresh, arrive_pos, ctx_pos, own_ref, other_ref, weight_ref, shift_ref, *rest):
    if fresh:
        gain_ref, bias_ref, mixed_ref, q_ref, k_ref, v_ref, own_normed, other_normed, out_ref = rest
    else:
        mixed_ref, q_ref, k_ref, v_ref, out_ref = rest
    for step in range(LEN // ROWS):
        half = LEN // ROWS // 2
        source = own_ref if step < half else other_ref
        rows = slice(step % half * ROWS, (step % half + 1) * ROWS)
        normed = source[rows, :]
        if fresh:
            normed = layer_norm(normed.astype(F32), gain_ref[...], bias_ref[...]).astype(BF16)
            (own_normed if step < half else other_normed)[rows, :] = normed
        piece = dot(normed, weight_ref[...]) + shift_ref[...]
        for part in range(ROWS // BLK):
            rows = rows_of(arrive_pos[step * (ROWS // BLK) + part])
            block = piece[part * BLK : (part + 1) * BLK, :]
            q_ref[rows, :] = (block[:, :HD].astype(BF16).astype(F32) * 0.125).astype(BF16)
            k_ref[rows, :] = block[:, HD : 2 * HD].astype(BF16)
            v_ref[rows, :] = block[:, 2 * HD :].astype(BF16)
    keep = lax.broadcasted_iota(jnp.int32, (ROWS, ROWS), 0) >= lax.broadcasted_iota(
        jnp.int32, (ROWS, ROWS), 1
    )
    for step in range(LEN // ROWS):
        start = step * ROWS
        queries = q_ref[start : start + ROWS, :]
        near = dot(queries, k_ref[start : start + ROWS, :], ((1,), (1,)))
        near = jnp.where(keep, near, NEGATIVE)
        highest = jnp.max(near, axis=1, keepdims=True)
        if step:
            far = dot(queries, k_ref[:start, :], ((1,), (1,)))
            highest = jnp.maximum(highest, jnp.max(far, axis=1, keepdims=True))
        weights = jnp.exp(near - highest)
        total = jnp.sum(weights, axis=1, keepdims=True)
        mixed = dot(weights.astype(BF16), v_ref[start : start + ROWS, :])
        if step:
            weights = jnp.exp(far - highest)
            total = total + jnp.sum(weights, axis=1, keepdims=True)
            mixed = mixed + dot(weights.astype(BF16), v_ref[:start, :])
        out_ref[start : start + ROWS, :] = (mixed / total).astype(BF16)
    for block in range(LEN // BLK):
        mixed_ref[block * BLK : (block + 1) * BLK, :] = out_ref[rows_of(ctx_pos[block]), :]


def attend_back_kernel(
    arrive_pos, ctx_pos, q_ref, k_ref, v_ref, grad_ref, weight_ref,
    to_arrive_ref, near_ref, far_ref, sums_ref, do_ref, dk_ref, dv_ref, all_ref
):
    for block in range(LEN // BLK):
        do_ref[rows_of(ctx_pos[block]), :] = grad_ref[block * BLK : (block + 1) * BLK, :]
    keep = lax.broadcasted_iota(jnp.int32, (ROWS, ROWS), 0) <= lax.broadcasted_iota(
        jnp.int32, (ROWS, ROWS), 1
    )
    for step in range(LEN // ROWS - 1, -1, -1):
        start = step * ROWS
        end = start + ROWS
        queries = q_ref[start:end, :]
        grads = do_ref[start:end, :]
        near_keys, near_values = k_ref[start:end, :], v_ref[start:end, :]
        near = jnp.where(keep, dot(near_keys, queries, ((1,), (1,))), NEGATIVE)
        highest = jnp.max(near, axis=0, keepdims=True)
        if step:
            far_keys, far_values = k_ref[:start, :], v_ref[:start, :]
            far = dot(far_keys, queries, ((1,), (1,)))
            highest = jnp.maximum(highest, jnp.max(far, axis=0, keepdims=True))
        near = jnp.exp(near - highest)
        total = jnp.sum(near, axis=0, keepdims=True)
        if step:
            far = jnp.exp(far - highest)
            total = total + jnp.sum(far, axis=0, keepdims=True)
        inverse = 1.0 / total
        near = near * inverse
        near_grad = dot(near_values, grads, ((1,), (1,)))
        inner = jnp.sum(near * near_grad, axis=0, keepdims=True)
        if step:
            far = far * inverse
            far_grad = dot(far_values, grads, ((1,), (1,)))
            inner = inner + jnp.sum(far * far_grad, axis=0, keepdims=True)
        near_scores = (near * (near_grad - inner)).astype(BF16)
        near_dk = dot(near_scores, queries)
        near_dv = dot(near.astype(BF16), grads)
        query_grad = dot(near_scores, near_keys, ((0,), (0,)))
        if step == LEN // ROWS - 1:
            dk_ref[start:end, :] = near_dk
            dv_ref[start:end, :] = near_dv
        else:
            dk_ref[start:end, :] += near_dk
            dv_ref[start:end, :] += near_dv
        if step:
            far_scores = (far * (far_grad - inner)).astype(BF16)
            far_dk = dot(far_scores, queries)
            far_dv = dot(far.astype(BF16), grads)
            query_grad = query_grad + dot(far_scores, far_keys, ((0,), (0,)))
            if step == LEN // ROWS - 1:
                dk_ref[:start, :] = far_dk
                dv_ref[:start, :] = far_dv
            else:
                dk_ref[:start, :] += far_dk
                dv_ref[:start, :] += far_dv
        all_ref[start:end, :] = jnp.concatenate(
            [query_grad * 0.125, dk_ref[start:end, :], dv_ref[start:end, :]], axis=1
        ).astype(BF16)
    for block in range(LEN // BLK):
        to_arrive_ref[block * BLK : (block + 1) * BLK, : 3 * HD] = all_ref[rows_of(arrive_pos[block]), :]
    to_arrive_ref[:, 3 * HD :] = jnp.zeros((LEN, HD), BF16)
    sums_ref[...] = jnp.sum(all_ref[...].astype(F32), axis=0, keepdims=True)
    for step in range(LEN // ROWS):
        rows = slice(step * ROWS, (step + 1) * ROWS)
        part = dot(to_arrive_ref[rows, : 3 * HD], weight_ref[...], ((1,), (1,))).astype(BF16)
        if step * ROWS < LEN // 2:
            near_ref[rows, :] = part
        else:
            far_ref[step * ROWS - LEN // 2 : (step + 1) * ROWS - LEN // 2, :] = part


SMEM = pl.BlockSpec(memory_space=pltpu.SMEM)
WHOLE = pl.BlockSpec()
VMEM_BYTES = 60 * 2**20


def attend(arrive_pos, ctx_pos, own, other, weight, shift, norm=None):
    head = jax.ShapeDtypeStruct((LEN, HD), BF16)
    fresh = norm is not None
    outs = (head,) * 4
    extra = ()
    if fresh:
        outs = outs + (jax.ShapeDtypeStruct((LEN // 2, D), BF16),) * 2
        extra = tuple(norm)
    return pl.pallas_call(
        functools.partial(attend_kernel, fresh),
        out_shape=outs,
        in_specs=[SMEM, SMEM] + [WHOLE] * (4 + len(extra)),
        out_specs=(WHOLE,) * len(outs),
        scratch_shapes=[pltpu.VMEM((LEN, HD), BF16)],
        compiler_params=pltpu.CompilerParams(vmem_limit_bytes=VMEM_BYTES),
        cost_estimate=pl.CostEstimate(flops=2 * 10**9, bytes_accessed=5 * 10**6, transcendentals=2 * 10**6),
    )(arrive_pos, ctx_pos, own, other, weight, shift, *extra)


def attend_back(arrive_pos, ctx_pos, queries, keys, values, grads, weight):
    return pl.pallas_call(
        attend_back_kernel,
        out_shape=(
            jax.ShapeDtypeStruct((LEN, 4 * HD), BF16),
            jax.ShapeDtypeStruct((LEN // 2, D), BF16),
            jax.ShapeDtypeStruct((LEN // 2, D), BF16),
            jax.ShapeDtypeStruct((1, 3 * HD), F32),
        ),
        in_specs=[SMEM, SMEM] + [WHOLE] * 5,
        out_specs=(WHOLE,) * 4,
        scratch_shapes=[
            pltpu.VMEM((LEN, HD), BF16),
            pltpu.VMEM((LEN, HD), F32),
            pltpu.VMEM((LEN, HD), F32),
            pltpu.VMEM((LEN, 3 * HD), BF16),
        ],
        compiler_params=pltpu.CompilerParams(vmem_limit_bytes=VMEM_BYTES),
        cost_estimate=pl.CostEstimate(flops=4 * 10**9, bytes_accessed=5 * 10**6, transcendentals=2 * 10**6),
    )(arrive_pos, ctx_pos, queries, keys, values, grads, weight)


GELU_SCALE = math.sqrt(2.0 / math.pi)
GELU_CUBE = 0.044715


def load_feed(rows_ref, up_ref, down_ref):
    for owner in range(S):
        for part in range(2):
            first = owner * 96 + part * 48
            up_ref[first : first + 48, :] = rows_ref[owner, 48:96, part * 384 : (part + 1) * 384]
        down_ref[owner * 48 : (owner + 1) * 48, :] = rows_ref[owner, 96:144, :]


def feed_kernel(own_ref, other_ref, rows_ref, shift_ref, hidden_ref, active_ref, near_ref, far_ref, up_ref, down_ref):
    load_feed(rows_ref, up_ref, down_ref)
    for side, (source, target) in enumerate(((own_ref, near_ref), (other_ref, far_ref))):
        for step in range(4 * TOK // ROWS):
            rows = slice(step * ROWS, (step + 1) * ROWS)
            saved = slice(side * 4 * TOK + step * ROWS, side * 4 * TOK + (step + 1) * ROWS)
            hidden = dot(source[rows, :], up_ref[...]) + shift_ref[...]
            hidden_ref[saved, :] = hidden
            inner = GELU_SCALE * (hidden + GELU_CUBE * hidden * hidden * hidden)
            active = (hidden * (0.5 * (1.0 + jnp.tanh(inner)))).astype(BF16)
            active_ref[saved, :] = active
            target[rows, :] = dot(active, down_ref[...]).astype(BF16)


def feed_back_kernel(own_ref, other_ref, rows_ref, hidden_ref, grad_ref, near_ref, far_ref, sums_ref, up_ref, down_ref):
    load_feed(rows_ref, up_ref, down_ref)
    sums = jnp.zeros((1, 384), F32)
    for side, (source, target) in enumerate(((own_ref, near_ref), (other_ref, far_ref))):
        for step in range(4 * TOK // ROWS):
            rows = slice(step * ROWS, (step + 1) * ROWS)
            saved = slice(side * 4 * TOK + step * ROWS, side * 4 * TOK + (step + 1) * ROWS)
            active_grad = dot(source[rows, :], down_ref[...], ((1,), (1,)))
            hidden = hidden_ref[saved, :]
            square = hidden * hidden
            bend = jnp.tanh(GELU_SCALE * (hidden + GELU_CUBE * square * hidden))
            slope = GELU_SCALE * (1.0 + 3.0 * GELU_CUBE * square)
            slope = 0.5 * (1.0 + bend) + 0.5 * hidden * (1.0 - bend * bend) * slope
            grad = (active_grad * slope).astype(BF16)
            grad_ref[saved, :] = grad
            sums = sums + jnp.sum(grad.astype(F32), axis=0, keepdims=True)
            target[rows, :] = dot(grad, up_ref[...], ((1,), (1,))).astype(BF16)
    sums_ref[...] = sums


def feed(own, other, rows, shift):
    half = jax.ShapeDtypeStruct((4 * TOK, D), BF16)
    return pl.pallas_call(
        feed_kernel,
        out_shape=(
            jax.ShapeDtypeStruct((8 * TOK, 384), F32),
            jax.ShapeDtypeStruct((8 * TOK, 384), BF16),
            half,
            half,
        ),
        in_specs=[WHOLE] * 4,
        out_specs=(WHOLE,) * 4,
        scratch_shapes=[pltpu.VMEM((D, 384), BF16), pltpu.VMEM((384, D), BF16)],
        compiler_params=pltpu.CompilerParams(vmem_limit_bytes=VMEM_BYTES),
        cost_estimate=pl.CostEstimate(flops=12 * 10**8, bytes_accessed=7 * 10**6, transcendentals=4 * 10**5),
    )(own, other, rows, shift)


def feed_back(own, other, rows, hidden):
    half = jax.ShapeDtypeStruct((4 * TOK, D), BF16)
    return pl.pallas_call(
        feed_back_kernel,
        out_shape=(
            jax.ShapeDtypeStruct((8 * TOK, 384), BF16),
            half,
            half,
            jax.ShapeDtypeStruct((1, 384), F32),
        ),
        in_specs=[WHOLE] * 4,
        out_specs=(WHOLE,) * 4,
        scratch_shapes=[pltpu.VMEM((D, 384), BF16), pltpu.VMEM((384, D), BF16)],
        compiler_params=pltpu.CompilerParams(vmem_limit_bytes=VMEM_BYTES),
        cost_estimate=pl.CostEstimate(flops=12 * 10**8, bytes_accessed=7 * 10**6, transcendentals=4 * 10**5),
    )(own, other, rows, hidden)


UPS, DOWNS, OUTS, FIRST = 0, 48, 96, 192
HEADS, SMALL, SECOND = 0, 64, 80
BOTH_ROWS = ((0,), (0,))


def first_grads_kernel(
    own_ref, other_ref, hidden_ref, active_ref, own_down_ref, other_down_ref, mixed_ref, attended_ref, out_ref
):
    half = 4 * TOK
    ups = dot(own_ref[...], hidden_ref[:half, :], BOTH_ROWS) + dot(other_ref[...], hidden_ref[half:, :], BOTH_ROWS)
    ups = ups.astype(BF16)
    for owner in range(S):
        for part in range(2):
            first = owner * 96 + part * 48
            out_ref[owner, UPS:DOWNS, part * 384 : (part + 1) * 384] = ups[first : first + 48, :]
    downs = dot(active_ref[:half, :], own_down_ref[...], BOTH_ROWS)
    downs = (downs + dot(active_ref[half:, :], other_down_ref[...], BOTH_ROWS)).astype(BF16)
    for owner in range(S):
        out_ref[owner, DOWNS:OUTS, :] = downs[owner * 48 : (owner + 1) * 48, :]
    outs = dot(mixed_ref[...], attended_ref[...], BOTH_ROWS).astype(BF16)
    for owner in range(S):
        out_ref[owner, OUTS:FIRST, :] = outs[owner * 96 : (owner + 1) * 96, :]


def first_grads(*parts):
    return pl.pallas_call(
        first_grads_kernel,
        out_shape=jax.ShapeDtypeStruct((S, FIRST, D), BF16),
        in_specs=[WHOLE] * len(parts),
        out_specs=WHOLE,
        compiler_params=pltpu.CompilerParams(vmem_limit_bytes=VMEM_BYTES),
        cost_estimate=pl.CostEstimate(flops=2 * 10**9, bytes_accessed=9 * 10**6, transcendentals=0),
    )(*parts)


def second_grads_kernel(layer, head, own_ref, other_ref, arrive_ref, sums_ref, hidden_sum_ref, *rest):
    vector_refs, prior_refs, out_ref = rest[:6], rest[6:-1], rest[-1]
    half = LEN // 2
    heads = dot(own_ref[...], arrive_ref[:half, :], BOTH_ROWS) + dot(other_ref[...], arrive_ref[half:, :], BOTH_ROWS)
    heads = heads.astype(BF16)
    here = lax.broadcasted_iota(jnp.int32, (1, D), 1) // HD == head[0]
    queries = jnp.where(here, jnp.concatenate([sums_ref[:, :HD]] * H, axis=1), 0.0)
    values = jnp.where(here, jnp.concatenate([sums_ref[:, 2 * HD : 3 * HD]] * H, axis=1), 0.0)
    vectors = [ref[...] for ref in vector_refs]
    vectors = vectors[:2] + [queries, values] + vectors[2:]
    row = lax.broadcasted_iota(jnp.int32, (SECOND - SMALL, D), 0)
    for owner in range(S):
        for part in range(3):
            first = owner * 96 + part * 32
            out_ref[owner, layer * 32 : (layer + 1) * 32, part * 256 : (part + 1) * 256] = heads[first : first + 32, :]
        mine = jnp.concatenate([member[:, owner * 96 : (owner + 1) * 96] for member in vectors], axis=1)
        hidden = jnp.concatenate(
            [hidden_sum_ref[:, owner * 48 : (owner + 1) * 48], jnp.zeros((1, D - 48), F32)], axis=1
        )
        block = jnp.where(row == 2 * layer, mine, jnp.where(row == 2 * layer + 1, hidden, 0.0))
        for prior_ref in prior_refs:
            block = block + prior_ref[owner, SMALL:SECOND, :].astype(F32)
            out_ref[owner, 32:SMALL, :] = prior_ref[owner, 32:SMALL, :]
        if not prior_refs:
            out_ref[owner, :32, :] = jnp.zeros((32, D), BF16)
        out_ref[owner, SMALL:SECOND, :] = block.astype(BF16)


def second_grads(layer, head, *parts):
    return pl.pallas_call(
        functools.partial(second_grads_kernel, layer),
        out_shape=jax.ShapeDtypeStruct((S, SECOND, D), BF16),
        in_specs=[SMEM] + [WHOLE] * len(parts),
        out_specs=WHOLE,
        compiler_params=pltpu.CompilerParams(vmem_limit_bytes=VMEM_BYTES),
        cost_estimate=pl.CostEstimate(flops=10**9, bytes_accessed=5 * 10**6, transcendentals=0),
    )(head, *parts)


def unpack_kernel(slots, late_ref, first_ref, last_ref, qkv_ref, out_ref, up_ref, down_ref, up_shift_ref, *vector_refs):
    for layer, wide_ref in enumerate((first_ref, last_ref)):
        def late(place, start, end):
            return late_ref[slots[place], start:end, :].astype(F32)

        def wide(place, start, end, wide_ref=wide_ref):
            return wide_ref[place, start:end, :].astype(F32)

        for head in range(H):
            block = late(head, layer * 32, (layer + 1) * 32)
            for part in range(3):
                for kind in range(3):
                    lane = part * 256 + kind * HD
                    column = kind * D + head * HD
                    qkv_ref[layer, part * 32 : (part + 1) * 32, column : column + HD] = block[:, lane : lane + HD]
        for rank in range(8):
            block = wide(rank, UPS, DOWNS) + wide(rank + 8, UPS, DOWNS)
            for part in range(2):
                for owner in range(S):
                    lane = part * 384 + owner * 48
                    column = owner * 384 + rank * 48
                    up_ref[layer, part * 48 : (part + 1) * 48, column : column + 48] = block[:, lane : lane + 48]
            block = wide(rank, DOWNS, OUTS) + wide(rank + 8, DOWNS, OUTS)
            down_ref[layer, rank * 48 : (rank + 1) * 48, :] = block
            small = late(rank, SMALL, SECOND) + late(rank + 8, SMALL, SECOND)
            up_shift_ref[layer : layer + 1, rank * 48 : (rank + 1) * 48] = small[2 * layer + 1 : 2 * layer + 2, :48]
            mine = small[2 * layer : 2 * layer + 1, :]
            vectors = mine if rank == 0 else vectors + mine
        for member, ref in enumerate(vector_refs):
            ref[layer : layer + 1, :] = vectors[:, member * 96 : (member + 1) * 96]
    for place in range(C):
        small = late_ref[slots[place], SMALL:SECOND, :].astype(F32)
        for layer in range(LAYERS):
            out_ref[layer, place * 6 : (place + 1) * 6, :] = small[4 + 6 * layer : 10 + 6 * layer, :]


def unpack(slots, late, first, last):
    shapes = [(96, 3 * D), (96, D), (96, FF), (384, D), (384,)] + [(96,)] * 8
    return pl.pallas_call(
        unpack_kernel,
        out_shape=tuple(jax.ShapeDtypeStruct((LAYERS,) + shape, F32) for shape in shapes),
        in_specs=[SMEM] + [WHOLE] * 3,
        out_specs=(WHOLE,) * len(shapes),
        compiler_params=pltpu.CompilerParams(vmem_limit_bytes=VMEM_BYTES),
        cost_estimate=pl.CostEstimate(flops=10**6, bytes_accessed=14 * 10**6, transcendentals=0),
    )(slots, late, first, last)


def join_cores(core, own, other, axis):
    return jnp.where(
        core == 0, jnp.concatenate([own, other], axis=axis), jnp.concatenate([other, own], axis=axis)
    )


def forward_layer(flowing, head_weight, layer_rows, join_out, small, places, gathered=None, carried=None):
    arrive_pos, ctx_pos = places
    head_shift, vectors, up_shift = small
    gain_one, bias_one, unused, unused, out_shift, gain_two, bias_two, down_shift = vectors
    if gathered is not None:
        mixed_head, queries, keys, values, own, other = attend(
            arrive_pos, ctx_pos, *gathered, head_weight, head_shift, (gain_one, bias_one)
        )
        mixed_head, layer_rows = lax.optimization_barrier((mixed_head, layer_rows))
    else:
        normed = layer_norm(flowing, gain_one, bias_one).astype(BF16)
        normed, layer_rows = lax.optimization_barrier((normed, layer_rows))
        own, other = (part.reshape(LEN // 2, D) for part in gather_ctx(normed))
        own, other, carried = lax.optimization_barrier((own, other, carried))
        carried = spread_to(carried, 4, "ctx", X_GROUPS)
        mixed_head, queries, keys, values = attend(arrive_pos, ctx_pos, own, other, head_weight, head_shift)
        mixed_head, carried = lax.optimization_barrier((mixed_head, carried))
        carried = (carried.reshape(4 * TOK, D), swap_core(carried).reshape(4 * TOK, D))
    out_full = join_out(layer_rows)
    mixed = exchange(mixed_head.reshape(C, TOK, HD), "ctx")[:H]
    mixed = mixed.transpose(1, 0, 2).reshape(TOK, D)
    middle = flowing + dot(mixed, out_full) + out_shift
    second = layer_norm(middle, gain_two, bias_two).astype(BF16)
    second_all = gather_x(second)
    hidden, activated, near, far = feed(*second_all, layer_rows, up_shift)
    output = middle + scatter_x(near, far) + down_shift
    saved = (flowing, own, other, queries, keys, values, mixed, middle, second_all, hidden, activated)
    return output, saved, carried, (head_weight, out_full, layer_rows)


def backward_layer(grad_out, down_all, saved, params, small, places, head, layer, prior, spread):
    arrive_pos, ctx_pos = places
    head_weight, out_full, layer_rows = params
    unused, vectors, unused = small
    gain_one, bias_one, unused, unused, unused, gain_two, bias_two, unused = vectors
    flowing, own, other, queries, keys, values, mixed, middle, second_all, hidden, activated = saved
    down_in = grad_out.astype(BF16)
    down_shift_grad = jnp.sum(down_in.astype(F32), axis=0, keepdims=True)
    if down_all is None:
        down_all = gather_x(down_in)
    hidden_grad, near, far, up_shift_grad = feed_back(*down_all, layer_rows, hidden)
    near, far, prior = lax.optimization_barrier((near, far, prior))
    second_grad = scatter_x(near, far)
    unused, norm_back = jax.vjp(layer_norm, middle, gain_two, bias_two)
    middle_part, gain_two_grad, bias_two_grad = norm_back(second_grad)
    middle_grad = grad_out + middle_part
    attended_in = middle_grad.astype(BF16)
    out_shift_grad = jnp.sum(attended_in.astype(F32), axis=0, keepdims=True)
    mixed_grad = dot(attended_in, out_full, ((1,), (1,))).astype(BF16)
    mixed_grad = mixed_grad.reshape(TOK, H, HD).transpose(1, 0, 2)
    mixed_grad = jnp.concatenate([mixed_grad, jnp.zeros((C - H, TOK, HD), BF16)], axis=0)
    mixed_grad = exchange(mixed_grad, "ctx").reshape(LEN, HD)
    packed = first_grads(*second_all, hidden_grad, activated, *down_all, mixed, attended_in)
    mixed_grad, packed = lax.optimization_barrier((mixed_grad, packed))
    owned = jnp.sum(exchange(packed, "shard").astype(F32), axis=0).astype(BF16)
    to_arrive, near, far, sums = attend_back(
        arrive_pos, ctx_pos, queries, keys, values, mixed_grad, head_weight
    )
    near, far, owned, spread = lax.optimization_barrier((near, far, owned, spread))
    normed_grad = scatter(near.reshape(8, TOK, D), far.reshape(8, TOK, D), CHIP_GROUPS)
    unused, first_back = jax.vjp(layer_norm, flowing, gain_one, bias_one)
    flowing_part, gain_one_grad, bias_one_grad = first_back(normed_grad)
    late = second_grads(
        layer,
        head,
        own,
        other,
        to_arrive,
        sums,
        up_shift_grad,
        gain_one_grad,
        bias_one_grad,
        out_shift_grad,
        gain_two_grad,
        bias_two_grad,
        down_shift_grad,
        *prior,
    )
    return middle_grad + flowing_part, owned, late, spread


def shards(
    states,
    cotangent,
    pair_order,
    norm1_gain,
    norm1_bias,
    qkv_weight,
    query_bias,
    value_bias,
    out_weight,
    out_bias,
    norm2_gain,
    norm2_bias,
    up_weight,
    up_bias,
    down_weight,
    down_bias,
):
    place = lax.axis_index("ctx")
    core = place % 2
    rank = place % 8
    head = jnp.minimum(place, H - 1)
    pairs = jnp.stack([pair_order, 2 * C - 1 - pair_order], axis=1)
    ctx_pos = pairs.reshape(-1)
    by_core = pairs.reshape(8, 2, 2).transpose(1, 0, 2)
    arrive_pos = jnp.where(core == 0, by_core, by_core[::-1]).reshape(-1)
    places = (arrive_pos, ctx_pos)

    states_all = tuple(part.reshape(LEN // 2, D) for part in gather_ctx(states.reshape(TOK, D)))

    unit = lax.broadcasted_iota(jnp.int32, (FF, 384), 0)
    column = lax.broadcasted_iota(jnp.int32, (FF, 384), 1)
    pick = (unit == (column // 48) * 384 + rank * 48 + column % 48).astype(BF16)
    up_piece = dot(up_weight.reshape(LAYERS * 96, FF), pick).astype(BF16).reshape(LAYERS, 96, 384)
    down_piece = lax.dynamic_slice_in_dim(down_weight, rank * 48, 48, axis=1)
    out_piece = lax.dynamic_slice_in_dim(out_weight, core * 384, 384, axis=2)

    def beside(piece):
        return jnp.concatenate([piece[:48], piece[48:]], axis=1)

    def apart(piece):
        return jnp.concatenate([piece[..., :384], piece[..., 384:]], axis=1).reshape(D, 384)

    def join_out(rows):
        own = apart(rows[:, :48])
        return join_cores(core, own, swap_core(own), 1)

    layer_pieces = [
        jnp.concatenate([beside(out_piece[layer]), beside(up_piece[layer]), down_piece[layer]], axis=0)
        for layer in range(LAYERS)
    ]

    vectors = jnp.stack(
        [norm1_gain, norm1_bias, query_bias, value_bias, out_bias, norm2_gain, norm2_bias, down_bias]
    )
    head_piece = lax.dynamic_slice_in_dim(qkv_weight.reshape(LAYERS, 96, 3, D), head * HD, HD, axis=3)
    head_piece = jnp.where(place < H, head_piece, jnp.zeros_like(head_piece))
    packed = jnp.concatenate(
        [
            head_piece.reshape(LAYERS * 96 * 3 * HD // D, D),
            vectors.reshape(2, D),
            up_bias.reshape(1, D),
            jnp.zeros((13, D), BF16),
        ],
        axis=0,
    )
    gathered = spread_to(packed, S, "shard")
    gathered, first_piece = lax.optimization_barrier((gathered, layer_pieces[0]))
    layer_rows = [spread_to(first_piece, S, "shard"), lax.all_gather(layer_pieces[1], "shard", axis=0)]
    head_weights = gathered[:, :48].reshape(S, LAYERS, 96, 3 * HD)
    vectors = gathered[:, 48:50].reshape(S, 8, LAYERS, 96).transpose(2, 1, 0, 3).reshape(LAYERS, 8, D)
    vectors = vectors.astype(F32)
    up_shifts = gathered[:, 50].reshape(S, LAYERS, 8, 48)
    up_shifts = lax.dynamic_index_in_dim(up_shifts, rank, 2, False).transpose(1, 0, 2).reshape(LAYERS, 1, 384)
    up_shifts = up_shifts.astype(F32)
    head_shifts = jnp.concatenate(
        [
            lax.dynamic_slice_in_dim(vectors[:, 2], head * HD, HD, axis=1),
            jnp.zeros((LAYERS, HD), F32),
            lax.dynamic_slice_in_dim(vectors[:, 3], head * HD, HD, axis=1),
        ],
        axis=1,
    ).reshape(LAYERS, 1, 3 * HD)

    flowing = states.reshape(TOK, D).astype(F32)
    saved_all = []
    smalls = []
    all_params = []
    for layer in range(LAYERS):
        small = (
            head_shifts[layer],
            [vectors[layer, member : member + 1] for member in range(8)],
            up_shifts[layer],
        )
        smalls.append(small)
        flowing, saved, carried, params = forward_layer(
            flowing,
            head_weights[:, layer].reshape(D, 3 * HD),
            layer_rows[layer],
            join_out,
            small,
            places,
            gathered=states_all if layer == 0 else None,
            carried=cotangent.reshape(TOK, D) if layer == LAYERS - 1 else None,
        )
        saved_all.append(saved)
        all_params.append(params)
    result = flowing.astype(BF16).reshape(states.shape)
    grad_flow = cotangent.reshape(TOK, D).astype(F32)
    held = jnp.where(place < H, place, -1).reshape(1)
    grad_flow, owned_last, late, unused = backward_layer(
        grad_flow, carried, saved_all[1], all_params[1], smalls[1], places, held, 1, (), ()
    )
    every_last = lax.all_gather(owned_last[:OUTS], "ctx", axis=0)
    grad_flow, owned, late, every_last = backward_layer(
        grad_flow, None, saved_all[0], all_params[0], smalls[0], places, held, 0, (late,), every_last
    )
    every_first = lax.all_gather(owned[:OUTS], "ctx", axis=0)
    outs = jnp.stack([owned[OUTS:], owned_last[OUTS:]]).reshape(LAYERS, C, 6, D)
    outs = outs.transpose(1, 0, 2, 3).reshape(C, 12, D)
    outs = exchange(jnp.pad(outs, ((0, 0), (0, 4), (0, 0))), "ctx").astype(F32)
    outs = jnp.sum(outs, axis=0)[:12].astype(BF16)
    late = jnp.sum(exchange(late, "shard").astype(F32), axis=0).astype(BF16)
    late = jnp.concatenate([late[: SMALL + 4], outs], axis=0)
    every_late = jnp.concatenate(gather_ctx(late), axis=0)
    places_of = jnp.arange(C, dtype=jnp.int32)
    slots = places_of // 2 + 8 * (places_of % 2 != core).astype(jnp.int32)
    qkv, outs, ups, downs, hiddens, *vectors = unpack(slots, every_late, every_first, every_last)
    return (
        result,
        grad_flow.astype(BF16).reshape(states.shape),
        vectors[0],
        vectors[1],
        qkv,
        vectors[2],
        vectors[3],
        outs,
        vectors[4],
        vectors[5],
        vectors[6],
        ups,
        hiddens,
        downs,
        vectors[7],
    )


def solution(mesh):
    matrix = P(None, "shard", None)
    vector = P(None, "shard")
    rows = P("shard", "ctx", None)
    params = (
        vector,
        vector,
        matrix,
        vector,
        vector,
        matrix,
        vector,
        vector,
        vector,
        matrix,
        vector,
        matrix,
        vector,
    )
    return jax.shard_map(
        shards,
        mesh=mesh,
        in_specs=(rows, rows, P()) + params,
        out_specs=(rows, rows) + params,
        check_vma=False,
    )
```

```python
import functools
import math

import jax
import jax.numpy as jnp
from jax import lax
from jax.experimental import pallas as pl
from jax.experimental.pallas import tpu as pltpu
from jax.sharding import PartitionSpec as P

H = 12
HD = 64
D = 768
FF = 3072
LAYERS = 2
S = 8
C = 16
TOK = 128
LEN = TOK * C
BLK = TOK // 2
ROWS = 256
EPSILON = 1e-05
NEGATIVE = -1e30
F32 = jnp.float32
BF16 = jnp.bfloat16

CHIP_GROUPS = [[2 * q + core for q in range(8)] for core in range(2)]
X_GROUPS = [[8 * y + 2 * x + core for x in range(4)] for y in range(2) for core in range(2)]
SWAP = [(i, i ^ 1) for i in range(C)]


def layer_norm(states, gain, shift):
    average = jnp.mean(states, axis=-1, keepdims=True)
    centered = states - average
    spread = jnp.mean(centered * centered, axis=-1, keepdims=True)
    return centered * lax.rsqrt(spread + EPSILON) * gain + shift


def exchange(parts, axis, groups=None):
    return lax.all_to_all(parts, axis, 0, 0, tiled=True, axis_index_groups=groups)


def spread_to(part, count, axis, groups=None):
    return exchange(jnp.broadcast_to(part[None], (count,) + part.shape), axis, groups)


def swap_core(part):
    return lax.ppermute(part, "ctx", SWAP)


def gather_ctx(part):
    own = spread_to(part, 8, "ctx", CHIP_GROUPS)
    return own, swap_core(own)


def gather_x(part, beside=()):
    own = spread_to(part, 4, "ctx", X_GROUPS)
    own, beside = lax.optimization_barrier((own, beside))
    return (own.reshape(4 * TOK, D), swap_core(own).reshape(4 * TOK, D)), beside


def scatter(near, far, groups, run=None):
    mine = near.astype(F32) + swap_core(far.astype(BF16)).astype(F32)
    mine = mine.astype(BF16)
    if run is None:
        return jnp.sum(exchange(mine, "ctx", groups).astype(F32), axis=0)
    start, ready = run
    mine, start = lax.optimization_barrier((mine, start))
    parts, result = lax.optimization_barrier((exchange(mine, "ctx", groups), ready(start)))
    return jnp.sum(parts.astype(F32), axis=0), result


def scatter_x(near, far, run=None):
    return scatter(near.reshape(4, TOK, D), far.reshape(4, TOK, D), X_GROUPS, run)


def dot(left, right, dims=((1,), (0,))):
    return lax.dot_general(left, right, (dims, ((), ())), preferred_element_type=F32)


def rows_of(block):
    return pl.ds(pl.multiple_of(block * BLK, BLK), BLK)


def attend_kernel(fresh, arrive_pos, ctx_pos, own_ref, other_ref, weight_ref, shift_ref, *rest):
    if fresh:
        gain_ref, bias_ref, mixed_ref, q_ref, k_ref, v_ref, own_normed, other_normed, out_ref = rest
    else:
        mixed_ref, q_ref, k_ref, v_ref, out_ref = rest
    for step in range(LEN // ROWS):
        half = LEN // ROWS // 2
        source = own_ref if step < half else other_ref
        rows = slice(step % half * ROWS, (step % half + 1) * ROWS)
        normed = source[rows, :]
        if fresh:
            normed = layer_norm(normed.astype(F32), gain_ref[...], bias_ref[...]).astype(BF16)
            (own_normed if step < half else other_normed)[rows, :] = normed
        piece = dot(normed, weight_ref[...]) + shift_ref[...]
        for part in range(ROWS // BLK):
            rows = rows_of(arrive_pos[step * (ROWS // BLK) + part])
            block = piece[part * BLK : (part + 1) * BLK, :]
            q_ref[rows, :] = (block[:, :HD].astype(BF16).astype(F32) * 0.125).astype(BF16)
            k_ref[rows, :] = block[:, HD : 2 * HD].astype(BF16)
            v_ref[rows, :] = block[:, 2 * HD :].astype(BF16)
    keep = lax.broadcasted_iota(jnp.int32, (ROWS, ROWS), 0) >= lax.broadcasted_iota(
        jnp.int32, (ROWS, ROWS), 1
    )
    for step in range(LEN // ROWS):
        start = step * ROWS
        queries = q_ref[start : start + ROWS, :]
        near = dot(queries, k_ref[start : start + ROWS, :], ((1,), (1,)))
        near = jnp.where(keep, near, NEGATIVE)
        highest = jnp.max(near, axis=1, keepdims=True)
        if step:
            far = dot(queries, k_ref[:start, :], ((1,), (1,)))
            highest = jnp.maximum(highest, jnp.max(far, axis=1, keepdims=True))
        weights = jnp.exp(near - highest)
        total = jnp.sum(weights, axis=1, keepdims=True)
        mixed = dot(weights.astype(BF16), v_ref[start : start + ROWS, :])
        if step:
            weights = jnp.exp(far - highest)
            total = total + jnp.sum(weights, axis=1, keepdims=True)
            mixed = mixed + dot(weights.astype(BF16), v_ref[:start, :])
        out_ref[start : start + ROWS, :] = (mixed / total).astype(BF16)
    for block in range(LEN // BLK):
        mixed_ref[block * BLK : (block + 1) * BLK, :] = out_ref[rows_of(ctx_pos[block]), :]


def attend_back_kernel(
    arrive_pos, ctx_pos, q_ref, k_ref, v_ref, grad_ref, weight_ref,
    to_arrive_ref, near_ref, far_ref, sums_ref, do_ref, dk_ref, dv_ref, all_ref
):
    for block in range(LEN // BLK):
        do_ref[rows_of(ctx_pos[block]), :] = grad_ref[block * BLK : (block + 1) * BLK, :]
    keep = lax.broadcasted_iota(jnp.int32, (ROWS, ROWS), 0) <= lax.broadcasted_iota(
        jnp.int32, (ROWS, ROWS), 1
    )
    for step in range(LEN // ROWS - 1, -1, -1):
        start = step * ROWS
        end = start + ROWS
        queries = q_ref[start:end, :]
        grads = do_ref[start:end, :]
        near_keys, near_values = k_ref[start:end, :], v_ref[start:end, :]
        near = jnp.where(keep, dot(near_keys, queries, ((1,), (1,))), NEGATIVE)
        highest = jnp.max(near, axis=0, keepdims=True)
        if step:
            far_keys, far_values = k_ref[:start, :], v_ref[:start, :]
            far = dot(far_keys, queries, ((1,), (1,)))
            highest = jnp.maximum(highest, jnp.max(far, axis=0, keepdims=True))
        near = jnp.exp(near - highest)
        total = jnp.sum(near, axis=0, keepdims=True)
        if step:
            far = jnp.exp(far - highest)
            total = total + jnp.sum(far, axis=0, keepdims=True)
        inverse = 1.0 / total
        near = near * inverse
        near_grad = dot(near_values, grads, ((1,), (1,)))
        inner = jnp.sum(near * near_grad, axis=0, keepdims=True)
        if step:
            far = far * inverse
            far_grad = dot(far_values, grads, ((1,), (1,)))
            inner = inner + jnp.sum(far * far_grad, axis=0, keepdims=True)
        near_scores = (near * (near_grad - inner)).astype(BF16)
        near_dk = dot(near_scores, queries)
        near_dv = dot(near.astype(BF16), grads)
        query_grad = dot(near_scores, near_keys, ((0,), (0,)))
        if step == LEN // ROWS - 1:
            dk_ref[start:end, :] = near_dk
            dv_ref[start:end, :] = near_dv
        else:
            dk_ref[start:end, :] += near_dk
            dv_ref[start:end, :] += near_dv
        if step:
            far_scores = (far * (far_grad - inner)).astype(BF16)
            far_dk = dot(far_scores, queries)
            far_dv = dot(far.astype(BF16), grads)
            query_grad = query_grad + dot(far_scores, far_keys, ((0,), (0,)))
            if step == LEN // ROWS - 1:
                dk_ref[:start, :] = far_dk
                dv_ref[:start, :] = far_dv
            else:
                dk_ref[:start, :] += far_dk
                dv_ref[:start, :] += far_dv
        all_ref[start:end, :] = jnp.concatenate(
            [query_grad * 0.125, dk_ref[start:end, :], dv_ref[start:end, :]], axis=1
        ).astype(BF16)
    for block in range(LEN // BLK):
        to_arrive_ref[block * BLK : (block + 1) * BLK, : 3 * HD] = all_ref[rows_of(arrive_pos[block]), :]
    to_arrive_ref[:, 3 * HD :] = jnp.zeros((LEN, HD), BF16)
    sums_ref[...] = jnp.sum(all_ref[...].astype(F32), axis=0, keepdims=True)
    for step in range(LEN // ROWS):
        rows = slice(step * ROWS, (step + 1) * ROWS)
        part = dot(to_arrive_ref[rows, : 3 * HD], weight_ref[...], ((1,), (1,))).astype(BF16)
        if step * ROWS < LEN // 2:
            near_ref[rows, :] = part
        else:
            far_ref[step * ROWS - LEN // 2 : (step + 1) * ROWS - LEN // 2, :] = part


SMEM = pl.BlockSpec(memory_space=pltpu.SMEM)
WHOLE = pl.BlockSpec()
VMEM_BYTES = 60 * 2**20


def attend(arrive_pos, ctx_pos, own, other, weight, shift, norm=None):
    head = jax.ShapeDtypeStruct((LEN, HD), BF16)
    fresh = norm is not None
    outs = (head,) * 4
    extra = ()
    if fresh:
        outs = outs + (jax.ShapeDtypeStruct((LEN // 2, D), BF16),) * 2
        extra = tuple(norm)
    return pl.pallas_call(
        functools.partial(attend_kernel, fresh),
        out_shape=outs,
        in_specs=[SMEM, SMEM] + [WHOLE] * (4 + len(extra)),
        out_specs=(WHOLE,) * len(outs),
        scratch_shapes=[pltpu.VMEM((LEN, HD), BF16)],
        compiler_params=pltpu.CompilerParams(vmem_limit_bytes=VMEM_BYTES),
        cost_estimate=pl.CostEstimate(flops=2 * 10**9, bytes_accessed=5 * 10**6, transcendentals=2 * 10**6),
    )(arrive_pos, ctx_pos, own, other, weight, shift, *extra)


def attend_back(arrive_pos, ctx_pos, queries, keys, values, grads, weight):
    return pl.pallas_call(
        attend_back_kernel,
        out_shape=(
            jax.ShapeDtypeStruct((LEN, 4 * HD), BF16),
            jax.ShapeDtypeStruct((LEN // 2, D), BF16),
            jax.ShapeDtypeStruct((LEN // 2, D), BF16),
            jax.ShapeDtypeStruct((1, 3 * HD), F32),
        ),
        in_specs=[SMEM, SMEM] + [WHOLE] * 5,
        out_specs=(WHOLE,) * 4,
        scratch_shapes=[
            pltpu.VMEM((LEN, HD), BF16),
            pltpu.VMEM((LEN, HD), F32),
            pltpu.VMEM((LEN, HD), F32),
            pltpu.VMEM((LEN, 3 * HD), BF16),
        ],
        compiler_params=pltpu.CompilerParams(vmem_limit_bytes=VMEM_BYTES),
        cost_estimate=pl.CostEstimate(flops=4 * 10**9, bytes_accessed=5 * 10**6, transcendentals=2 * 10**6),
    )(arrive_pos, ctx_pos, queries, keys, values, grads, weight)


GELU_SCALE = math.sqrt(2.0 / math.pi)
GELU_CUBE = 0.044715


def load_feed(rows_ref, up_ref, down_ref):
    for owner in range(S):
        for part in range(2):
            first = owner * 96 + part * 48
            up_ref[first : first + 48, :] = rows_ref[owner, 48:96, part * 384 : (part + 1) * 384]
        down_ref[owner * 48 : (owner + 1) * 48, :] = rows_ref[owner, 96:144, :]


def feed_kernel(own_ref, other_ref, rows_ref, shift_ref, hidden_ref, active_ref, near_ref, far_ref, up_ref, down_ref):
    load_feed(rows_ref, up_ref, down_ref)
    for side, (source, target) in enumerate(((own_ref, near_ref), (other_ref, far_ref))):
        for step in range(4 * TOK // ROWS):
            rows = slice(step * ROWS, (step + 1) * ROWS)
            saved = slice(side * 4 * TOK + step * ROWS, side * 4 * TOK + (step + 1) * ROWS)
            hidden = dot(source[rows, :], up_ref[...]) + shift_ref[...]
            hidden_ref[saved, :] = hidden
            inner = GELU_SCALE * (hidden + GELU_CUBE * hidden * hidden * hidden)
            active = (hidden * (0.5 * (1.0 + jnp.tanh(inner)))).astype(BF16)
            active_ref[saved, :] = active
            target[rows, :] = dot(active, down_ref[...]).astype(BF16)


def feed_back_kernel(own_ref, other_ref, rows_ref, hidden_ref, grad_ref, near_ref, far_ref, sums_ref, up_ref, down_ref):
    load_feed(rows_ref, up_ref, down_ref)
    sums = jnp.zeros((1, 384), F32)
    for side, (source, target) in enumerate(((own_ref, near_ref), (other_ref, far_ref))):
        for step in range(4 * TOK // ROWS):
            rows = slice(step * ROWS, (step + 1) * ROWS)
            saved = slice(side * 4 * TOK + step * ROWS, side * 4 * TOK + (step + 1) * ROWS)
            active_grad = dot(source[rows, :], down_ref[...], ((1,), (1,)))
            hidden = hidden_ref[saved, :]
            square = hidden * hidden
            bend = jnp.tanh(GELU_SCALE * (hidden + GELU_CUBE * square * hidden))
            slope = GELU_SCALE * (1.0 + 3.0 * GELU_CUBE * square)
            slope = 0.5 * (1.0 + bend) + 0.5 * hidden * (1.0 - bend * bend) * slope
            grad = (active_grad * slope).astype(BF16)
            grad_ref[saved, :] = grad
            sums = sums + jnp.sum(grad.astype(F32), axis=0, keepdims=True)
            target[rows, :] = dot(grad, up_ref[...], ((1,), (1,))).astype(BF16)
    sums_ref[...] = sums


def feed(own, other, rows, shift):
    half = jax.ShapeDtypeStruct((4 * TOK, D), BF16)
    return pl.pallas_call(
        feed_kernel,
        out_shape=(
            jax.ShapeDtypeStruct((8 * TOK, 384), F32),
            jax.ShapeDtypeStruct((8 * TOK, 384), BF16),
            half,
            half,
        ),
        in_specs=[WHOLE] * 4,
        out_specs=(WHOLE,) * 4,
        scratch_shapes=[pltpu.VMEM((D, 384), BF16), pltpu.VMEM((384, D), BF16)],
        compiler_params=pltpu.CompilerParams(vmem_limit_bytes=VMEM_BYTES),
        cost_estimate=pl.CostEstimate(flops=10**6, bytes_accessed=10**5, transcendentals=0),
    )(own, other, rows, shift)


def feed_back(own, other, rows, hidden):
    half = jax.ShapeDtypeStruct((4 * TOK, D), BF16)
    return pl.pallas_call(
        feed_back_kernel,
        out_shape=(
            jax.ShapeDtypeStruct((8 * TOK, 384), BF16),
            half,
            half,
            jax.ShapeDtypeStruct((1, 384), F32),
        ),
        in_specs=[WHOLE] * 4,
        out_specs=(WHOLE,) * 4,
        scratch_shapes=[pltpu.VMEM((D, 384), BF16), pltpu.VMEM((384, D), BF16)],
        compiler_params=pltpu.CompilerParams(vmem_limit_bytes=VMEM_BYTES),
        cost_estimate=pl.CostEstimate(flops=12 * 10**8, bytes_accessed=7 * 10**6, transcendentals=4 * 10**5),
    )(own, other, rows, hidden)


UPS, DOWNS, OUTS, FIRST = 0, 48, 96, 192
HEADS, SMALL, SECOND = 0, 64, 80
BOTH_ROWS = ((0,), (0,))


def first_grads_kernel(
    own_ref, other_ref, hidden_ref, active_ref, own_down_ref, other_down_ref, mixed_ref, attended_ref, out_ref
):
    half = 4 * TOK
    ups = dot(own_ref[...], hidden_ref[:half, :], BOTH_ROWS) + dot(other_ref[...], hidden_ref[half:, :], BOTH_ROWS)
    ups = ups.astype(BF16)
    for owner in range(S):
        for part in range(2):
            first = owner * 96 + part * 48
            out_ref[owner, UPS:DOWNS, part * 384 : (part + 1) * 384] = ups[first : first + 48, :]
    downs = dot(active_ref[:half, :], own_down_ref[...], BOTH_ROWS)
    downs = (downs + dot(active_ref[half:, :], other_down_ref[...], BOTH_ROWS)).astype(BF16)
    for owner in range(S):
        out_ref[owner, DOWNS:OUTS, :] = downs[owner * 48 : (owner + 1) * 48, :]
    outs = dot(mixed_ref[...], attended_ref[...], BOTH_ROWS).astype(BF16)
    for owner in range(S):
        out_ref[owner, OUTS:FIRST, :] = outs[owner * 96 : (owner + 1) * 96, :]


def first_grads(*parts):
    return pl.pallas_call(
        first_grads_kernel,
        out_shape=jax.ShapeDtypeStruct((S, FIRST, D), BF16),
        in_specs=[WHOLE] * len(parts),
        out_specs=WHOLE,
        compiler_params=pltpu.CompilerParams(vmem_limit_bytes=VMEM_BYTES),
        cost_estimate=pl.CostEstimate(flops=2 * 10**9, bytes_accessed=9 * 10**6, transcendentals=0),
    )(*parts)


def second_grads_kernel(layer, head, own_ref, other_ref, arrive_ref, sums_ref, hidden_sum_ref, *rest):
    vector_refs, prior_refs, out_ref = rest[:6], rest[6:-1], rest[-1]
    half = LEN // 2
    heads = dot(own_ref[...], arrive_ref[:half, :], BOTH_ROWS) + dot(other_ref[...], arrive_ref[half:, :], BOTH_ROWS)
    heads = heads.astype(BF16)
    here = lax.broadcasted_iota(jnp.int32, (1, D), 1) // HD == head[0]
    queries = jnp.where(here, jnp.concatenate([sums_ref[:, :HD]] * H, axis=1), 0.0)
    values = jnp.where(here, jnp.concatenate([sums_ref[:, 2 * HD : 3 * HD]] * H, axis=1), 0.0)
    vectors = [ref[...] for ref in vector_refs]
    vectors = vectors[:2] + [queries, values] + vectors[2:]
    row = lax.broadcasted_iota(jnp.int32, (SECOND - SMALL, D), 0)
    for owner in range(S):
        for part in range(3):
            first = owner * 96 + part * 32
            out_ref[owner, layer * 32 : (layer + 1) * 32, part * 256 : (part + 1) * 256] = heads[first : first + 32, :]
        mine = jnp.concatenate([member[:, owner * 96 : (owner + 1) * 96] for member in vectors], axis=1)
        hidden = jnp.concatenate(
            [hidden_sum_ref[:, owner * 48 : (owner + 1) * 48], jnp.zeros((1, D - 48), F32)], axis=1
        )
        block = jnp.where(row == 2 * layer, mine, jnp.where(row == 2 * layer + 1, hidden, 0.0))
        for prior_ref in prior_refs:
            block = block + prior_ref[owner, SMALL:SECOND, :].astype(F32)
            out_ref[owner, 32:SMALL, :] = prior_ref[owner, 32:SMALL, :]
        if not prior_refs:
            out_ref[owner, :32, :] = jnp.zeros((32, D), BF16)
        out_ref[owner, SMALL:SECOND, :] = block.astype(BF16)


def second_grads(layer, head, *parts):
    return pl.pallas_call(
        functools.partial(second_grads_kernel, layer),
        out_shape=jax.ShapeDtypeStruct((S, SECOND, D), BF16),
        in_specs=[SMEM] + [WHOLE] * len(parts),
        out_specs=WHOLE,
        compiler_params=pltpu.CompilerParams(vmem_limit_bytes=VMEM_BYTES),
        cost_estimate=pl.CostEstimate(flops=10**9, bytes_accessed=5 * 10**6, transcendentals=0),
    )(head, *parts)


def unpack_wide_kernel(first_ref, last_ref, up_ref, down_ref):
    for layer, wide_ref in enumerate((first_ref, last_ref)):
        def wide(place, start, end, wide_ref=wide_ref):
            return wide_ref[place, start:end, :].astype(F32)

        for rank in range(8):
            block = wide(rank, UPS, DOWNS) + wide(rank + 8, UPS, DOWNS)
            for part in range(2):
                for owner in range(S):
                    lane = part * 384 + owner * 48
                    column = owner * 384 + rank * 48
                    up_ref[layer, part * 48 : (part + 1) * 48, column : column + 48] = block[:, lane : lane + 48]
            block = wide(rank, DOWNS, OUTS) + wide(rank + 8, DOWNS, OUTS)
            down_ref[layer, rank * 48 : (rank + 1) * 48, :] = block


def unpack_late_kernel(slots, late_ref, qkv_ref, out_ref, up_shift_ref, *vector_refs):
    def late(place, start, end):
        return late_ref[slots[place], start:end, :].astype(F32)

    for layer in range(LAYERS):
        for head in range(H):
            block = late(head, layer * 32, (layer + 1) * 32)
            for part in range(3):
                for kind in range(3):
                    lane = part * 256 + kind * HD
                    column = kind * D + head * HD
                    qkv_ref[layer, part * 32 : (part + 1) * 32, column : column + HD] = block[:, lane : lane + HD]
    totals = [None] * LAYERS
    for rank in range(8):
        low, high = late(rank, SMALL, SECOND), late(rank + 8, SMALL, SECOND)
        small = low + high
        for layer in range(LAYERS):
            up_shift_ref[layer : layer + 1, rank * 48 : (rank + 1) * 48] = small[2 * layer + 1 : 2 * layer + 2, :48]
            mine = small[2 * layer : 2 * layer + 1, :]
            totals[layer] = mine if rank == 0 else totals[layer] + mine
            rows = slice(4 + 6 * layer, 10 + 6 * layer)
            out_ref[layer, rank * 6 : (rank + 1) * 6, :] = low[rows, :]
            out_ref[layer, (rank + 8) * 6 : (rank + 9) * 6, :] = high[rows, :]
    for layer in range(LAYERS):
        for member, ref in enumerate(vector_refs):
            ref[layer : layer + 1, :] = totals[layer][:, member * 96 : (member + 1) * 96]


def unpack_wide(first, last):
    shapes = [(96, FF), (384, D)]
    return pl.pallas_call(
        unpack_wide_kernel,
        out_shape=tuple(jax.ShapeDtypeStruct((LAYERS,) + shape, F32) for shape in shapes),
        in_specs=[WHOLE] * 2,
        out_specs=(WHOLE,) * len(shapes),
        compiler_params=pltpu.CompilerParams(vmem_limit_bytes=VMEM_BYTES),
        cost_estimate=pl.CostEstimate(flops=10**6, bytes_accessed=10 * 10**6, transcendentals=0),
    )(first, last)


def unpack_late(slots, late):
    shapes = [(96, 3 * D), (96, D), (384,)] + [(96,)] * 8
    return pl.pallas_call(
        unpack_late_kernel,
        out_shape=tuple(jax.ShapeDtypeStruct((LAYERS,) + shape, F32) for shape in shapes),
        in_specs=[SMEM, WHOLE],
        out_specs=(WHOLE,) * len(shapes),
        compiler_params=pltpu.CompilerParams(vmem_limit_bytes=VMEM_BYTES),
        cost_estimate=pl.CostEstimate(flops=10**6, bytes_accessed=5 * 10**6, transcendentals=0),
    )(slots, late)


def join_cores(core, own, other, axis):
    return jnp.where(
        core == 0, jnp.concatenate([own, other], axis=axis), jnp.concatenate([other, own], axis=axis)
    )


def forward_layer(flowing, head_weight, layer_rows, join_out, small, places, gathered=None, carried=None):
    arrive_pos, ctx_pos = places
    head_shift, vectors, up_shift = small
    gain_one, bias_one, unused, unused, out_shift, gain_two, bias_two, down_shift = vectors
    if gathered is not None:
        mixed_head, queries, keys, values, own, other = attend(
            arrive_pos, ctx_pos, *gathered, head_weight, head_shift, (gain_one, bias_one)
        )
        mixed_head, layer_rows = lax.optimization_barrier((mixed_head, layer_rows))
    else:
        normed = layer_norm(flowing, gain_one, bias_one).astype(BF16)
        normed, layer_rows = lax.optimization_barrier((normed, layer_rows))
        own, other = (part.reshape(LEN // 2, D) for part in gather_ctx(normed))
        own, other, carried = lax.optimization_barrier((own, other, carried))
        carried = spread_to(carried, 4, "ctx", X_GROUPS)
        mixed_head, queries, keys, values = attend(arrive_pos, ctx_pos, own, other, head_weight, head_shift)
        mixed_head, carried = lax.optimization_barrier((mixed_head, carried))
        carried = (carried.reshape(4 * TOK, D), swap_core(carried).reshape(4 * TOK, D))
    out_full = join_out(layer_rows)
    mixed = exchange(mixed_head.reshape(C, TOK, HD), "ctx")[:H]
    mixed = mixed.transpose(1, 0, 2).reshape(TOK, D)
    middle = flowing + dot(mixed, out_full) + out_shift
    second = layer_norm(middle, gain_two, bias_two).astype(BF16)
    second_all, unused = gather_x(second)
    hidden, activated, near, far = feed(*second_all, layer_rows, up_shift)
    if carried is None:
        summed = scatter_x(near, far)
    else:
        run = ((carried, layer_rows, hidden), lambda start: feed_back(*start[0], start[1], start[2]))
        summed, begun = scatter_x(near, far, run)
        carried = (carried, begun)
    output = middle + summed + down_shift
    saved = (flowing, own, other, queries, keys, values, mixed, middle, second_all, hidden, activated)
    return output, saved, carried, (head_weight, out_full, layer_rows)


def backward_layer(grad_out, begun, saved, params, small, places, head, layer, prior, spread):
    arrive_pos, ctx_pos = places
    head_weight, out_full, layer_rows = params
    unused, vectors, unused = small
    gain_one, bias_one, unused, unused, unused, gain_two, bias_two, unused = vectors
    flowing, own, other, queries, keys, values, mixed, middle, second_all, hidden, activated = saved
    down_in = grad_out.astype(BF16)
    down_shift_grad = jnp.sum(down_in.astype(F32), axis=0, keepdims=True)
    if begun is None:
        down_all, prior = gather_x(down_in, prior)
        begun = feed_back(*down_all, layer_rows, hidden)
    else:
        down_all, begun = begun
    hidden_grad, near, far, up_shift_grad = begun
    second_grad = scatter_x(near, far)
    unused, norm_back = jax.vjp(layer_norm, middle, gain_two, bias_two)
    middle_part, gain_two_grad, bias_two_grad = norm_back(second_grad)
    middle_grad = grad_out + middle_part
    attended_in = middle_grad.astype(BF16)
    out_shift_grad = jnp.sum(attended_in.astype(F32), axis=0, keepdims=True)
    mixed_grad = dot(attended_in, out_full, ((1,), (1,))).astype(BF16)
    mixed_grad = mixed_grad.reshape(TOK, H, HD).transpose(1, 0, 2)
    mixed_grad = jnp.concatenate([mixed_grad, jnp.zeros((C - H, TOK, HD), BF16)], axis=0)
    mixed_grad = exchange(mixed_grad, "ctx").reshape(LEN, HD)
    packed = first_grads(*second_all, hidden_grad, activated, *down_all, mixed, attended_in)
    mixed_grad, packed = lax.optimization_barrier((mixed_grad, packed))
    owned = jnp.sum(exchange(packed, "shard").astype(F32), axis=0).astype(BF16)
    to_arrive, near, far, sums = attend_back(
        arrive_pos, ctx_pos, queries, keys, values, mixed_grad, head_weight
    )
    near, far, owned, spread = lax.optimization_barrier((near, far, owned, spread))
    normed_grad = scatter(near.reshape(8, TOK, D), far.reshape(8, TOK, D), CHIP_GROUPS)
    unused, first_back = jax.vjp(layer_norm, flowing, gain_one, bias_one)
    flowing_part, gain_one_grad, bias_one_grad = first_back(normed_grad)
    late = second_grads(
        layer,
        head,
        own,
        other,
        to_arrive,
        sums,
        up_shift_grad,
        gain_one_grad,
        bias_one_grad,
        out_shift_grad,
        gain_two_grad,
        bias_two_grad,
        down_shift_grad,
        *prior,
    )
    return middle_grad + flowing_part, owned, late, spread


def shards(
    states,
    cotangent,
    pair_order,
    norm1_gain,
    norm1_bias,
    qkv_weight,
    query_bias,
    value_bias,
    out_weight,
    out_bias,
    norm2_gain,
    norm2_bias,
    up_weight,
    up_bias,
    down_weight,
    down_bias,
):
    place = lax.axis_index("ctx")
    core = place % 2
    rank = place % 8
    head = jnp.minimum(place, H - 1)
    pairs = jnp.stack([pair_order, 2 * C - 1 - pair_order], axis=1)
    ctx_pos = pairs.reshape(-1)
    by_core = pairs.reshape(8, 2, 2).transpose(1, 0, 2)
    arrive_pos = jnp.where(core == 0, by_core, by_core[::-1]).reshape(-1)
    places = (arrive_pos, ctx_pos)

    states_all = tuple(part.reshape(LEN // 2, D) for part in gather_ctx(states.reshape(TOK, D)))

    unit = lax.broadcasted_iota(jnp.int32, (FF, 384), 0)
    column = lax.broadcasted_iota(jnp.int32, (FF, 384), 1)
    pick = (unit == (column // 48) * 384 + rank * 48 + column % 48).astype(BF16)
    up_piece = dot(up_weight.reshape(LAYERS * 96, FF), pick).astype(BF16).reshape(LAYERS, 96, 384)
    down_piece = lax.dynamic_slice_in_dim(down_weight, rank * 48, 48, axis=1)
    out_piece = lax.dynamic_slice_in_dim(out_weight, core * 384, 384, axis=2)

    def beside(piece):
        return jnp.concatenate([piece[:48], piece[48:]], axis=1)

    def apart(piece):
        return jnp.concatenate([piece[..., :384], piece[..., 384:]], axis=1).reshape(D, 384)

    def join_out(rows):
        own = apart(rows[:, :48])
        return join_cores(core, own, swap_core(own), 1)

    layer_pieces = [
        jnp.concatenate([beside(out_piece[layer]), beside(up_piece[layer]), down_piece[layer]], axis=0)
        for layer in range(LAYERS)
    ]

    vectors = jnp.stack(
        [norm1_gain, norm1_bias, query_bias, value_bias, out_bias, norm2_gain, norm2_bias, down_bias]
    )
    head_piece = lax.dynamic_slice_in_dim(qkv_weight.reshape(LAYERS, 96, 3, D), head * HD, HD, axis=3)
    head_piece = jnp.where(place < H, head_piece, jnp.zeros_like(head_piece))
    packed = jnp.concatenate(
        [
            head_piece.reshape(LAYERS * 96 * 3 * HD // D, D),
            vectors.reshape(2, D),
            up_bias.reshape(1, D),
            jnp.zeros((13, D), BF16),
        ],
        axis=0,
    )
    gathered = spread_to(packed, S, "shard")
    gathered, first_piece = lax.optimization_barrier((gathered, layer_pieces[0]))
    layer_rows = [spread_to(first_piece, S, "shard"), lax.all_gather(layer_pieces[1], "shard", axis=0)]
    head_weights = gathered[:, :48].reshape(S, LAYERS, 96, 3 * HD)
    vectors = gathered[:, 48:50].reshape(S, 8, LAYERS, 96).transpose(2, 1, 0, 3).reshape(LAYERS, 8, D)
    vectors = vectors.astype(F32)
    up_shifts = gathered[:, 50].reshape(S, LAYERS, 8, 48)
    up_shifts = lax.dynamic_index_in_dim(up_shifts, rank, 2, False).transpose(1, 0, 2).reshape(LAYERS, 1, 384)
    up_shifts = up_shifts.astype(F32)
    head_shifts = jnp.concatenate(
        [
            lax.dynamic_slice_in_dim(vectors[:, 2], head * HD, HD, axis=1),
            jnp.zeros((LAYERS, HD), F32),
            lax.dynamic_slice_in_dim(vectors[:, 3], head * HD, HD, axis=1),
        ],
        axis=1,
    ).reshape(LAYERS, 1, 3 * HD)

    flowing = states.reshape(TOK, D).astype(F32)
    saved_all = []
    smalls = []
    all_params = []
    for layer in range(LAYERS):
        small = (
            head_shifts[layer],
            [vectors[layer, member : member + 1] for member in range(8)],
            up_shifts[layer],
        )
        smalls.append(small)
        flowing, saved, carried, params = forward_layer(
            flowing,
            head_weights[:, layer].reshape(D, 3 * HD),
            layer_rows[layer],
            join_out,
            small,
            places,
            gathered=states_all if layer == 0 else None,
            carried=cotangent.reshape(TOK, D) if layer == LAYERS - 1 else None,
        )
        saved_all.append(saved)
        all_params.append(params)
    result = flowing.astype(BF16).reshape(states.shape)
    grad_flow = cotangent.reshape(TOK, D).astype(F32)
    held = jnp.where(place < H, place, -1).reshape(1)
    grad_flow, owned_last, late, unused = backward_layer(
        grad_flow, carried, saved_all[1], all_params[1], smalls[1], places, held, 1, (), ()
    )
    every_last = lax.all_gather(owned_last[:OUTS], "ctx", axis=0)
    grad_flow, owned, late, every_last = backward_layer(
        grad_flow, None, saved_all[0], all_params[0], smalls[0], places, held, 0, (late,), every_last
    )
    every_first = lax.all_gather(owned[:OUTS], "ctx", axis=0)
    outs = jnp.stack([owned[OUTS:], owned_last[OUTS:]]).reshape(LAYERS, C, 6, D)
    outs = outs.transpose(1, 0, 2, 3).reshape(C, 12, D)
    outs = exchange(jnp.pad(outs, ((0, 0), (0, 4), (0, 0))), "ctx").astype(F32)
    outs = jnp.sum(outs, axis=0)[:12].astype(BF16)
    late = jnp.sum(exchange(late, "shard").astype(F32), axis=0).astype(BF16)
    late = jnp.concatenate([late[: SMALL + 4], outs], axis=0)
    near = spread_to(late, 8, "ctx", CHIP_GROUPS)
    near, wide = lax.optimization_barrier((near, unpack_wide(every_first, every_last)))
    ups, downs = wide
    every_late = jnp.concatenate([near, swap_core(near)], axis=0)
    places_of = jnp.arange(C, dtype=jnp.int32)
    slots = places_of // 2 + 8 * (places_of % 2 != core).astype(jnp.int32)
    qkv, outs, hiddens, *vectors = unpack_late(slots, every_late)
    return (
        result,
        grad_flow.astype(BF16).reshape(states.shape),
        vectors[0],
        vectors[1],
        qkv,
        vectors[2],
        vectors[3],
        outs,
        vectors[4],
        vectors[5],
        vectors[6],
        ups,
        hiddens,
        downs,
        vectors[7],
    )


def solution(mesh):
    matrix = P(None, "shard", None)
    vector = P(None, "shard")
    rows = P("shard", "ctx", None)
    params = (
        vector,
        vector,
        matrix,
        vector,
        vector,
        matrix,
        vector,
        vector,
        vector,
        matrix,
        vector,
        matrix,
        vector,
    )
    return jax.shard_map(
        shards,
        mesh=mesh,
        in_specs=(rows, rows, P()) + params,
        out_specs=(rows, rows) + params,
        check_vma=False,
    )
```

```python
import functools
import math

import jax
import jax.numpy as jnp
from jax import lax
from jax.experimental import pallas as pl
from jax.experimental.pallas import tpu as pltpu
from jax.sharding import PartitionSpec as P

H = 12
HD = 64
D = 768
FF = 3072
LAYERS = 2
S = 8
C = 16
TOK = 128
LEN = TOK * C
BLK = TOK // 2
ROWS = 256
EPSILON = 1e-05
NEGATIVE = -1e30
F32 = jnp.float32
BF16 = jnp.bfloat16

CHIP_GROUPS = [[2 * q + core for q in range(8)] for core in range(2)]
X_GROUPS = [[8 * y + 2 * x + core for x in range(4)] for y in range(2) for core in range(2)]
SWAP = [(i, i ^ 1) for i in range(C)]


def layer_norm(states, gain, shift):
    average = jnp.mean(states, axis=-1, keepdims=True)
    centered = states - average
    spread = jnp.mean(centered * centered, axis=-1, keepdims=True)
    return centered * lax.rsqrt(spread + EPSILON) * gain + shift


def exchange(parts, axis, groups=None):
    return lax.all_to_all(parts, axis, 0, 0, tiled=True, axis_index_groups=groups)


def spread_to(part, count, axis, groups=None):
    return exchange(jnp.broadcast_to(part[None], (count,) + part.shape), axis, groups)


def swap_core(part):
    return lax.ppermute(part, "ctx", SWAP)


def gather_ctx(part):
    own = spread_to(part, 8, "ctx", CHIP_GROUPS)
    return own, swap_core(own)


def gather_x(part, beside=()):
    own = spread_to(part, 4, "ctx", X_GROUPS)
    own, beside = lax.optimization_barrier((own, beside))
    return (own.reshape(4 * TOK, D), swap_core(own).reshape(4 * TOK, D)), beside


def scatter(near, far, groups, run=None):
    mine = near.astype(F32) + swap_core(far.astype(BF16)).astype(F32)
    mine = mine.astype(BF16)
    if run is None:
        return jnp.sum(exchange(mine, "ctx", groups).astype(F32), axis=0)
    start, ready = run
    mine, start = lax.optimization_barrier((mine, start))
    parts, result = lax.optimization_barrier((exchange(mine, "ctx", groups), ready(start)))
    return jnp.sum(parts.astype(F32), axis=0), result


def scatter_x(near, far, run=None):
    return scatter(near.reshape(4, TOK, D), far.reshape(4, TOK, D), X_GROUPS, run)


def dot(left, right, dims=((1,), (0,))):
    return lax.dot_general(left, right, (dims, ((), ())), preferred_element_type=F32)


def rows_of(block):
    return pl.ds(pl.multiple_of(block * BLK, BLK), BLK)


def attend_kernel(fresh, arrive_pos, ctx_pos, own_ref, other_ref, weight_ref, shift_ref, *rest):
    if fresh:
        gain_ref, bias_ref, mixed_ref, q_ref, k_ref, v_ref, own_normed, other_normed, out_ref = rest
    else:
        mixed_ref, q_ref, k_ref, v_ref, out_ref = rest
    for step in range(LEN // ROWS):
        half = LEN // ROWS // 2
        source = own_ref if step < half else other_ref
        rows = slice(step % half * ROWS, (step % half + 1) * ROWS)
        normed = source[rows, :]
        if fresh:
            normed = layer_norm(normed.astype(F32), gain_ref[...], bias_ref[...]).astype(BF16)
            (own_normed if step < half else other_normed)[rows, :] = normed
        piece = dot(normed, weight_ref[...]) + shift_ref[...]
        for part in range(ROWS // BLK):
            rows = rows_of(arrive_pos[step * (ROWS // BLK) + part])
            block = piece[part * BLK : (part + 1) * BLK, :]
            q_ref[rows, :] = (block[:, :HD].astype(BF16).astype(F32) * 0.125).astype(BF16)
            k_ref[rows, :] = block[:, HD : 2 * HD].astype(BF16)
            v_ref[rows, :] = block[:, 2 * HD :].astype(BF16)
    keep = lax.broadcasted_iota(jnp.int32, (ROWS, ROWS), 0) >= lax.broadcasted_iota(
        jnp.int32, (ROWS, ROWS), 1
    )
    for step in range(LEN // ROWS):
        start = step * ROWS
        queries = q_ref[start : start + ROWS, :]
        near = dot(queries, k_ref[start : start + ROWS, :], ((1,), (1,)))
        near = jnp.where(keep, near, NEGATIVE)
        highest = jnp.max(near, axis=1, keepdims=True)
        if step:
            far = dot(queries, k_ref[:start, :], ((1,), (1,)))
            highest = jnp.maximum(highest, jnp.max(far, axis=1, keepdims=True))
        weights = jnp.exp(near - highest)
        total = jnp.sum(weights, axis=1, keepdims=True)
        mixed = dot(weights.astype(BF16), v_ref[start : start + ROWS, :])
        if step:
            weights = jnp.exp(far - highest)
            total = total + jnp.sum(weights, axis=1, keepdims=True)
            mixed = mixed + dot(weights.astype(BF16), v_ref[:start, :])
        out_ref[start : start + ROWS, :] = (mixed / total).astype(BF16)
    for block in range(LEN // BLK):
        mixed_ref[block * BLK : (block + 1) * BLK, :] = out_ref[rows_of(ctx_pos[block]), :]


def attend_back_kernel(
    arrive_pos, ctx_pos, q_ref, k_ref, v_ref, grad_ref, weight_ref,
    to_arrive_ref, near_ref, far_ref, sums_ref, do_ref, dk_ref, dv_ref, all_ref
):
    for block in range(LEN // BLK):
        do_ref[rows_of(ctx_pos[block]), :] = grad_ref[block * BLK : (block + 1) * BLK, :]
    keep = lax.broadcasted_iota(jnp.int32, (ROWS, ROWS), 0) <= lax.broadcasted_iota(
        jnp.int32, (ROWS, ROWS), 1
    )
    for step in range(LEN // ROWS - 1, -1, -1):
        start = step * ROWS
        end = start + ROWS
        queries = q_ref[start:end, :]
        grads = do_ref[start:end, :]
        near_keys, near_values = k_ref[start:end, :], v_ref[start:end, :]
        near = jnp.where(keep, dot(near_keys, queries, ((1,), (1,))), NEGATIVE)
        highest = jnp.max(near, axis=0, keepdims=True)
        if step:
            far_keys, far_values = k_ref[:start, :], v_ref[:start, :]
            far = dot(far_keys, queries, ((1,), (1,)))
            highest = jnp.maximum(highest, jnp.max(far, axis=0, keepdims=True))
        near = jnp.exp(near - highest)
        total = jnp.sum(near, axis=0, keepdims=True)
        if step:
            far = jnp.exp(far - highest)
            total = total + jnp.sum(far, axis=0, keepdims=True)
        inverse = 1.0 / total
        near = near * inverse
        near_grad = dot(near_values, grads, ((1,), (1,)))
        inner = jnp.sum(near * near_grad, axis=0, keepdims=True)
        if step:
            far = far * inverse
            far_grad = dot(far_values, grads, ((1,), (1,)))
            inner = inner + jnp.sum(far * far_grad, axis=0, keepdims=True)
        near_scores = (near * (near_grad - inner)).astype(BF16)
        near_dk = dot(near_scores, queries)
        near_dv = dot(near.astype(BF16), grads)
        query_grad = dot(near_scores, near_keys, ((0,), (0,)))
        if step == LEN // ROWS - 1:
            dk_ref[start:end, :] = near_dk
            dv_ref[start:end, :] = near_dv
        else:
            dk_ref[start:end, :] += near_dk
            dv_ref[start:end, :] += near_dv
        if step:
            far_scores = (far * (far_grad - inner)).astype(BF16)
            far_dk = dot(far_scores, queries)
            far_dv = dot(far.astype(BF16), grads)
            query_grad = query_grad + dot(far_scores, far_keys, ((0,), (0,)))
            if step == LEN // ROWS - 1:
                dk_ref[:start, :] = far_dk
                dv_ref[:start, :] = far_dv
            else:
                dk_ref[:start, :] += far_dk
                dv_ref[:start, :] += far_dv
        all_ref[start:end, :] = jnp.concatenate(
            [query_grad * 0.125, dk_ref[start:end, :], dv_ref[start:end, :]], axis=1
        ).astype(BF16)
    for block in range(LEN // BLK):
        to_arrive_ref[block * BLK : (block + 1) * BLK, : 3 * HD] = all_ref[rows_of(arrive_pos[block]), :]
    to_arrive_ref[:, 3 * HD :] = jnp.zeros((LEN, HD), BF16)
    sums_ref[...] = jnp.sum(all_ref[...].astype(F32), axis=0, keepdims=True)
    for step in range(LEN // ROWS):
        rows = slice(step * ROWS, (step + 1) * ROWS)
        part = dot(to_arrive_ref[rows, : 3 * HD], weight_ref[...], ((1,), (1,))).astype(BF16)
        if step * ROWS < LEN // 2:
            near_ref[rows, :] = part
        else:
            far_ref[step * ROWS - LEN // 2 : (step + 1) * ROWS - LEN // 2, :] = part


SMEM = pl.BlockSpec(memory_space=pltpu.SMEM)
WHOLE = pl.BlockSpec()
VMEM_BYTES = 60 * 2**20


def attend(arrive_pos, ctx_pos, own, other, weight, shift, norm=None):
    head = jax.ShapeDtypeStruct((LEN, HD), BF16)
    fresh = norm is not None
    outs = (head,) * 4
    extra = ()
    if fresh:
        outs = outs + (jax.ShapeDtypeStruct((LEN // 2, D), BF16),) * 2
        extra = tuple(norm)
    return pl.pallas_call(
        functools.partial(attend_kernel, fresh),
        out_shape=outs,
        in_specs=[SMEM, SMEM] + [WHOLE] * (4 + len(extra)),
        out_specs=(WHOLE,) * len(outs),
        scratch_shapes=[pltpu.VMEM((LEN, HD), BF16)],
        compiler_params=pltpu.CompilerParams(vmem_limit_bytes=VMEM_BYTES),
        cost_estimate=pl.CostEstimate(flops=2 * 10**9, bytes_accessed=5 * 10**6, transcendentals=2 * 10**6),
    )(arrive_pos, ctx_pos, own, other, weight, shift, *extra)


def attend_back(arrive_pos, ctx_pos, queries, keys, values, grads, weight):
    return pl.pallas_call(
        attend_back_kernel,
        out_shape=(
            jax.ShapeDtypeStruct((LEN, 4 * HD), BF16),
            jax.ShapeDtypeStruct((LEN // 2, D), BF16),
            jax.ShapeDtypeStruct((LEN // 2, D), BF16),
            jax.ShapeDtypeStruct((1, 3 * HD), F32),
        ),
        in_specs=[SMEM, SMEM] + [WHOLE] * 5,
        out_specs=(WHOLE,) * 4,
        scratch_shapes=[
            pltpu.VMEM((LEN, HD), BF16),
            pltpu.VMEM((LEN, HD), F32),
            pltpu.VMEM((LEN, HD), F32),
            pltpu.VMEM((LEN, 3 * HD), BF16),
        ],
        compiler_params=pltpu.CompilerParams(vmem_limit_bytes=VMEM_BYTES),
        cost_estimate=pl.CostEstimate(flops=4 * 10**9, bytes_accessed=5 * 10**6, transcendentals=2 * 10**6),
    )(arrive_pos, ctx_pos, queries, keys, values, grads, weight)


GELU_SCALE = math.sqrt(2.0 / math.pi)
GELU_CUBE = 0.044715


def load_feed(rows_ref, up_ref, down_ref):
    for owner in range(S):
        for part in range(2):
            first = owner * 96 + part * 48
            up_ref[first : first + 48, :] = rows_ref[owner, 48:96, part * 384 : (part + 1) * 384]
        down_ref[owner * 48 : (owner + 1) * 48, :] = rows_ref[owner, 96:144, :]


def feed_kernel(own_ref, other_ref, rows_ref, shift_ref, hidden_ref, active_ref, near_ref, far_ref, up_ref, down_ref):
    load_feed(rows_ref, up_ref, down_ref)
    for side, (source, target) in enumerate(((own_ref, near_ref), (other_ref, far_ref))):
        for step in range(4 * TOK // ROWS):
            rows = slice(step * ROWS, (step + 1) * ROWS)
            saved = slice(side * 4 * TOK + step * ROWS, side * 4 * TOK + (step + 1) * ROWS)
            hidden = dot(source[rows, :], up_ref[...]) + shift_ref[...]
            hidden_ref[saved, :] = hidden
            inner = GELU_SCALE * (hidden + GELU_CUBE * hidden * hidden * hidden)
            active = (hidden * (0.5 * (1.0 + jnp.tanh(inner)))).astype(BF16)
            active_ref[saved, :] = active
            target[rows, :] = dot(active, down_ref[...]).astype(BF16)


def feed_back_kernel(own_ref, other_ref, rows_ref, hidden_ref, grad_ref, near_ref, far_ref, sums_ref, up_ref, down_ref):
    load_feed(rows_ref, up_ref, down_ref)
    sums = jnp.zeros((1, 384), F32)
    for side, (source, target) in enumerate(((own_ref, near_ref), (other_ref, far_ref))):
        for step in range(4 * TOK // ROWS):
            rows = slice(step * ROWS, (step + 1) * ROWS)
            saved = slice(side * 4 * TOK + step * ROWS, side * 4 * TOK + (step + 1) * ROWS)
            active_grad = dot(source[rows, :], down_ref[...], ((1,), (1,)))
            hidden = hidden_ref[saved, :]
            square = hidden * hidden
            bend = jnp.tanh(GELU_SCALE * (hidden + GELU_CUBE * square * hidden))
            slope = GELU_SCALE * (1.0 + 3.0 * GELU_CUBE * square)
            slope = 0.5 * (1.0 + bend) + 0.5 * hidden * (1.0 - bend * bend) * slope
            grad = (active_grad * slope).astype(BF16)
            grad_ref[saved, :] = grad
            sums = sums + jnp.sum(grad.astype(F32), axis=0, keepdims=True)
            target[rows, :] = dot(grad, up_ref[...], ((1,), (1,))).astype(BF16)
    sums_ref[...] = sums


def feed(own, other, rows, shift):
    half = jax.ShapeDtypeStruct((4 * TOK, D), BF16)
    return pl.pallas_call(
        feed_kernel,
        out_shape=(
            jax.ShapeDtypeStruct((8 * TOK, 384), F32),
            jax.ShapeDtypeStruct((8 * TOK, 384), BF16),
            half,
            half,
        ),
        in_specs=[WHOLE] * 4,
        out_specs=(WHOLE,) * 4,
        scratch_shapes=[pltpu.VMEM((D, 384), BF16), pltpu.VMEM((384, D), BF16)],
        compiler_params=pltpu.CompilerParams(vmem_limit_bytes=VMEM_BYTES),
        cost_estimate=pl.CostEstimate(flops=10**6, bytes_accessed=10**5, transcendentals=0),
    )(own, other, rows, shift)


def feed_back(own, other, rows, hidden):
    half = jax.ShapeDtypeStruct((4 * TOK, D), BF16)
    return pl.pallas_call(
        feed_back_kernel,
        out_shape=(
            jax.ShapeDtypeStruct((8 * TOK, 384), BF16),
            half,
            half,
            jax.ShapeDtypeStruct((1, 384), F32),
        ),
        in_specs=[WHOLE] * 4,
        out_specs=(WHOLE,) * 4,
        scratch_shapes=[pltpu.VMEM((D, 384), BF16), pltpu.VMEM((384, D), BF16)],
        compiler_params=pltpu.CompilerParams(vmem_limit_bytes=VMEM_BYTES),
        cost_estimate=pl.CostEstimate(flops=12 * 10**8, bytes_accessed=7 * 10**6, transcendentals=4 * 10**5),
    )(own, other, rows, hidden)


UPS, DOWNS, OUTS, FIRST = 0, 48, 96, 192
HEADS, SMALL, SECOND = 0, 64, 80
BOTH_ROWS = ((0,), (0,))


def first_grads_kernel(
    own_ref, other_ref, hidden_ref, active_ref, own_down_ref, other_down_ref, mixed_ref, attended_ref, out_ref
):
    half = 4 * TOK
    ups = dot(own_ref[...], hidden_ref[:half, :], BOTH_ROWS) + dot(other_ref[...], hidden_ref[half:, :], BOTH_ROWS)
    ups = ups.astype(BF16)
    for owner in range(S):
        for part in range(2):
            first = owner * 96 + part * 48
            out_ref[owner, UPS:DOWNS, part * 384 : (part + 1) * 384] = ups[first : first + 48, :]
    downs = dot(active_ref[:half, :], own_down_ref[...], BOTH_ROWS)
    downs = (downs + dot(active_ref[half:, :], other_down_ref[...], BOTH_ROWS)).astype(BF16)
    for owner in range(S):
        out_ref[owner, DOWNS:OUTS, :] = downs[owner * 48 : (owner + 1) * 48, :]
    outs = dot(mixed_ref[...], attended_ref[...], BOTH_ROWS).astype(BF16)
    for owner in range(S):
        out_ref[owner, OUTS:FIRST, :] = outs[owner * 96 : (owner + 1) * 96, :]


def first_grads(*parts):
    return pl.pallas_call(
        first_grads_kernel,
        out_shape=jax.ShapeDtypeStruct((S, FIRST, D), BF16),
        in_specs=[WHOLE] * len(parts),
        out_specs=WHOLE,
        compiler_params=pltpu.CompilerParams(vmem_limit_bytes=VMEM_BYTES),
        cost_estimate=pl.CostEstimate(flops=2 * 10**9, bytes_accessed=9 * 10**6, transcendentals=0),
    )(*parts)


def second_grads_kernel(layer, head, own_ref, other_ref, arrive_ref, sums_ref, hidden_sum_ref, *rest):
    vector_refs, prior_refs, out_ref = rest[:6], rest[6:-1], rest[-1]
    half = LEN // 2
    heads = dot(own_ref[...], arrive_ref[:half, :], BOTH_ROWS) + dot(other_ref[...], arrive_ref[half:, :], BOTH_ROWS)
    heads = heads.astype(BF16)
    here = lax.broadcasted_iota(jnp.int32, (1, D), 1) // HD == head[0]
    queries = jnp.where(here, jnp.concatenate([sums_ref[:, :HD]] * H, axis=1), 0.0)
    values = jnp.where(here, jnp.concatenate([sums_ref[:, 2 * HD : 3 * HD]] * H, axis=1), 0.0)
    vectors = [ref[...] for ref in vector_refs]
    vectors = vectors[:2] + [queries, values] + vectors[2:]
    row = lax.broadcasted_iota(jnp.int32, (SECOND - SMALL, D), 0)
    for owner in range(S):
        for part in range(3):
            first = owner * 96 + part * 32
            out_ref[owner, layer * 32 : (layer + 1) * 32, part * 256 : (part + 1) * 256] = heads[first : first + 32, :]
        mine = jnp.concatenate([member[:, owner * 96 : (owner + 1) * 96] for member in vectors], axis=1)
        hidden = jnp.concatenate(
            [hidden_sum_ref[:, owner * 48 : (owner + 1) * 48], jnp.zeros((1, D - 48), F32)], axis=1
        )
        block = jnp.where(row == 2 * layer, mine, jnp.where(row == 2 * layer + 1, hidden, 0.0))
        for prior_ref in prior_refs:
            block = block + prior_ref[owner, SMALL:SECOND, :].astype(F32)
            out_ref[owner, 32:SMALL, :] = prior_ref[owner, 32:SMALL, :]
        if not prior_refs:
            out_ref[owner, :32, :] = jnp.zeros((32, D), BF16)
        out_ref[owner, SMALL:SECOND, :] = block.astype(BF16)


def second_grads(layer, head, *parts):
    return pl.pallas_call(
        functools.partial(second_grads_kernel, layer),
        out_shape=jax.ShapeDtypeStruct((S, SECOND, D), BF16),
        in_specs=[SMEM] + [WHOLE] * len(parts),
        out_specs=WHOLE,
        compiler_params=pltpu.CompilerParams(vmem_limit_bytes=VMEM_BYTES),
        cost_estimate=pl.CostEstimate(flops=10**9, bytes_accessed=5 * 10**6, transcendentals=0),
    )(head, *parts)


def unpack_wide_kernel(first_ref, last_ref, up_ref, down_ref):
    for layer, wide_ref in enumerate((first_ref, last_ref)):
        def wide(place, start, end, wide_ref=wide_ref):
            return wide_ref[place, start:end, :].astype(F32)

        for rank in range(8):
            block = wide(rank, UPS, DOWNS) + wide(rank + 8, UPS, DOWNS)
            for part in range(2):
                for owner in range(S):
                    lane = part * 384 + owner * 48
                    column = owner * 384 + rank * 48
                    up_ref[layer, part * 48 : (part + 1) * 48, column : column + 48] = block[:, lane : lane + 48]
            block = wide(rank, DOWNS, OUTS) + wide(rank + 8, DOWNS, OUTS)
            down_ref[layer, rank * 48 : (rank + 1) * 48, :] = block


def unpack_late_kernel(slots, late_ref, qkv_ref, out_ref, up_shift_ref, *vector_refs):
    def late(place, start, end):
        return late_ref[slots[place], start:end, :].astype(F32)

    for layer in range(LAYERS):
        for head in range(H):
            block = late(head, layer * 32, (layer + 1) * 32)
            for part in range(3):
                for kind in range(3):
                    lane = part * 256 + kind * HD
                    column = kind * D + head * HD
                    qkv_ref[layer, part * 32 : (part + 1) * 32, column : column + HD] = block[:, lane : lane + HD]
    totals = [None] * LAYERS
    for rank in range(8):
        low, high = late(rank, SMALL, SECOND), late(rank + 8, SMALL, SECOND)
        small = low + high
        for layer in range(LAYERS):
            up_shift_ref[layer : layer + 1, rank * 48 : (rank + 1) * 48] = small[2 * layer + 1 : 2 * layer + 2, :48]
            mine = small[2 * layer : 2 * layer + 1, :]
            totals[layer] = mine if rank == 0 else totals[layer] + mine
            rows = slice(4 + 6 * layer, 10 + 6 * layer)
            out_ref[layer, rank * 6 : (rank + 1) * 6, :] = low[rows, :]
            out_ref[layer, (rank + 8) * 6 : (rank + 9) * 6, :] = high[rows, :]
    for layer in range(LAYERS):
        for member, ref in enumerate(vector_refs):
            ref[layer : layer + 1, :] = totals[layer][:, member * 96 : (member + 1) * 96]


def unpack_wide(first, last):
    shapes = [(96, FF), (384, D)]
    return pl.pallas_call(
        unpack_wide_kernel,
        out_shape=tuple(jax.ShapeDtypeStruct((LAYERS,) + shape, F32) for shape in shapes),
        in_specs=[WHOLE] * 2,
        out_specs=(WHOLE,) * len(shapes),
        compiler_params=pltpu.CompilerParams(vmem_limit_bytes=VMEM_BYTES),
        cost_estimate=pl.CostEstimate(flops=10**6, bytes_accessed=10 * 10**6, transcendentals=0),
    )(first, last)


def unpack_late(slots, late):
    shapes = [(96, 3 * D), (96, D), (384,)] + [(96,)] * 8
    return pl.pallas_call(
        unpack_late_kernel,
        out_shape=tuple(jax.ShapeDtypeStruct((LAYERS,) + shape, F32) for shape in shapes),
        in_specs=[SMEM, WHOLE],
        out_specs=(WHOLE,) * len(shapes),
        compiler_params=pltpu.CompilerParams(vmem_limit_bytes=VMEM_BYTES),
        cost_estimate=pl.CostEstimate(flops=10**6, bytes_accessed=5 * 10**6, transcendentals=0),
    )(slots, late)


def join_cores(core, own, other, axis):
    return jnp.where(
        core == 0, jnp.concatenate([own, other], axis=axis), jnp.concatenate([other, own], axis=axis)
    )


def forward_layer(flowing, head_weight, layer_rows, join_out, small, places, gathered=None, carried=None):
    arrive_pos, ctx_pos = places
    head_shift, vectors, up_shift = small
    gain_one, bias_one, unused, unused, out_shift, gain_two, bias_two, down_shift = vectors
    if gathered is not None:
        mixed_head, queries, keys, values, own, other = attend(
            arrive_pos, ctx_pos, *gathered, head_weight, head_shift, (gain_one, bias_one)
        )
        mixed_head, layer_rows = lax.optimization_barrier((mixed_head, layer_rows))
    else:
        normed = layer_norm(flowing, gain_one, bias_one).astype(BF16)
        normed, layer_rows = lax.optimization_barrier((normed, layer_rows))
        own, other = (part.reshape(LEN // 2, D) for part in gather_ctx(normed))
        own, other, carried = lax.optimization_barrier((own, other, carried))
        carried = spread_to(carried, 4, "ctx", X_GROUPS)
        mixed_head, queries, keys, values = attend(arrive_pos, ctx_pos, own, other, head_weight, head_shift)
        mixed_head, carried = lax.optimization_barrier((mixed_head, carried))
        carried = (carried.reshape(4 * TOK, D), swap_core(carried).reshape(4 * TOK, D))
    out_full = join_out(layer_rows)
    mixed = exchange(mixed_head.reshape(C, TOK, HD), "ctx")[:H]
    mixed = mixed.transpose(1, 0, 2).reshape(TOK, D)
    middle = flowing + dot(mixed, out_full) + out_shift
    second = layer_norm(middle, gain_two, bias_two).astype(BF16)
    second_all, unused = gather_x(second)
    hidden, activated, near, far = feed(*second_all, layer_rows, up_shift)
    if carried is None:
        summed = scatter_x(near, far)
    else:
        run = ((carried, layer_rows, hidden), lambda start: feed_back(*start[0], start[1], start[2]))
        summed, begun = scatter_x(near, far, run)
        carried = (carried, begun)
    output = middle + summed + down_shift
    saved = (flowing, own, other, queries, keys, values, mixed, middle, second_all, hidden, activated)
    return output, saved, carried, (head_weight, out_full, layer_rows)


def backward_layer(grad_out, begun, saved, params, small, places, head, layer, prior, spread):
    arrive_pos, ctx_pos = places
    head_weight, out_full, layer_rows = params
    unused, vectors, unused = small
    gain_one, bias_one, unused, unused, unused, gain_two, bias_two, unused = vectors
    flowing, own, other, queries, keys, values, mixed, middle, second_all, hidden, activated = saved
    down_in = grad_out.astype(BF16)
    down_shift_grad = jnp.sum(down_in.astype(F32), axis=0, keepdims=True)
    if begun is None:
        down_all, prior = gather_x(down_in, prior)
        begun = feed_back(*down_all, layer_rows, hidden)
    else:
        down_all, begun = begun
    hidden_grad, near, far, up_shift_grad = begun
    second_grad = scatter_x(near, far)
    unused, norm_back = jax.vjp(layer_norm, middle, gain_two, bias_two)
    middle_part, gain_two_grad, bias_two_grad = norm_back(second_grad)
    middle_grad = grad_out + middle_part
    attended_in = middle_grad.astype(BF16)
    out_shift_grad = jnp.sum(attended_in.astype(F32), axis=0, keepdims=True)
    mixed_grad = dot(attended_in, out_full, ((1,), (1,))).astype(BF16)
    mixed_grad = mixed_grad.reshape(TOK, H, HD).transpose(1, 0, 2)
    mixed_grad = jnp.concatenate([mixed_grad, jnp.zeros((C - H, TOK, HD), BF16)], axis=0)
    mixed_grad = exchange(mixed_grad, "ctx").reshape(LEN, HD)
    packed = first_grads(*second_all, hidden_grad, activated, *down_all, mixed, attended_in)
    mixed_grad, packed = lax.optimization_barrier((mixed_grad, packed))
    owned = jnp.sum(exchange(packed, "shard").astype(F32), axis=0).astype(BF16)
    to_arrive, near, far, sums = attend_back(
        arrive_pos, ctx_pos, queries, keys, values, mixed_grad, head_weight
    )
    near, far = near.reshape(8, TOK, D), far.reshape(8, TOK, D)
    near = (near.astype(F32) + swap_core(far).astype(F32)).astype(BF16)
    near, owned, spread = lax.optimization_barrier((near, owned, spread))
    normed_grad = jnp.sum(exchange(near, "ctx", CHIP_GROUPS).astype(F32), axis=0)
    unused, first_back = jax.vjp(layer_norm, flowing, gain_one, bias_one)
    flowing_part, gain_one_grad, bias_one_grad = first_back(normed_grad)
    late = second_grads(
        layer,
        head,
        own,
        other,
        to_arrive,
        sums,
        up_shift_grad,
        gain_one_grad,
        bias_one_grad,
        out_shift_grad,
        gain_two_grad,
        bias_two_grad,
        down_shift_grad,
        *prior,
    )
    return middle_grad + flowing_part, owned, late, spread


def shards(
    states,
    cotangent,
    pair_order,
    norm1_gain,
    norm1_bias,
    qkv_weight,
    query_bias,
    value_bias,
    out_weight,
    out_bias,
    norm2_gain,
    norm2_bias,
    up_weight,
    up_bias,
    down_weight,
    down_bias,
):
    place = lax.axis_index("ctx")
    core = place % 2
    rank = place % 8
    head = jnp.minimum(place, H - 1)
    pairs = jnp.stack([pair_order, 2 * C - 1 - pair_order], axis=1)
    ctx_pos = pairs.reshape(-1)
    by_core = pairs.reshape(8, 2, 2).transpose(1, 0, 2)
    arrive_pos = jnp.where(core == 0, by_core, by_core[::-1]).reshape(-1)
    places = (arrive_pos, ctx_pos)

    states_all = tuple(part.reshape(LEN // 2, D) for part in gather_ctx(states.reshape(TOK, D)))

    unit = lax.broadcasted_iota(jnp.int32, (FF, 384), 0)
    column = lax.broadcasted_iota(jnp.int32, (FF, 384), 1)
    pick = (unit == (column // 48) * 384 + rank * 48 + column % 48).astype(BF16)
    up_piece = dot(up_weight.reshape(LAYERS * 96, FF), pick).astype(BF16).reshape(LAYERS, 96, 384)
    down_piece = lax.dynamic_slice_in_dim(down_weight, rank * 48, 48, axis=1)
    out_piece = lax.dynamic_slice_in_dim(out_weight, core * 384, 384, axis=2)

    def beside(piece):
        return jnp.concatenate([piece[:48], piece[48:]], axis=1)

    def apart(piece):
        return jnp.concatenate([piece[..., :384], piece[..., 384:]], axis=1).reshape(D, 384)

    def join_out(rows):
        own = apart(rows[:, :48])
        return join_cores(core, own, swap_core(own), 1)

    layer_pieces = [
        jnp.concatenate([beside(out_piece[layer]), beside(up_piece[layer]), down_piece[layer]], axis=0)
        for layer in range(LAYERS)
    ]

    vectors = jnp.stack(
        [norm1_gain, norm1_bias, query_bias, value_bias, out_bias, norm2_gain, norm2_bias, down_bias]
    )
    head_piece = lax.dynamic_slice_in_dim(qkv_weight.reshape(LAYERS, 96, 3, D), head * HD, HD, axis=3)
    head_piece = jnp.where(place < H, head_piece, jnp.zeros_like(head_piece))
    packed = jnp.concatenate(
        [
            head_piece.reshape(LAYERS * 96 * 3 * HD // D, D),
            vectors.reshape(2, D),
            up_bias.reshape(1, D),
            jnp.zeros((13, D), BF16),
        ],
        axis=0,
    )
    gathered = spread_to(packed, S, "shard")
    gathered, first_piece = lax.optimization_barrier((gathered, layer_pieces[0]))
    layer_rows = [spread_to(first_piece, S, "shard"), lax.all_gather(layer_pieces[1], "shard", axis=0)]
    head_weights = gathered[:, :48].reshape(S, LAYERS, 96, 3 * HD)
    vectors = gathered[:, 48:50].reshape(S, 8, LAYERS, 96).transpose(2, 1, 0, 3).reshape(LAYERS, 8, D)
    vectors = vectors.astype(F32)
    up_shifts = gathered[:, 50].reshape(S, LAYERS, 8, 48)
    up_shifts = lax.dynamic_index_in_dim(up_shifts, rank, 2, False).transpose(1, 0, 2).reshape(LAYERS, 1, 384)
    up_shifts = up_shifts.astype(F32)
    head_shifts = jnp.concatenate(
        [
            lax.dynamic_slice_in_dim(vectors[:, 2], head * HD, HD, axis=1),
            jnp.zeros((LAYERS, HD), F32),
            lax.dynamic_slice_in_dim(vectors[:, 3], head * HD, HD, axis=1),
        ],
        axis=1,
    ).reshape(LAYERS, 1, 3 * HD)

    flowing = states.reshape(TOK, D).astype(F32)
    saved_all = []
    smalls = []
    all_params = []
    for layer in range(LAYERS):
        small = (
            head_shifts[layer],
            [vectors[layer, member : member + 1] for member in range(8)],
            up_shifts[layer],
        )
        smalls.append(small)
        flowing, saved, carried, params = forward_layer(
            flowing,
            head_weights[:, layer].reshape(D, 3 * HD),
            layer_rows[layer],
            join_out,
            small,
            places,
            gathered=states_all if layer == 0 else None,
            carried=cotangent.reshape(TOK, D) if layer == LAYERS - 1 else None,
        )
        saved_all.append(saved)
        all_params.append(params)
    result = flowing.astype(BF16).reshape(states.shape)
    grad_flow = cotangent.reshape(TOK, D).astype(F32)
    held = jnp.where(place < H, place, -1).reshape(1)
    grad_flow, owned_last, late, unused = backward_layer(
        grad_flow, carried, saved_all[1], all_params[1], smalls[1], places, held, 1, (), ()
    )
    every_last = lax.all_gather(owned_last[:OUTS], "ctx", axis=0)
    grad_flow, owned, late, every_last = backward_layer(
        grad_flow, None, saved_all[0], all_params[0], smalls[0], places, held, 0, (late,), every_last
    )
    every_first = lax.all_gather(owned[:OUTS], "ctx", axis=0)
    outs = jnp.stack([owned[OUTS:], owned_last[OUTS:]]).reshape(LAYERS, C, 6, D)
    outs = outs.transpose(1, 0, 2, 3).reshape(C, 12, D)
    outs = exchange(jnp.pad(outs, ((0, 0), (0, 4), (0, 0))), "ctx").astype(F32)
    outs = jnp.sum(outs, axis=0)[:12].astype(BF16)
    late = jnp.sum(exchange(late, "shard").astype(F32), axis=0).astype(BF16)
    late = jnp.concatenate([late[: SMALL + 4], outs], axis=0)
    near = spread_to(late, 8, "ctx", CHIP_GROUPS)
    near, wide = lax.optimization_barrier((near, unpack_wide(every_first, every_last)))
    ups, downs = wide
    every_late = jnp.concatenate([near, swap_core(near)], axis=0)
    places_of = jnp.arange(C, dtype=jnp.int32)
    slots = places_of // 2 + 8 * (places_of % 2 != core).astype(jnp.int32)
    qkv, outs, hiddens, *vectors = unpack_late(slots, every_late)
    return (
        result,
        grad_flow.astype(BF16).reshape(states.shape),
        vectors[0],
        vectors[1],
        qkv,
        vectors[2],
        vectors[3],
        outs,
        vectors[4],
        vectors[5],
        vectors[6],
        ups,
        hiddens,
        downs,
        vectors[7],
    )


def solution(mesh):
    matrix = P(None, "shard", None)
    vector = P(None, "shard")
    rows = P("shard", "ctx", None)
    params = (
        vector,
        vector,
        matrix,
        vector,
        vector,
        matrix,
        vector,
        vector,
        vector,
        matrix,
        vector,
        matrix,
        vector,
    )
    return jax.shard_map(
        shards,
        mesh=mesh,
        in_specs=(rows, rows, P()) + params,
        out_specs=(rows, rows) + params,
        check_vma=False,
    )
```

```python
import functools
import math

import jax
import jax.numpy as jnp
from jax import lax
from jax.experimental import pallas as pl
from jax.experimental.pallas import tpu as pltpu
from jax.sharding import PartitionSpec as P

H = 12
HD = 64
D = 768
FF = 3072
LAYERS = 2
S = 8
C = 16
TOK = 128
LEN = TOK * C
BLK = TOK // 2
ROWS = 256
EPSILON = 1e-05
NEGATIVE = -1e30
F32 = jnp.float32
BF16 = jnp.bfloat16

CHIP_GROUPS = [[2 * q + core for q in range(8)] for core in range(2)]
X_GROUPS = [[8 * y + 2 * x + core for x in range(4)] for y in range(2) for core in range(2)]
SWAP = [(i, i ^ 1) for i in range(C)]


def layer_norm(states, gain, shift):
    average = jnp.mean(states, axis=-1, keepdims=True)
    centered = states - average
    spread = jnp.mean(centered * centered, axis=-1, keepdims=True)
    return centered * lax.rsqrt(spread + EPSILON) * gain + shift


def exchange(parts, axis, groups=None):
    return lax.all_to_all(parts, axis, 0, 0, tiled=True, axis_index_groups=groups)


def spread_to(part, count, axis, groups=None):
    return exchange(jnp.broadcast_to(part[None], (count,) + part.shape), axis, groups)


def swap_core(part):
    return lax.ppermute(part, "ctx", SWAP)


def gather_ctx(part):
    own = spread_to(part, 8, "ctx", CHIP_GROUPS)
    return own, swap_core(own)


def gather_x(part, beside=()):
    own = spread_to(part, 4, "ctx", X_GROUPS)
    own, beside = lax.optimization_barrier((own, beside))
    return (own.reshape(4 * TOK, D), swap_core(own).reshape(4 * TOK, D)), beside


def scatter(near, far, groups, run=None):
    mine = near.astype(F32) + swap_core(far.astype(BF16)).astype(F32)
    mine = mine.astype(BF16)
    if run is None:
        return jnp.sum(exchange(mine, "ctx", groups).astype(F32), axis=0)
    start, ready = run
    mine, start = lax.optimization_barrier((mine, start))
    parts, result = lax.optimization_barrier((exchange(mine, "ctx", groups), ready(start)))
    return jnp.sum(parts.astype(F32), axis=0), result


def scatter_x(near, far, run=None):
    return scatter(near.reshape(4, TOK, D), far.reshape(4, TOK, D), X_GROUPS, run)


def dot(left, right, dims=((1,), (0,))):
    return lax.dot_general(left, right, (dims, ((), ())), preferred_element_type=F32)


def rows_of(block):
    return pl.ds(pl.multiple_of(block * BLK, BLK), BLK)


def attend_kernel(fresh, arrive_pos, ctx_pos, own_ref, other_ref, weight_ref, shift_ref, *rest):
    if fresh:
        gain_ref, bias_ref, mixed_ref, q_ref, k_ref, v_ref, own_normed, other_normed, out_ref = rest
    else:
        mixed_ref, q_ref, k_ref, v_ref, out_ref = rest
    for step in range(LEN // ROWS):
        half = LEN // ROWS // 2
        source = own_ref if step < half else other_ref
        rows = slice(step % half * ROWS, (step % half + 1) * ROWS)
        normed = source[rows, :]
        if fresh:
            normed = layer_norm(normed.astype(F32), gain_ref[...], bias_ref[...]).astype(BF16)
            (own_normed if step < half else other_normed)[rows, :] = normed
        piece = dot(normed, weight_ref[...]) + shift_ref[...]
        for part in range(ROWS // BLK):
            rows = rows_of(arrive_pos[step * (ROWS // BLK) + part])
            block = piece[part * BLK : (part + 1) * BLK, :]
            q_ref[rows, :] = (block[:, :HD].astype(BF16).astype(F32) * 0.125).astype(BF16)
            k_ref[rows, :] = block[:, HD : 2 * HD].astype(BF16)
            v_ref[rows, :] = block[:, 2 * HD :].astype(BF16)
    keep = lax.broadcasted_iota(jnp.int32, (ROWS, ROWS), 0) >= lax.broadcasted_iota(
        jnp.int32, (ROWS, ROWS), 1
    )
    for step in range(LEN // ROWS):
        start = step * ROWS
        queries = q_ref[start : start + ROWS, :]
        near = dot(queries, k_ref[start : start + ROWS, :], ((1,), (1,)))
        near = jnp.where(keep, near, NEGATIVE)
        highest = jnp.max(near, axis=1, keepdims=True)
        if step:
            far = dot(queries, k_ref[:start, :], ((1,), (1,)))
            highest = jnp.maximum(highest, jnp.max(far, axis=1, keepdims=True))
        weights = jnp.exp(near - highest)
        total = jnp.sum(weights, axis=1, keepdims=True)
        mixed = dot(weights.astype(BF16), v_ref[start : start + ROWS, :])
        if step:
            weights = jnp.exp(far - highest)
            total = total + jnp.sum(weights, axis=1, keepdims=True)
            mixed = mixed + dot(weights.astype(BF16), v_ref[:start, :])
        out_ref[start : start + ROWS, :] = (mixed / total).astype(BF16)
    for block in range(LEN // BLK):
        mixed_ref[block * BLK : (block + 1) * BLK, :] = out_ref[rows_of(ctx_pos[block]), :]


def attend_back_kernel(
    arrive_pos, ctx_pos, q_ref, k_ref, v_ref, grad_ref, weight_ref,
    to_arrive_ref, near_ref, far_ref, sums_ref, do_ref, dk_ref, dv_ref, all_ref
):
    for block in range(LEN // BLK):
        do_ref[rows_of(ctx_pos[block]), :] = grad_ref[block * BLK : (block + 1) * BLK, :]
    keep = lax.broadcasted_iota(jnp.int32, (ROWS, ROWS), 0) <= lax.broadcasted_iota(
        jnp.int32, (ROWS, ROWS), 1
    )
    for step in range(LEN // ROWS - 1, -1, -1):
        start = step * ROWS
        end = start + ROWS
        queries = q_ref[start:end, :]
        grads = do_ref[start:end, :]
        near_keys, near_values = k_ref[start:end, :], v_ref[start:end, :]
        near = jnp.where(keep, dot(near_keys, queries, ((1,), (1,))), NEGATIVE)
        highest = jnp.max(near, axis=0, keepdims=True)
        if step:
            far_keys, far_values = k_ref[:start, :], v_ref[:start, :]
            far = dot(far_keys, queries, ((1,), (1,)))
            highest = jnp.maximum(highest, jnp.max(far, axis=0, keepdims=True))
        near = jnp.exp(near - highest)
        total = jnp.sum(near, axis=0, keepdims=True)
        if step:
            far = jnp.exp(far - highest)
            total = total + jnp.sum(far, axis=0, keepdims=True)
        inverse = 1.0 / total
        near = near * inverse
        near_grad = dot(near_values, grads, ((1,), (1,)))
        inner = jnp.sum(near * near_grad, axis=0, keepdims=True)
        if step:
            far = far * inverse
            far_grad = dot(far_values, grads, ((1,), (1,)))
            inner = inner + jnp.sum(far * far_grad, axis=0, keepdims=True)
        near_scores = (near * (near_grad - inner)).astype(BF16)
        near_dk = dot(near_scores, queries)
        near_dv = dot(near.astype(BF16), grads)
        query_grad = dot(near_scores, near_keys, ((0,), (0,)))
        if step == LEN // ROWS - 1:
            dk_ref[start:end, :] = near_dk
            dv_ref[start:end, :] = near_dv
        else:
            dk_ref[start:end, :] += near_dk
            dv_ref[start:end, :] += near_dv
        if step:
            far_scores = (far * (far_grad - inner)).astype(BF16)
            far_dk = dot(far_scores, queries)
            far_dv = dot(far.astype(BF16), grads)
            query_grad = query_grad + dot(far_scores, far_keys, ((0,), (0,)))
            if step == LEN // ROWS - 1:
                dk_ref[:start, :] = far_dk
                dv_ref[:start, :] = far_dv
            else:
                dk_ref[:start, :] += far_dk
                dv_ref[:start, :] += far_dv
        all_ref[start:end, :] = jnp.concatenate(
            [query_grad * 0.125, dk_ref[start:end, :], dv_ref[start:end, :]], axis=1
        ).astype(BF16)
    for block in range(LEN // BLK):
        to_arrive_ref[block * BLK : (block + 1) * BLK, : 3 * HD] = all_ref[rows_of(arrive_pos[block]), :]
    to_arrive_ref[:, 3 * HD :] = jnp.zeros((LEN, HD), BF16)
    sums_ref[...] = jnp.sum(all_ref[...].astype(F32), axis=0, keepdims=True)
    for step in range(LEN // ROWS):
        rows = slice(step * ROWS, (step + 1) * ROWS)
        part = dot(to_arrive_ref[rows, : 3 * HD], weight_ref[...], ((1,), (1,))).astype(BF16)
        if step * ROWS < LEN // 2:
            near_ref[rows, :] = part
        else:
            far_ref[step * ROWS - LEN // 2 : (step + 1) * ROWS - LEN // 2, :] = part


SMEM = pl.BlockSpec(memory_space=pltpu.SMEM)
WHOLE = pl.BlockSpec()
VMEM_BYTES = 60 * 2**20


def attend(arrive_pos, ctx_pos, own, other, weight, shift, norm=None):
    head = jax.ShapeDtypeStruct((LEN, HD), BF16)
    fresh = norm is not None
    outs = (head,) * 4
    extra = ()
    if fresh:
        outs = outs + (jax.ShapeDtypeStruct((LEN // 2, D), BF16),) * 2
        extra = tuple(norm)
    return pl.pallas_call(
        functools.partial(attend_kernel, fresh),
        out_shape=outs,
        in_specs=[SMEM, SMEM] + [WHOLE] * (4 + len(extra)),
        out_specs=(WHOLE,) * len(outs),
        scratch_shapes=[pltpu.VMEM((LEN, HD), BF16)],
        compiler_params=pltpu.CompilerParams(vmem_limit_bytes=VMEM_BYTES),
        cost_estimate=pl.CostEstimate(flops=2 * 10**9, bytes_accessed=5 * 10**6, transcendentals=2 * 10**6),
    )(arrive_pos, ctx_pos, own, other, weight, shift, *extra)


def attend_back(arrive_pos, ctx_pos, queries, keys, values, grads, weight):
    return pl.pallas_call(
        attend_back_kernel,
        out_shape=(
            jax.ShapeDtypeStruct((LEN, 4 * HD), BF16),
            jax.ShapeDtypeStruct((LEN // 2, D), BF16),
            jax.ShapeDtypeStruct((LEN // 2, D), BF16),
            jax.ShapeDtypeStruct((1, 3 * HD), F32),
        ),
        in_specs=[SMEM, SMEM] + [WHOLE] * 5,
        out_specs=(WHOLE,) * 4,
        scratch_shapes=[
            pltpu.VMEM((LEN, HD), BF16),
            pltpu.VMEM((LEN, HD), F32),
            pltpu.VMEM((LEN, HD), F32),
            pltpu.VMEM((LEN, 3 * HD), BF16),
        ],
        compiler_params=pltpu.CompilerParams(vmem_limit_bytes=VMEM_BYTES),
        cost_estimate=pl.CostEstimate(flops=4 * 10**9, bytes_accessed=5 * 10**6, transcendentals=2 * 10**6),
    )(arrive_pos, ctx_pos, queries, keys, values, grads, weight)


GELU_SCALE = math.sqrt(2.0 / math.pi)
GELU_CUBE = 0.044715


def load_feed(rows_ref, up_ref, down_ref):
    for owner in range(S):
        for part in range(2):
            first = owner * 96 + part * 48
            up_ref[first : first + 48, :] = rows_ref[owner, 48:96, part * 384 : (part + 1) * 384]
        down_ref[owner * 48 : (owner + 1) * 48, :] = rows_ref[owner, 96:144, :]


def feed_kernel(own_ref, other_ref, rows_ref, shift_ref, hidden_ref, active_ref, near_ref, far_ref, up_ref, down_ref):
    load_feed(rows_ref, up_ref, down_ref)
    for side, (source, target) in enumerate(((own_ref, near_ref), (other_ref, far_ref))):
        for step in range(4 * TOK // ROWS):
            rows = slice(step * ROWS, (step + 1) * ROWS)
            saved = slice(side * 4 * TOK + step * ROWS, side * 4 * TOK + (step + 1) * ROWS)
            hidden = dot(source[rows, :], up_ref[...]) + shift_ref[...]
            hidden_ref[saved, :] = hidden
            inner = GELU_SCALE * (hidden + GELU_CUBE * hidden * hidden * hidden)
            active = (hidden * (0.5 * (1.0 + jnp.tanh(inner)))).astype(BF16)
            active_ref[saved, :] = active
            target[rows, :] = dot(active, down_ref[...]).astype(BF16)


def feed_back_kernel(own_ref, other_ref, rows_ref, hidden_ref, grad_ref, near_ref, far_ref, sums_ref, up_ref, down_ref):
    load_feed(rows_ref, up_ref, down_ref)
    sums = jnp.zeros((1, 384), F32)
    for side, (source, target) in enumerate(((own_ref, near_ref), (other_ref, far_ref))):
        for step in range(4 * TOK // ROWS):
            rows = slice(step * ROWS, (step + 1) * ROWS)
            saved = slice(side * 4 * TOK + step * ROWS, side * 4 * TOK + (step + 1) * ROWS)
            active_grad = dot(source[rows, :], down_ref[...], ((1,), (1,)))
            hidden = hidden_ref[saved, :]
            square = hidden * hidden
            bend = jnp.tanh(GELU_SCALE * (hidden + GELU_CUBE * square * hidden))
            slope = GELU_SCALE * (1.0 + 3.0 * GELU_CUBE * square)
            slope = 0.5 * (1.0 + bend) + 0.5 * hidden * (1.0 - bend * bend) * slope
            grad = (active_grad * slope).astype(BF16)
            grad_ref[saved, :] = grad
            sums = sums + jnp.sum(grad.astype(F32), axis=0, keepdims=True)
            target[rows, :] = dot(grad, up_ref[...], ((1,), (1,))).astype(BF16)
    sums_ref[...] = sums


def feed(own, other, rows, shift):
    half = jax.ShapeDtypeStruct((4 * TOK, D), BF16)
    return pl.pallas_call(
        feed_kernel,
        out_shape=(
            jax.ShapeDtypeStruct((8 * TOK, 384), F32),
            jax.ShapeDtypeStruct((8 * TOK, 384), BF16),
            half,
            half,
        ),
        in_specs=[WHOLE] * 4,
        out_specs=(WHOLE,) * 4,
        scratch_shapes=[pltpu.VMEM((D, 384), BF16), pltpu.VMEM((384, D), BF16)],
        compiler_params=pltpu.CompilerParams(vmem_limit_bytes=VMEM_BYTES),
        cost_estimate=pl.CostEstimate(flops=10**6, bytes_accessed=10**5, transcendentals=0),
    )(own, other, rows, shift)


def feed_back(own, other, rows, hidden):
    half = jax.ShapeDtypeStruct((4 * TOK, D), BF16)
    return pl.pallas_call(
        feed_back_kernel,
        out_shape=(
            jax.ShapeDtypeStruct((8 * TOK, 384), BF16),
            half,
            half,
            jax.ShapeDtypeStruct((1, 384), F32),
        ),
        in_specs=[WHOLE] * 4,
        out_specs=(WHOLE,) * 4,
        scratch_shapes=[pltpu.VMEM((D, 384), BF16), pltpu.VMEM((384, D), BF16)],
        compiler_params=pltpu.CompilerParams(vmem_limit_bytes=VMEM_BYTES),
        cost_estimate=pl.CostEstimate(flops=12 * 10**8, bytes_accessed=7 * 10**6, transcendentals=4 * 10**5),
    )(own, other, rows, hidden)


UPS, DOWNS, OUTS, FIRST = 0, 48, 96, 192
HEADS, SMALL, SECOND = 0, 64, 80
BOTH_ROWS = ((0,), (0,))


def first_grads_kernel(
    own_ref, other_ref, hidden_ref, active_ref, own_down_ref, other_down_ref, mixed_ref, attended_ref, out_ref
):
    half = 4 * TOK
    ups = dot(own_ref[...], hidden_ref[:half, :], BOTH_ROWS) + dot(other_ref[...], hidden_ref[half:, :], BOTH_ROWS)
    ups = ups.astype(BF16)
    for owner in range(S):
        for part in range(2):
            first = owner * 96 + part * 48
            out_ref[owner, UPS:DOWNS, part * 384 : (part + 1) * 384] = ups[first : first + 48, :]
    downs = dot(active_ref[:half, :], own_down_ref[...], BOTH_ROWS)
    downs = (downs + dot(active_ref[half:, :], other_down_ref[...], BOTH_ROWS)).astype(BF16)
    for owner in range(S):
        out_ref[owner, DOWNS:OUTS, :] = downs[owner * 48 : (owner + 1) * 48, :]
    outs = dot(mixed_ref[...], attended_ref[...], BOTH_ROWS).astype(BF16)
    for owner in range(S):
        out_ref[owner, OUTS:FIRST, :] = outs[owner * 96 : (owner + 1) * 96, :]


def first_grads(*parts):
    return pl.pallas_call(
        first_grads_kernel,
        out_shape=jax.ShapeDtypeStruct((S, FIRST, D), BF16),
        in_specs=[WHOLE] * len(parts),
        out_specs=WHOLE,
        compiler_params=pltpu.CompilerParams(vmem_limit_bytes=VMEM_BYTES),
        cost_estimate=pl.CostEstimate(flops=2 * 10**9, bytes_accessed=9 * 10**6, transcendentals=0),
    )(*parts)


def second_grads_kernel(layer, head, own_ref, other_ref, arrive_ref, sums_ref, hidden_sum_ref, *rest):
    vector_refs, prior_refs, out_ref = rest[:6], rest[6:-1], rest[-1]
    half = LEN // 2
    heads = dot(own_ref[...], arrive_ref[:half, :], BOTH_ROWS) + dot(other_ref[...], arrive_ref[half:, :], BOTH_ROWS)
    heads = heads.astype(BF16)
    here = lax.broadcasted_iota(jnp.int32, (1, D), 1) // HD == head[0]
    queries = jnp.where(here, jnp.concatenate([sums_ref[:, :HD]] * H, axis=1), 0.0)
    values = jnp.where(here, jnp.concatenate([sums_ref[:, 2 * HD : 3 * HD]] * H, axis=1), 0.0)
    vectors = [ref[...] for ref in vector_refs]
    vectors = vectors[:2] + [queries, values] + vectors[2:]
    row = lax.broadcasted_iota(jnp.int32, (SECOND - SMALL, D), 0)
    for owner in range(S):
        for part in range(3):
            first = owner * 96 + part * 32
            out_ref[owner, layer * 32 : (layer + 1) * 32, part * 256 : (part + 1) * 256] = heads[first : first + 32, :]
        mine = jnp.concatenate([member[:, owner * 96 : (owner + 1) * 96] for member in vectors], axis=1)
        hidden = jnp.concatenate(
            [hidden_sum_ref[:, owner * 48 : (owner + 1) * 48], jnp.zeros((1, D - 48), F32)], axis=1
        )
        block = jnp.where(row == 2 * layer, mine, jnp.where(row == 2 * layer + 1, hidden, 0.0))
        for prior_ref in prior_refs:
            block = block + prior_ref[owner, SMALL:SECOND, :].astype(F32)
            out_ref[owner, 32:SMALL, :] = prior_ref[owner, 32:SMALL, :]
        if not prior_refs:
            out_ref[owner, :32, :] = jnp.zeros((32, D), BF16)
        out_ref[owner, SMALL:SECOND, :] = block.astype(BF16)


def second_grads(layer, head, *parts):
    return pl.pallas_call(
        functools.partial(second_grads_kernel, layer),
        out_shape=jax.ShapeDtypeStruct((S, SECOND, D), BF16),
        in_specs=[SMEM] + [WHOLE] * len(parts),
        out_specs=WHOLE,
        compiler_params=pltpu.CompilerParams(vmem_limit_bytes=VMEM_BYTES),
        cost_estimate=pl.CostEstimate(flops=10**9, bytes_accessed=5 * 10**6, transcendentals=0),
    )(head, *parts)


def unpack_wide_kernel(first_ref, last_ref, up_ref, down_ref):
    for layer, wide_ref in enumerate((first_ref, last_ref)):
        def wide(place, start, end, wide_ref=wide_ref):
            return wide_ref[place, start:end, :].astype(F32)

        for rank in range(8):
            block = wide(rank, UPS, DOWNS) + wide(rank + 8, UPS, DOWNS)
            for part in range(2):
                for owner in range(S):
                    lane = part * 384 + owner * 48
                    column = owner * 384 + rank * 48
                    up_ref[layer, part * 48 : (part + 1) * 48, column : column + 48] = block[:, lane : lane + 48]
            block = wide(rank, DOWNS, OUTS) + wide(rank + 8, DOWNS, OUTS)
            down_ref[layer, rank * 48 : (rank + 1) * 48, :] = block


def unpack_late_kernel(slots, late_ref, qkv_ref, out_ref, up_shift_ref, *vector_refs):
    def late(place, start, end):
        return late_ref[slots[place], start:end, :].astype(F32)

    for layer in range(LAYERS):
        for head in range(H):
            block = late(head, layer * 32, (layer + 1) * 32)
            for part in range(3):
                for kind in range(3):
                    lane = part * 256 + kind * HD
                    column = kind * D + head * HD
                    qkv_ref[layer, part * 32 : (part + 1) * 32, column : column + HD] = block[:, lane : lane + HD]
    totals = [None] * LAYERS
    for rank in range(8):
        low, high = late(rank, SMALL, SECOND), late(rank + 8, SMALL, SECOND)
        small = low + high
        for layer in range(LAYERS):
            up_shift_ref[layer : layer + 1, rank * 48 : (rank + 1) * 48] = small[2 * layer + 1 : 2 * layer + 2, :48]
            mine = small[2 * layer : 2 * layer + 1, :]
            totals[layer] = mine if rank == 0 else totals[layer] + mine
            rows = slice(4 + 6 * layer, 10 + 6 * layer)
            out_ref[layer, rank * 6 : (rank + 1) * 6, :] = low[rows, :]
            out_ref[layer, (rank + 8) * 6 : (rank + 9) * 6, :] = high[rows, :]
    for layer in range(LAYERS):
        for member, ref in enumerate(vector_refs):
            ref[layer : layer + 1, :] = totals[layer][:, member * 96 : (member + 1) * 96]


def unpack_wide(first, last):
    shapes = [(96, FF), (384, D)]
    return pl.pallas_call(
        unpack_wide_kernel,
        out_shape=tuple(jax.ShapeDtypeStruct((LAYERS,) + shape, F32) for shape in shapes),
        in_specs=[WHOLE] * 2,
        out_specs=(WHOLE,) * len(shapes),
        compiler_params=pltpu.CompilerParams(vmem_limit_bytes=VMEM_BYTES),
        cost_estimate=pl.CostEstimate(flops=10**6, bytes_accessed=10 * 10**6, transcendentals=0),
    )(first, last)


def unpack_late(slots, late):
    shapes = [(96, 3 * D), (96, D), (384,)] + [(96,)] * 8
    return pl.pallas_call(
        unpack_late_kernel,
        out_shape=tuple(jax.ShapeDtypeStruct((LAYERS,) + shape, F32) for shape in shapes),
        in_specs=[SMEM, WHOLE],
        out_specs=(WHOLE,) * len(shapes),
        compiler_params=pltpu.CompilerParams(vmem_limit_bytes=VMEM_BYTES),
        cost_estimate=pl.CostEstimate(flops=10**6, bytes_accessed=5 * 10**6, transcendentals=0),
    )(slots, late)


def join_cores(core, own, other, axis):
    return jnp.where(
        core == 0, jnp.concatenate([own, other], axis=axis), jnp.concatenate([other, own], axis=axis)
    )


def forward_layer(flowing, head_weight, layer_rows, join_out, small, places, gathered=None, carried=None):
    arrive_pos, ctx_pos = places
    head_shift, vectors, up_shift = small
    gain_one, bias_one, unused, unused, out_shift, gain_two, bias_two, down_shift = vectors
    if gathered is not None:
        mixed_head, queries, keys, values, own, other = attend(
            arrive_pos, ctx_pos, *gathered, head_weight, head_shift, (gain_one, bias_one)
        )
        mixed_head, layer_rows = lax.optimization_barrier((mixed_head, layer_rows))
    else:
        normed = layer_norm(flowing, gain_one, bias_one).astype(BF16)
        own = spread_to(normed, 8, "ctx", CHIP_GROUPS)
        own, layer_rows = lax.optimization_barrier((own, layer_rows))
        other = swap_core(own).reshape(LEN // 2, D)
        own = own.reshape(LEN // 2, D)
        own, other, carried = lax.optimization_barrier((own, other, carried))
        carried = spread_to(carried, 4, "ctx", X_GROUPS)
        mixed_head, queries, keys, values = attend(arrive_pos, ctx_pos, own, other, head_weight, head_shift)
        mixed_head, carried = lax.optimization_barrier((mixed_head, carried))
        carried = (carried.reshape(4 * TOK, D), swap_core(carried).reshape(4 * TOK, D))
    out_full = join_out(layer_rows)
    mixed = exchange(mixed_head.reshape(C, TOK, HD), "ctx")[:H]
    mixed = mixed.transpose(1, 0, 2).reshape(TOK, D)
    middle = flowing + dot(mixed, out_full) + out_shift
    second = layer_norm(middle, gain_two, bias_two).astype(BF16)
    second_all, unused = gather_x(second)
    hidden, activated, near, far = feed(*second_all, layer_rows, up_shift)
    if carried is None:
        summed = scatter_x(near, far)
    else:
        run = ((carried, layer_rows, hidden), lambda start: feed_back(*start[0], start[1], start[2]))
        summed, begun = scatter_x(near, far, run)
        carried = (carried, begun)
    output = middle + summed + down_shift
    saved = (flowing, own, other, queries, keys, values, mixed, middle, second_all, hidden, activated)
    return output, saved, carried, (head_weight, out_full, layer_rows)


def backward_layer(grad_out, begun, saved, params, small, places, head, layer, prior, spread):
    arrive_pos, ctx_pos = places
    head_weight, out_full, layer_rows = params
    unused, vectors, unused = small
    gain_one, bias_one, unused, unused, unused, gain_two, bias_two, unused = vectors
    flowing, own, other, queries, keys, values, mixed, middle, second_all, hidden, activated = saved
    down_in = grad_out.astype(BF16)
    down_shift_grad = jnp.sum(down_in.astype(F32), axis=0, keepdims=True)
    if begun is None:
        down_all, prior = gather_x(down_in, prior)
        begun = feed_back(*down_all, layer_rows, hidden)
    else:
        down_all, begun = begun
    hidden_grad, near, far, up_shift_grad = begun
    second_grad = scatter_x(near, far)
    unused, norm_back = jax.vjp(layer_norm, middle, gain_two, bias_two)
    middle_part, gain_two_grad, bias_two_grad = norm_back(second_grad)
    middle_grad = grad_out + middle_part
    attended_in = middle_grad.astype(BF16)
    out_shift_grad = jnp.sum(attended_in.astype(F32), axis=0, keepdims=True)
    mixed_grad = dot(attended_in, out_full, ((1,), (1,))).astype(BF16)
    mixed_grad = mixed_grad.reshape(TOK, H, HD).transpose(1, 0, 2)
    mixed_grad = jnp.concatenate([mixed_grad, jnp.zeros((C - H, TOK, HD), BF16)], axis=0)
    mixed_grad = exchange(mixed_grad, "ctx").reshape(LEN, HD)
    packed = first_grads(*second_all, hidden_grad, activated, *down_all, mixed, attended_in)
    mixed_grad, packed = lax.optimization_barrier((mixed_grad, packed))
    owned = jnp.sum(exchange(packed, "shard").astype(F32), axis=0).astype(BF16)
    to_arrive, near, far, sums = attend_back(
        arrive_pos, ctx_pos, queries, keys, values, mixed_grad, head_weight
    )
    near, far = near.reshape(8, TOK, D), far.reshape(8, TOK, D)
    near = (near.astype(F32) + swap_core(far).astype(F32)).astype(BF16)
    near, owned, spread = lax.optimization_barrier((near, owned, spread))
    normed_grad = jnp.sum(exchange(near, "ctx", CHIP_GROUPS).astype(F32), axis=0)
    unused, first_back = jax.vjp(layer_norm, flowing, gain_one, bias_one)
    flowing_part, gain_one_grad, bias_one_grad = first_back(normed_grad)
    late = second_grads(
        layer,
        head,
        own,
        other,
        to_arrive,
        sums,
        up_shift_grad,
        gain_one_grad,
        bias_one_grad,
        out_shift_grad,
        gain_two_grad,
        bias_two_grad,
        down_shift_grad,
        *prior,
    )
    return middle_grad + flowing_part, owned, late, spread


def shards(
    states,
    cotangent,
    pair_order,
    norm1_gain,
    norm1_bias,
    qkv_weight,
    query_bias,
    value_bias,
    out_weight,
    out_bias,
    norm2_gain,
    norm2_bias,
    up_weight,
    up_bias,
    down_weight,
    down_bias,
):
    place = lax.axis_index("ctx")
    core = place % 2
    rank = place % 8
    head = jnp.minimum(place, H - 1)
    pairs = jnp.stack([pair_order, 2 * C - 1 - pair_order], axis=1)
    ctx_pos = pairs.reshape(-1)
    by_core = pairs.reshape(8, 2, 2).transpose(1, 0, 2)
    arrive_pos = jnp.where(core == 0, by_core, by_core[::-1]).reshape(-1)
    places = (arrive_pos, ctx_pos)

    states_all = tuple(part.reshape(LEN // 2, D) for part in gather_ctx(states.reshape(TOK, D)))

    unit = lax.broadcasted_iota(jnp.int32, (FF, 384), 0)
    column = lax.broadcasted_iota(jnp.int32, (FF, 384), 1)
    pick = (unit == (column // 48) * 384 + rank * 48 + column % 48).astype(BF16)
    up_piece = dot(up_weight.reshape(LAYERS * 96, FF), pick).astype(BF16).reshape(LAYERS, 96, 384)
    down_piece = lax.dynamic_slice_in_dim(down_weight, rank * 48, 48, axis=1)
    out_piece = lax.dynamic_slice_in_dim(out_weight, core * 384, 384, axis=2)

    def beside(piece):
        return jnp.concatenate([piece[:48], piece[48:]], axis=1)

    def apart(piece):
        return jnp.concatenate([piece[..., :384], piece[..., 384:]], axis=1).reshape(D, 384)

    def join_out(rows):
        own = apart(rows[:, :48])
        return join_cores(core, own, swap_core(own), 1)

    layer_pieces = [
        jnp.concatenate([beside(out_piece[layer]), beside(up_piece[layer]), down_piece[layer]], axis=0)
        for layer in range(LAYERS)
    ]

    vectors = jnp.stack(
        [norm1_gain, norm1_bias, query_bias, value_bias, out_bias, norm2_gain, norm2_bias, down_bias]
    )
    head_piece = lax.dynamic_slice_in_dim(qkv_weight.reshape(LAYERS, 96, 3, D), head * HD, HD, axis=3)
    head_piece = jnp.where(place < H, head_piece, jnp.zeros_like(head_piece))
    packed = jnp.concatenate(
        [
            head_piece.reshape(LAYERS * 96 * 3 * HD // D, D),
            vectors.reshape(2, D),
            up_bias.reshape(1, D),
            jnp.zeros((13, D), BF16),
        ],
        axis=0,
    )
    gathered = spread_to(packed, S, "shard")
    gathered, first_piece = lax.optimization_barrier((gathered, layer_pieces[0]))
    layer_rows = [spread_to(first_piece, S, "shard"), lax.all_gather(layer_pieces[1], "shard", axis=0)]
    head_weights = gathered[:, :48].reshape(S, LAYERS, 96, 3 * HD)
    vectors = gathered[:, 48:50].reshape(S, 8, LAYERS, 96).transpose(2, 1, 0, 3).reshape(LAYERS, 8, D)
    vectors = vectors.astype(F32)
    up_shifts = gathered[:, 50].reshape(S, LAYERS, 8, 48)
    up_shifts = lax.dynamic_index_in_dim(up_shifts, rank, 2, False).transpose(1, 0, 2).reshape(LAYERS, 1, 384)
    up_shifts = up_shifts.astype(F32)
    head_shifts = jnp.concatenate(
        [
            lax.dynamic_slice_in_dim(vectors[:, 2], head * HD, HD, axis=1),
            jnp.zeros((LAYERS, HD), F32),
            lax.dynamic_slice_in_dim(vectors[:, 3], head * HD, HD, axis=1),
        ],
        axis=1,
    ).reshape(LAYERS, 1, 3 * HD)

    flowing = states.reshape(TOK, D).astype(F32)
    saved_all = []
    smalls = []
    all_params = []
    for layer in range(LAYERS):
        small = (
            head_shifts[layer],
            [vectors[layer, member : member + 1] for member in range(8)],
            up_shifts[layer],
        )
        smalls.append(small)
        flowing, saved, carried, params = forward_layer(
            flowing,
            head_weights[:, layer].reshape(D, 3 * HD),
            layer_rows[layer],
            join_out,
            small,
            places,
            gathered=states_all if layer == 0 else None,
            carried=cotangent.reshape(TOK, D) if layer == LAYERS - 1 else None,
        )
        saved_all.append(saved)
        all_params.append(params)
    result = flowing.astype(BF16).reshape(states.shape)
    grad_flow = cotangent.reshape(TOK, D).astype(F32)
    held = jnp.where(place < H, place, -1).reshape(1)
    grad_flow, owned_last, late, unused = backward_layer(
        grad_flow, carried, saved_all[1], all_params[1], smalls[1], places, held, 1, (), ()
    )
    every_last = lax.all_gather(owned_last[:OUTS], "ctx", axis=0)
    grad_flow, owned, late, every_last = backward_layer(
        grad_flow, None, saved_all[0], all_params[0], smalls[0], places, held, 0, (late,), every_last
    )
    every_first = lax.all_gather(owned[:OUTS], "ctx", axis=0)
    outs = jnp.stack([owned[OUTS:], owned_last[OUTS:]]).reshape(LAYERS, C, 6, D)
    outs = outs.transpose(1, 0, 2, 3).reshape(C, 12, D)
    outs = exchange(jnp.pad(outs, ((0, 0), (0, 4), (0, 0))), "ctx").astype(F32)
    outs = jnp.sum(outs, axis=0)[:12].astype(BF16)
    late = jnp.sum(exchange(late, "shard").astype(F32), axis=0).astype(BF16)
    late = jnp.concatenate([late[: SMALL + 4], outs], axis=0)
    near = spread_to(late, 8, "ctx", CHIP_GROUPS)
    near, wide = lax.optimization_barrier((near, unpack_wide(every_first, every_last)))
    ups, downs = wide
    every_late = jnp.concatenate([near, swap_core(near)], axis=0)
    places_of = jnp.arange(C, dtype=jnp.int32)
    slots = places_of // 2 + 8 * (places_of % 2 != core).astype(jnp.int32)
    qkv, outs, hiddens, *vectors = unpack_late(slots, every_late)
    return (
        result,
        grad_flow.astype(BF16).reshape(states.shape),
        vectors[0],
        vectors[1],
        qkv,
        vectors[2],
        vectors[3],
        outs,
        vectors[4],
        vectors[5],
        vectors[6],
        ups,
        hiddens,
        downs,
        vectors[7],
    )


def solution(mesh):
    matrix = P(None, "shard", None)
    vector = P(None, "shard")
    rows = P("shard", "ctx", None)
    params = (
        vector,
        vector,
        matrix,
        vector,
        vector,
        matrix,
        vector,
        vector,
        vector,
        matrix,
        vector,
        matrix,
        vector,
    )
    return jax.shard_map(
        shards,
        mesh=mesh,
        in_specs=(rows, rows, P()) + params,
        out_specs=(rows, rows) + params,
        check_vma=False,
    )
```

```python
import functools
import math

import jax
import jax.numpy as jnp
from jax import lax
from jax.experimental import pallas as pl
from jax.experimental.pallas import tpu as pltpu
from jax.sharding import PartitionSpec as P

H = 12
HD = 64
D = 768
FF = 3072
LAYERS = 2
S = 8
C = 16
TOK = 128
LEN = TOK * C
BLK = TOK // 2
ROWS = 256
EPSILON = 1e-05
NEGATIVE = -1e30
F32 = jnp.float32
BF16 = jnp.bfloat16

CHIP_GROUPS = [[2 * q + core for q in range(8)] for core in range(2)]
X_GROUPS = [[8 * y + 2 * x + core for x in range(4)] for y in range(2) for core in range(2)]
SWAP = [(i, i ^ 1) for i in range(C)]


def layer_norm(states, gain, shift):
    average = jnp.mean(states, axis=-1, keepdims=True)
    centered = states - average
    spread = jnp.mean(centered * centered, axis=-1, keepdims=True)
    return centered * lax.rsqrt(spread + EPSILON) * gain + shift


def exchange(parts, axis, groups=None):
    return lax.all_to_all(parts, axis, 0, 0, tiled=True, axis_index_groups=groups)


def spread_to(part, count, axis, groups=None):
    return exchange(jnp.broadcast_to(part[None], (count,) + part.shape), axis, groups)


def swap_core(part):
    return lax.ppermute(part, "ctx", SWAP)


def gather_ctx(part):
    own = spread_to(part, 8, "ctx", CHIP_GROUPS)
    return own, swap_core(own)


def gather_x(part, beside=()):
    own = spread_to(part, 4, "ctx", X_GROUPS)
    own, beside = lax.optimization_barrier((own, beside))
    return (own.reshape(4 * TOK, D), swap_core(own).reshape(4 * TOK, D)), beside


def scatter(near, far, groups, run=None):
    mine = near.astype(F32) + swap_core(far.astype(BF16)).astype(F32)
    mine = mine.astype(BF16)
    if run is None:
        return jnp.sum(exchange(mine, "ctx", groups).astype(F32), axis=0)
    start, ready = run
    mine, start = lax.optimization_barrier((mine, start))
    parts, result = lax.optimization_barrier((exchange(mine, "ctx", groups), ready(start)))
    return jnp.sum(parts.astype(F32), axis=0), result


def scatter_x(near, far, run=None):
    return scatter(near.reshape(4, TOK, D), far.reshape(4, TOK, D), X_GROUPS, run)


def dot(left, right, dims=((1,), (0,))):
    return lax.dot_general(left, right, (dims, ((), ())), preferred_element_type=F32)


def rows_of(block):
    return pl.ds(pl.multiple_of(block * BLK, BLK), BLK)


def attend_kernel(fresh, arrive_pos, ctx_pos, own_ref, other_ref, weight_ref, shift_ref, *rest):
    if fresh:
        gain_ref, bias_ref, mixed_ref, q_ref, k_ref, v_ref, own_normed, other_normed, out_ref = rest
    else:
        mixed_ref, q_ref, k_ref, v_ref, out_ref = rest
    for step in range(LEN // ROWS):
        half = LEN // ROWS // 2
        source = own_ref if step < half else other_ref
        rows = slice(step % half * ROWS, (step % half + 1) * ROWS)
        normed = source[rows, :]
        if fresh:
            normed = layer_norm(normed.astype(F32), gain_ref[...], bias_ref[...]).astype(BF16)
            (own_normed if step < half else other_normed)[rows, :] = normed
        piece = dot(normed, weight_ref[...]) + shift_ref[...]
        for part in range(ROWS // BLK):
            rows = rows_of(arrive_pos[step * (ROWS // BLK) + part])
            block = piece[part * BLK : (part + 1) * BLK, :]
            q_ref[rows, :] = (block[:, :HD].astype(BF16).astype(F32) * 0.125).astype(BF16)
            k_ref[rows, :] = block[:, HD : 2 * HD].astype(BF16)
            v_ref[rows, :] = block[:, 2 * HD :].astype(BF16)
    keep = lax.broadcasted_iota(jnp.int32, (ROWS, ROWS), 0) >= lax.broadcasted_iota(
        jnp.int32, (ROWS, ROWS), 1
    )
    for step in range(LEN // ROWS):
        start = step * ROWS
        queries = q_ref[start : start + ROWS, :]
        near = dot(queries, k_ref[start : start + ROWS, :], ((1,), (1,)))
        near = jnp.where(keep, near, NEGATIVE)
        highest = jnp.max(near, axis=1, keepdims=True)
        if step:
            far = dot(queries, k_ref[:start, :], ((1,), (1,)))
            highest = jnp.maximum(highest, jnp.max(far, axis=1, keepdims=True))
        weights = jnp.exp(near - highest)
        total = jnp.sum(weights, axis=1, keepdims=True)
        mixed = dot(weights.astype(BF16), v_ref[start : start + ROWS, :])
        if step:
            weights = jnp.exp(far - highest)
            total = total + jnp.sum(weights, axis=1, keepdims=True)
            mixed = mixed + dot(weights.astype(BF16), v_ref[:start, :])
        out_ref[start : start + ROWS, :] = (mixed / total).astype(BF16)
    for block in range(LEN // BLK):
        mixed_ref[block * BLK : (block + 1) * BLK, :] = out_ref[rows_of(ctx_pos[block]), :]


def attend_back_kernel(
    arrive_pos, ctx_pos, q_ref, k_ref, v_ref, grad_ref, weight_ref,
    to_arrive_ref, near_ref, far_ref, sums_ref, do_ref, dk_ref, dv_ref, all_ref
):
    for block in range(LEN // BLK):
        do_ref[rows_of(ctx_pos[block]), :] = grad_ref[block * BLK : (block + 1) * BLK, :]
    keep = lax.broadcasted_iota(jnp.int32, (ROWS, ROWS), 0) <= lax.broadcasted_iota(
        jnp.int32, (ROWS, ROWS), 1
    )
    for step in range(LEN // ROWS - 1, -1, -1):
        start = step * ROWS
        end = start + ROWS
        queries = q_ref[start:end, :]
        grads = do_ref[start:end, :]
        near_keys, near_values = k_ref[start:end, :], v_ref[start:end, :]
        near = jnp.where(keep, dot(near_keys, queries, ((1,), (1,))), NEGATIVE)
        highest = jnp.max(near, axis=0, keepdims=True)
        if step:
            far_keys, far_values = k_ref[:start, :], v_ref[:start, :]
            far = dot(far_keys, queries, ((1,), (1,)))
            highest = jnp.maximum(highest, jnp.max(far, axis=0, keepdims=True))
        near = jnp.exp(near - highest)
        total = jnp.sum(near, axis=0, keepdims=True)
        if step:
            far = jnp.exp(far - highest)
            total = total + jnp.sum(far, axis=0, keepdims=True)
        inverse = 1.0 / total
        near = near * inverse
        near_grad = dot(near_values, grads, ((1,), (1,)))
        inner = jnp.sum(near * near_grad, axis=0, keepdims=True)
        if step:
            far = far * inverse
            far_grad = dot(far_values, grads, ((1,), (1,)))
            inner = inner + jnp.sum(far * far_grad, axis=0, keepdims=True)
        near_scores = (near * (near_grad - inner)).astype(BF16)
        near_dk = dot(near_scores, queries)
        near_dv = dot(near.astype(BF16), grads)
        query_grad = dot(near_scores, near_keys, ((0,), (0,)))
        if step == LEN // ROWS - 1:
            dk_ref[start:end, :] = near_dk
            dv_ref[start:end, :] = near_dv
        else:
            dk_ref[start:end, :] += near_dk
            dv_ref[start:end, :] += near_dv
        if step:
            far_scores = (far * (far_grad - inner)).astype(BF16)
            far_dk = dot(far_scores, queries)
            far_dv = dot(far.astype(BF16), grads)
            query_grad = query_grad + dot(far_scores, far_keys, ((0,), (0,)))
            if step == LEN // ROWS - 1:
                dk_ref[:start, :] = far_dk
                dv_ref[:start, :] = far_dv
            else:
                dk_ref[:start, :] += far_dk
                dv_ref[:start, :] += far_dv
        all_ref[start:end, :] = jnp.concatenate(
            [query_grad * 0.125, dk_ref[start:end, :], dv_ref[start:end, :]], axis=1
        ).astype(BF16)
    for block in range(LEN // BLK):
        to_arrive_ref[block * BLK : (block + 1) * BLK, : 3 * HD] = all_ref[rows_of(arrive_pos[block]), :]
    to_arrive_ref[:, 3 * HD :] = jnp.zeros((LEN, HD), BF16)
    sums_ref[...] = jnp.sum(all_ref[...].astype(F32), axis=0, keepdims=True)
    for step in range(LEN // ROWS):
        rows = slice(step * ROWS, (step + 1) * ROWS)
        part = dot(to_arrive_ref[rows, : 3 * HD], weight_ref[...], ((1,), (1,))).astype(BF16)
        if step * ROWS < LEN // 2:
            near_ref[rows, :] = part
        else:
            far_ref[step * ROWS - LEN // 2 : (step + 1) * ROWS - LEN // 2, :] = part


SMEM = pl.BlockSpec(memory_space=pltpu.SMEM)
WHOLE = pl.BlockSpec()
VMEM_BYTES = 60 * 2**20


def attend(arrive_pos, ctx_pos, own, other, weight, shift, norm=None):
    head = jax.ShapeDtypeStruct((LEN, HD), BF16)
    fresh = norm is not None
    outs = (head,) * 4
    extra = ()
    if fresh:
        outs = outs + (jax.ShapeDtypeStruct((LEN // 2, D), BF16),) * 2
        extra = tuple(norm)
    return pl.pallas_call(
        functools.partial(attend_kernel, fresh),
        out_shape=outs,
        in_specs=[SMEM, SMEM] + [WHOLE] * (4 + len(extra)),
        out_specs=(WHOLE,) * len(outs),
        scratch_shapes=[pltpu.VMEM((LEN, HD), BF16)],
        compiler_params=pltpu.CompilerParams(vmem_limit_bytes=VMEM_BYTES),
        cost_estimate=pl.CostEstimate(flops=2 * 10**9, bytes_accessed=5 * 10**6, transcendentals=2 * 10**6),
    )(arrive_pos, ctx_pos, own, other, weight, shift, *extra)


def attend_back(arrive_pos, ctx_pos, queries, keys, values, grads, weight):
    return pl.pallas_call(
        attend_back_kernel,
        out_shape=(
            jax.ShapeDtypeStruct((LEN, 4 * HD), BF16),
            jax.ShapeDtypeStruct((LEN // 2, D), BF16),
            jax.ShapeDtypeStruct((LEN // 2, D), BF16),
            jax.ShapeDtypeStruct((1, 3 * HD), F32),
        ),
        in_specs=[SMEM, SMEM] + [WHOLE] * 5,
        out_specs=(WHOLE,) * 4,
        scratch_shapes=[
            pltpu.VMEM((LEN, HD), BF16),
            pltpu.VMEM((LEN, HD), F32),
            pltpu.VMEM((LEN, HD), F32),
            pltpu.VMEM((LEN, 3 * HD), BF16),
        ],
        compiler_params=pltpu.CompilerParams(vmem_limit_bytes=VMEM_BYTES),
        cost_estimate=pl.CostEstimate(flops=4 * 10**9, bytes_accessed=5 * 10**6, transcendentals=2 * 10**6),
    )(arrive_pos, ctx_pos, queries, keys, values, grads, weight)


GELU_SCALE = math.sqrt(2.0 / math.pi)
GELU_CUBE = 0.044715


def load_feed(rows_ref, up_ref, down_ref):
    for owner in range(S):
        for part in range(2):
            first = owner * 96 + part * 48
            up_ref[first : first + 48, :] = rows_ref[owner, 48:96, part * 384 : (part + 1) * 384]
        down_ref[owner * 48 : (owner + 1) * 48, :] = rows_ref[owner, 96:144, :]


def feed_kernel(own_ref, other_ref, rows_ref, shift_ref, hidden_ref, active_ref, near_ref, far_ref, up_ref, down_ref):
    load_feed(rows_ref, up_ref, down_ref)
    for side, (source, target) in enumerate(((own_ref, near_ref), (other_ref, far_ref))):
        for step in range(4 * TOK // ROWS):
            rows = slice(step * ROWS, (step + 1) * ROWS)
            saved = slice(side * 4 * TOK + step * ROWS, side * 4 * TOK + (step + 1) * ROWS)
            hidden = dot(source[rows, :], up_ref[...]) + shift_ref[...]
            hidden_ref[saved, :] = hidden
            inner = GELU_SCALE * (hidden + GELU_CUBE * hidden * hidden * hidden)
            active = (hidden * (0.5 * (1.0 + jnp.tanh(inner)))).astype(BF16)
            active_ref[saved, :] = active
            target[rows, :] = dot(active, down_ref[...]).astype(BF16)


def feed_back_kernel(own_ref, other_ref, rows_ref, hidden_ref, grad_ref, near_ref, far_ref, sums_ref, up_ref, down_ref):
    load_feed(rows_ref, up_ref, down_ref)
    sums = jnp.zeros((1, 384), F32)
    for side, (source, target) in enumerate(((own_ref, near_ref), (other_ref, far_ref))):
        for step in range(4 * TOK // ROWS):
            rows = slice(step * ROWS, (step + 1) * ROWS)
            saved = slice(side * 4 * TOK + step * ROWS, side * 4 * TOK + (step + 1) * ROWS)
            active_grad = dot(source[rows, :], down_ref[...], ((1,), (1,)))
            hidden = hidden_ref[saved, :]
            square = hidden * hidden
            bend = jnp.tanh(GELU_SCALE * (hidden + GELU_CUBE * square * hidden))
            slope = GELU_SCALE * (1.0 + 3.0 * GELU_CUBE * square)
            slope = 0.5 * (1.0 + bend) + 0.5 * hidden * (1.0 - bend * bend) * slope
            grad = (active_grad * slope).astype(BF16)
            grad_ref[saved, :] = grad
            sums = sums + jnp.sum(grad.astype(F32), axis=0, keepdims=True)
            target[rows, :] = dot(grad, up_ref[...], ((1,), (1,))).astype(BF16)
    sums_ref[...] = sums


def feed(own, other, rows, shift):
    half = jax.ShapeDtypeStruct((4 * TOK, D), BF16)
    return pl.pallas_call(
        feed_kernel,
        out_shape=(
            jax.ShapeDtypeStruct((8 * TOK, 384), F32),
            jax.ShapeDtypeStruct((8 * TOK, 384), BF16),
            half,
            half,
        ),
        in_specs=[WHOLE] * 4,
        out_specs=(WHOLE,) * 4,
        scratch_shapes=[pltpu.VMEM((D, 384), BF16), pltpu.VMEM((384, D), BF16)],
        compiler_params=pltpu.CompilerParams(vmem_limit_bytes=VMEM_BYTES),
        cost_estimate=pl.CostEstimate(flops=10**6, bytes_accessed=10**5, transcendentals=0),
    )(own, other, rows, shift)


def feed_back(own, other, rows, hidden):
    half = jax.ShapeDtypeStruct((4 * TOK, D), BF16)
    return pl.pallas_call(
        feed_back_kernel,
        out_shape=(
            jax.ShapeDtypeStruct((8 * TOK, 384), BF16),
            half,
            half,
            jax.ShapeDtypeStruct((1, 384), F32),
        ),
        in_specs=[WHOLE] * 4,
        out_specs=(WHOLE,) * 4,
        scratch_shapes=[pltpu.VMEM((D, 384), BF16), pltpu.VMEM((384, D), BF16)],
        compiler_params=pltpu.CompilerParams(vmem_limit_bytes=VMEM_BYTES),
        cost_estimate=pl.CostEstimate(flops=12 * 10**8, bytes_accessed=7 * 10**6, transcendentals=4 * 10**5),
    )(own, other, rows, hidden)


UPS, DOWNS, OUTS, FIRST = 0, 48, 96, 192
HEADS, SMALL, SECOND = 0, 64, 80
BOTH_ROWS = ((0,), (0,))


def first_grads_kernel(
    own_ref, other_ref, hidden_ref, active_ref, own_down_ref, other_down_ref, mixed_ref, attended_ref, out_ref
):
    half = 4 * TOK
    ups = dot(own_ref[...], hidden_ref[:half, :], BOTH_ROWS) + dot(other_ref[...], hidden_ref[half:, :], BOTH_ROWS)
    ups = ups.astype(BF16)
    for owner in range(S):
        for part in range(2):
            first = owner * 96 + part * 48
            out_ref[owner, UPS:DOWNS, part * 384 : (part + 1) * 384] = ups[first : first + 48, :]
    downs = dot(active_ref[:half, :], own_down_ref[...], BOTH_ROWS)
    downs = (downs + dot(active_ref[half:, :], other_down_ref[...], BOTH_ROWS)).astype(BF16)
    for owner in range(S):
        out_ref[owner, DOWNS:OUTS, :] = downs[owner * 48 : (owner + 1) * 48, :]
    outs = dot(mixed_ref[...], attended_ref[...], BOTH_ROWS).astype(BF16)
    for owner in range(S):
        out_ref[owner, OUTS:FIRST, :] = outs[owner * 96 : (owner + 1) * 96, :]


def first_grads(*parts):
    return pl.pallas_call(
        first_grads_kernel,
        out_shape=jax.ShapeDtypeStruct((S, FIRST, D), BF16),
        in_specs=[WHOLE] * len(parts),
        out_specs=WHOLE,
        compiler_params=pltpu.CompilerParams(vmem_limit_bytes=VMEM_BYTES),
        cost_estimate=pl.CostEstimate(flops=2 * 10**9, bytes_accessed=9 * 10**6, transcendentals=0),
    )(*parts)


def second_grads_kernel(layer, head, own_ref, other_ref, arrive_ref, sums_ref, hidden_sum_ref, *rest):
    vector_refs, prior_refs, out_ref = rest[:6], rest[6:-1], rest[-1]
    half = LEN // 2
    heads = dot(own_ref[...], arrive_ref[:half, :], BOTH_ROWS) + dot(other_ref[...], arrive_ref[half:, :], BOTH_ROWS)
    heads = heads.astype(BF16)
    here = lax.broadcasted_iota(jnp.int32, (1, D), 1) // HD == head[0]
    queries = jnp.where(here, jnp.concatenate([sums_ref[:, :HD]] * H, axis=1), 0.0)
    values = jnp.where(here, jnp.concatenate([sums_ref[:, 2 * HD : 3 * HD]] * H, axis=1), 0.0)
    vectors = [ref[...] for ref in vector_refs]
    vectors = vectors[:2] + [queries, values] + vectors[2:]
    row = lax.broadcasted_iota(jnp.int32, (SECOND - SMALL, D), 0)
    for owner in range(S):
        for part in range(3):
            first = owner * 96 + part * 32
            out_ref[owner, layer * 32 : (layer + 1) * 32, part * 256 : (part + 1) * 256] = heads[first : first + 32, :]
        mine = jnp.concatenate([member[:, owner * 96 : (owner + 1) * 96] for member in vectors], axis=1)
        hidden = jnp.concatenate(
            [hidden_sum_ref[:, owner * 48 : (owner + 1) * 48], jnp.zeros((1, D - 48), F32)], axis=1
        )
        block = jnp.where(row == 2 * layer, mine, jnp.where(row == 2 * layer + 1, hidden, 0.0))
        for prior_ref in prior_refs:
            block = block + prior_ref[owner, SMALL:SECOND, :].astype(F32)
            out_ref[owner, 32:SMALL, :] = prior_ref[owner, 32:SMALL, :]
        if not prior_refs:
            out_ref[owner, :32, :] = jnp.zeros((32, D), BF16)
        out_ref[owner, SMALL:SECOND, :] = block.astype(BF16)


def second_grads(layer, head, *parts):
    return pl.pallas_call(
        functools.partial(second_grads_kernel, layer),
        out_shape=jax.ShapeDtypeStruct((S, SECOND, D), BF16),
        in_specs=[SMEM] + [WHOLE] * len(parts),
        out_specs=WHOLE,
        compiler_params=pltpu.CompilerParams(vmem_limit_bytes=VMEM_BYTES),
        cost_estimate=pl.CostEstimate(flops=10**9, bytes_accessed=5 * 10**6, transcendentals=0),
    )(head, *parts)


def unpack_wide_kernel(first_ref, last_ref, up_ref, down_ref):
    for layer, wide_ref in enumerate((first_ref, last_ref)):
        def wide(place, start, end, wide_ref=wide_ref):
            return wide_ref[place, start:end, :].astype(F32)

        for rank in range(8):
            block = wide(rank, UPS, DOWNS) + wide(rank + 8, UPS, DOWNS)
            for part in range(2):
                for owner in range(S):
                    lane = part * 384 + owner * 48
                    column = owner * 384 + rank * 48
                    up_ref[layer, part * 48 : (part + 1) * 48, column : column + 48] = block[:, lane : lane + 48]
            block = wide(rank, DOWNS, OUTS) + wide(rank + 8, DOWNS, OUTS)
            down_ref[layer, rank * 48 : (rank + 1) * 48, :] = block


def unpack_late_kernel(slots, late_ref, qkv_ref, out_ref, up_shift_ref, *vector_refs):
    def late(place, start, end):
        return late_ref[slots[place], start:end, :].astype(F32)

    for layer in range(LAYERS):
        for head in range(H):
            block = late(head, layer * 32, (layer + 1) * 32)
            for part in range(3):
                for kind in range(3):
                    lane = part * 256 + kind * HD
                    column = kind * D + head * HD
                    qkv_ref[layer, part * 32 : (part + 1) * 32, column : column + HD] = block[:, lane : lane + HD]
    totals = [None] * LAYERS
    for rank in range(8):
        low, high = late(rank, SMALL, SECOND), late(rank + 8, SMALL, SECOND)
        small = low + high
        for layer in range(LAYERS):
            up_shift_ref[layer : layer + 1, rank * 48 : (rank + 1) * 48] = small[2 * layer + 1 : 2 * layer + 2, :48]
            mine = small[2 * layer : 2 * layer + 1, :]
            totals[layer] = mine if rank == 0 else totals[layer] + mine
            rows = slice(4 + 6 * layer, 10 + 6 * layer)
            out_ref[layer, rank * 6 : (rank + 1) * 6, :] = low[rows, :]
            out_ref[layer, (rank + 8) * 6 : (rank + 9) * 6, :] = high[rows, :]
    for layer in range(LAYERS):
        for member, ref in enumerate(vector_refs):
            ref[layer : layer + 1, :] = totals[layer][:, member * 96 : (member + 1) * 96]


def unpack_wide(first, last):
    shapes = [(96, FF), (384, D)]
    return pl.pallas_call(
        unpack_wide_kernel,
        out_shape=tuple(jax.ShapeDtypeStruct((LAYERS,) + shape, F32) for shape in shapes),
        in_specs=[WHOLE] * 2,
        out_specs=(WHOLE,) * len(shapes),
        compiler_params=pltpu.CompilerParams(vmem_limit_bytes=VMEM_BYTES),
        cost_estimate=pl.CostEstimate(flops=10**6, bytes_accessed=10 * 10**6, transcendentals=0),
    )(first, last)


def unpack_late(slots, late):
    shapes = [(96, 3 * D), (96, D), (384,)] + [(96,)] * 8
    return pl.pallas_call(
        unpack_late_kernel,
        out_shape=tuple(jax.ShapeDtypeStruct((LAYERS,) + shape, F32) for shape in shapes),
        in_specs=[SMEM, WHOLE],
        out_specs=(WHOLE,) * len(shapes),
        compiler_params=pltpu.CompilerParams(vmem_limit_bytes=VMEM_BYTES),
        cost_estimate=pl.CostEstimate(flops=10**6, bytes_accessed=5 * 10**6, transcendentals=0),
    )(slots, late)


def join_cores(core, own, other, axis):
    return jnp.where(
        core == 0, jnp.concatenate([own, other], axis=axis), jnp.concatenate([other, own], axis=axis)
    )


def forward_layer(flowing, head_weight, layer_rows, join_out, small, places, gathered=None, carried=None):
    arrive_pos, ctx_pos = places
    head_shift, vectors, up_shift = small
    gain_one, bias_one, unused, unused, out_shift, gain_two, bias_two, down_shift = vectors
    if gathered is not None:
        mixed_head, queries, keys, values, own, other = attend(
            arrive_pos, ctx_pos, *gathered, head_weight, head_shift, (gain_one, bias_one)
        )
        mixed_head, layer_rows = lax.optimization_barrier((mixed_head, layer_rows))
    else:
        normed = layer_norm(flowing, gain_one, bias_one).astype(BF16)
        normed, layer_rows = lax.optimization_barrier((normed, layer_rows))
        own, other = (part.reshape(LEN // 2, D) for part in gather_ctx(normed))
        own, other, carried = lax.optimization_barrier((own, other, carried))
        carried = spread_to(carried, 4, "ctx", X_GROUPS)
        mixed_head, queries, keys, values = attend(arrive_pos, ctx_pos, own, other, head_weight, head_shift)
        mixed_head, carried = lax.optimization_barrier((mixed_head, carried))
        carried = (carried.reshape(4 * TOK, D), swap_core(carried).reshape(4 * TOK, D))
    out_full = join_out(layer_rows)
    mixed = exchange(mixed_head.reshape(C, TOK, HD), "ctx")[:H]
    mixed = mixed.transpose(1, 0, 2).reshape(TOK, D)
    middle = flowing + dot(mixed, out_full) + out_shift
    second = layer_norm(middle, gain_two, bias_two).astype(BF16)
    second_all, unused = gather_x(second)
    hidden, activated, near, far = feed(*second_all, layer_rows, up_shift)
    if carried is None:
        summed = scatter_x(near, far)
    else:
        run = ((carried, layer_rows, hidden), lambda start: feed_back(*start[0], start[1], start[2]))
        summed, begun = scatter_x(near, far, run)
        carried = (carried, begun)
    output = middle + summed + down_shift
    saved = (flowing, own, other, queries, keys, values, mixed, middle, second_all, hidden, activated)
    return output, saved, carried, (head_weight, out_full, layer_rows)


def backward_layer(grad_out, begun, saved, params, small, places, head, layer, prior, spread):
    arrive_pos, ctx_pos = places
    head_weight, out_full, layer_rows = params
    unused, vectors, unused = small
    gain_one, bias_one, unused, unused, unused, gain_two, bias_two, unused = vectors
    flowing, own, other, queries, keys, values, mixed, middle, second_all, hidden, activated = saved
    down_in = grad_out.astype(BF16)
    down_shift_grad = jnp.sum(down_in.astype(F32), axis=0, keepdims=True)
    if begun is None:
        down_all, prior = gather_x(down_in, prior)
        begun = feed_back(*down_all, layer_rows, hidden)
    else:
        down_all, begun = begun
    hidden_grad, near, far, up_shift_grad = begun
    second_grad = scatter_x(near, far)
    unused, norm_back = jax.vjp(layer_norm, middle, gain_two, bias_two)
    middle_part, gain_two_grad, bias_two_grad = norm_back(second_grad)
    middle_grad = grad_out + middle_part
    attended_in = middle_grad.astype(BF16)
    out_shift_grad = jnp.sum(attended_in.astype(F32), axis=0, keepdims=True)
    mixed_grad = dot(attended_in, out_full, ((1,), (1,))).astype(BF16)
    mixed_grad = mixed_grad.reshape(TOK, H, HD).transpose(1, 0, 2)
    mixed_grad = jnp.concatenate([mixed_grad, jnp.zeros((C - H, TOK, HD), BF16)], axis=0)
    mixed_grad = exchange(mixed_grad, "ctx").reshape(LEN, HD)
    packed = first_grads(*second_all, hidden_grad, activated, *down_all, mixed, attended_in)
    mixed_grad, packed = lax.optimization_barrier((mixed_grad, packed))
    owned = jnp.sum(exchange(packed, "shard").astype(F32), axis=0).astype(BF16)
    to_arrive, near, far, sums = attend_back(
        arrive_pos, ctx_pos, queries, keys, values, mixed_grad, head_weight
    )
    near, far = near.reshape(8, TOK, D), far.reshape(8, TOK, D)
    near = (near.astype(F32) + swap_core(far).astype(F32)).astype(BF16)
    near, owned, spread = lax.optimization_barrier((near, owned, spread))
    normed_grad = jnp.sum(exchange(near, "ctx", CHIP_GROUPS).astype(F32), axis=0)
    unused, first_back = jax.vjp(layer_norm, flowing, gain_one, bias_one)
    flowing_part, gain_one_grad, bias_one_grad = first_back(normed_grad)
    late = second_grads(
        layer,
        head,
        own,
        other,
        to_arrive,
        sums,
        up_shift_grad,
        gain_one_grad,
        bias_one_grad,
        out_shift_grad,
        gain_two_grad,
        bias_two_grad,
        down_shift_grad,
        *prior,
    )
    return middle_grad + flowing_part, owned, late, spread


def shards(
    states,
    cotangent,
    pair_order,
    norm1_gain,
    norm1_bias,
    qkv_weight,
    query_bias,
    value_bias,
    out_weight,
    out_bias,
    norm2_gain,
    norm2_bias,
    up_weight,
    up_bias,
    down_weight,
    down_bias,
):
    place = lax.axis_index("ctx")
    core = place % 2
    rank = place % 8
    head = jnp.minimum(place, H - 1)
    pairs = jnp.stack([pair_order, 2 * C - 1 - pair_order], axis=1)
    ctx_pos = pairs.reshape(-1)
    by_core = pairs.reshape(8, 2, 2).transpose(1, 0, 2)
    arrive_pos = jnp.where(core == 0, by_core, by_core[::-1]).reshape(-1)
    places = (arrive_pos, ctx_pos)

    states_all = tuple(part.reshape(LEN // 2, D) for part in gather_ctx(states.reshape(TOK, D)))

    unit = lax.broadcasted_iota(jnp.int32, (FF, 384), 0)
    column = lax.broadcasted_iota(jnp.int32, (FF, 384), 1)
    pick = (unit == (column // 48) * 384 + rank * 48 + column % 48).astype(BF16)
    up_piece = dot(up_weight.reshape(LAYERS * 96, FF), pick).astype(BF16).reshape(LAYERS, 96, 384)
    down_piece = lax.dynamic_slice_in_dim(down_weight, rank * 48, 48, axis=1)
    out_piece = lax.dynamic_slice_in_dim(out_weight, core * 384, 384, axis=2)

    def beside(piece):
        return jnp.concatenate([piece[:48], piece[48:]], axis=1)

    def apart(piece):
        return jnp.concatenate([piece[..., :384], piece[..., 384:]], axis=1).reshape(D, 384)

    def join_out(rows):
        own = apart(rows[:, :48])
        return join_cores(core, own, swap_core(own), 1)

    layer_pieces = [
        jnp.concatenate([beside(out_piece[layer]), beside(up_piece[layer]), down_piece[layer]], axis=0)
        for layer in range(LAYERS)
    ]

    vectors = jnp.stack(
        [norm1_gain, norm1_bias, query_bias, value_bias, out_bias, norm2_gain, norm2_bias, down_bias]
    )
    head_piece = lax.dynamic_slice_in_dim(qkv_weight.reshape(LAYERS, 96, 3, D), head * HD, HD, axis=3)
    head_piece = jnp.where(place < H, head_piece, jnp.zeros_like(head_piece))
    packed = jnp.concatenate(
        [
            head_piece.reshape(LAYERS * 96 * 3 * HD // D, D),
            vectors.reshape(2, D),
            up_bias.reshape(1, D),
            jnp.zeros((13, D), BF16),
        ],
        axis=0,
    )
    gathered = spread_to(packed, S, "shard")
    gathered, pieces = lax.optimization_barrier((gathered, jnp.concatenate(layer_pieces, axis=0)))
    both_rows = spread_to(pieces, S, "shard")
    layer_rows = [both_rows[:, :144], both_rows[:, 144:]]
    head_weights = gathered[:, :48].reshape(S, LAYERS, 96, 3 * HD)
    vectors = gathered[:, 48:50].reshape(S, 8, LAYERS, 96).transpose(2, 1, 0, 3).reshape(LAYERS, 8, D)
    vectors = vectors.astype(F32)
    up_shifts = gathered[:, 50].reshape(S, LAYERS, 8, 48)
    up_shifts = lax.dynamic_index_in_dim(up_shifts, rank, 2, False).transpose(1, 0, 2).reshape(LAYERS, 1, 384)
    up_shifts = up_shifts.astype(F32)
    head_shifts = jnp.concatenate(
        [
            lax.dynamic_slice_in_dim(vectors[:, 2], head * HD, HD, axis=1),
            jnp.zeros((LAYERS, HD), F32),
            lax.dynamic_slice_in_dim(vectors[:, 3], head * HD, HD, axis=1),
        ],
        axis=1,
    ).reshape(LAYERS, 1, 3 * HD)

    flowing = states.reshape(TOK, D).astype(F32)
    saved_all = []
    smalls = []
    all_params = []
    for layer in range(LAYERS):
        small = (
            head_shifts[layer],
            [vectors[layer, member : member + 1] for member in range(8)],
            up_shifts[layer],
        )
        smalls.append(small)
        flowing, saved, carried, params = forward_layer(
            flowing,
            head_weights[:, layer].reshape(D, 3 * HD),
            layer_rows[layer],
            join_out,
            small,
            places,
            gathered=states_all if layer == 0 else None,
            carried=cotangent.reshape(TOK, D) if layer == LAYERS - 1 else None,
        )
        saved_all.append(saved)
        all_params.append(params)
    result = flowing.astype(BF16).reshape(states.shape)
    grad_flow = cotangent.reshape(TOK, D).astype(F32)
    held = jnp.where(place < H, place, -1).reshape(1)
    grad_flow, owned_last, late, unused = backward_layer(
        grad_flow, carried, saved_all[1], all_params[1], smalls[1], places, held, 1, (), ()
    )
    every_last = lax.all_gather(owned_last[:OUTS], "ctx", axis=0)
    grad_flow, owned, late, every_last = backward_layer(
        grad_flow, None, saved_all[0], all_params[0], smalls[0], places, held, 0, (late,), every_last
    )
    every_first = lax.all_gather(owned[:OUTS], "ctx", axis=0)
    outs = jnp.stack([owned[OUTS:], owned_last[OUTS:]]).reshape(LAYERS, C, 6, D)
    outs = outs.transpose(1, 0, 2, 3).reshape(C, 12, D)
    outs = exchange(jnp.pad(outs, ((0, 0), (0, 4), (0, 0))), "ctx").astype(F32)
    outs = jnp.sum(outs, axis=0)[:12].astype(BF16)
    late = jnp.sum(exchange(late, "shard").astype(F32), axis=0).astype(BF16)
    late = jnp.concatenate([late[: SMALL + 4], outs], axis=0)
    near = spread_to(late, 8, "ctx", CHIP_GROUPS)
    near, wide = lax.optimization_barrier((near, unpack_wide(every_first, every_last)))
    ups, downs = wide
    every_late = jnp.concatenate([near, swap_core(near)], axis=0)
    places_of = jnp.arange(C, dtype=jnp.int32)
    slots = places_of // 2 + 8 * (places_of % 2 != core).astype(jnp.int32)
    qkv, outs, hiddens, *vectors = unpack_late(slots, every_late)
    return (
        result,
        grad_flow.astype(BF16).reshape(states.shape),
        vectors[0],
        vectors[1],
        qkv,
        vectors[2],
        vectors[3],
        outs,
        vectors[4],
        vectors[5],
        vectors[6],
        ups,
        hiddens,
        downs,
        vectors[7],
    )


def solution(mesh):
    matrix = P(None, "shard", None)
    vector = P(None, "shard")
    rows = P("shard", "ctx", None)
    params = (
        vector,
        vector,
        matrix,
        vector,
        vector,
        matrix,
        vector,
        vector,
        vector,
        matrix,
        vector,
        matrix,
        vector,
    )
    return jax.shard_map(
        shards,
        mesh=mesh,
        in_specs=(rows, rows, P()) + params,
        out_specs=(rows, rows) + params,
        check_vma=False,
    )
```
